32 devices in a mesh: dp: 8 (over z, y), rep: 4 (over x, core).
Axes of the slice: x: 2, y: 2, z: 4, core: 2. Of those that a mesh axis runs over, the one named last changes fastest.
Arguments:
- features: bfloat16 [32, 64, 64, 512], P(('dp', 'rep')), may hold values from -8 to 8
- cotangent: bfloat16 [32, 64, 64, 512], P(('dp', 'rep')), may hold values from -6 to 6
- holes: int32 [32, 64, 64], P(('dp', 'rep')), may hold values from 0 to 1
- w_ll: bfloat16 [1, 1152, 128], P(None, 'dp'), may hold values from -0.09375 to 0.09375
- w_gl: bfloat16 [1, 3456, 128], P(None, 'dp'), may hold values from -0.09375 to 0.09375
- w_lg: bfloat16 [1, 1152, 384], P(None, 'dp'), may hold values from -0.1875 to 0.1875
- w_in: bfloat16 [1, 384, 192], P(None, 'dp'), may hold values from -0.3125 to 0.3125
- w_fu: bfloat16 [1, 384, 384], P(None, 'dp'), may hold values from -0.3125 to 0.3125
- w_out: bfloat16 [1, 192, 384], P(None, 'dp'), may hold values from -0.4375 to 0.4375
- gains: bfloat16 [1, 1088], P(None, 'dp'), may hold values from 0.5 to 1.5
- biases: bfloat16 [1, 1088], P(None, 'dp'), may hold values from -2 to 2
Outputs:
- block_out: bfloat16 [32, 64, 64, 512], P(('dp', 'rep'))
- input_grad: bfloat16 [32, 64, 64, 512], P(('dp', 'rep'))
- grad_ll: float32 [1, 1152, 128], P(None, 'dp')
- grad_gl: float32 [1, 3456, 128], P(None, 'dp')
- grad_lg: float32 [1, 1152, 384], P(None, 'dp')
- grad_in: float32 [1, 384, 192], P(None, 'dp')
- grad_fu: float32 [1, 384, 384], P(None, 'dp')
- grad_out: float32 [1, 192, 384], P(None, 'dp')
- gain_grad: float32 [1, 1088], P(None, 'dp')
- bias_grad: float32 [1, 1088], P(None, 'dp')
The draws below stay inside these ranges and needn't reach their ends.
All inputs are finite; a program needn't handle non-finite values.
Results may differ from the reference program's by a relative error of at most 0.013.
Values may be sent and summed in bfloat16 or wider, within the bound.
A program may use at most 192 MiB of HBM per device.

```python
import jax
import jax.numpy as jnp
from jax import lax

LOC = 128
GLO = 384
HALF = 192
SIDE = 64
LAYERS = 1
IMAGES = 32
NORMS = 1088


def draw_features(key, part):
    key = jax.random.fold_in(key, 11)
    noise_key, channel_key = jax.random.split(key)
    shape = (IMAGES, SIDE, SIDE, LOC + GLO)
    position_share = jnp.arange(IMAGES, dtype=jnp.float32) / max(IMAGES - 1, 1)
    channel_scale = jnp.exp(jax.random.uniform(channel_key, (LOC + GLO,), minval=0.0, maxval=1.1))
    values = jax.random.normal(noise_key, shape)
    image_scale = 0.5 + position_share
    drawn = values * image_scale[:, None, None, None] * channel_scale
    return jnp.clip(drawn, -8.0, 8.0).astype(jnp.bfloat16)


def draw_holes(key, part):
    key = jax.random.fold_in(key, 23)
    level_key, pixel_key = jax.random.split(key)
    level = jax.random.randint(level_key, (IMAGES,), 0, 10)
    percent = level * level * 90 // 81
    rolled = jax.random.randint(pixel_key, (IMAGES, SIDE, SIDE), 0, 100)
    return (rolled < percent[:, None, None]).astype(jnp.int32)


def block_scale(rng, extent, pieces, smallest, top_value):
    def one(dim, blocks):
        draws = jax.random.uniform(jax.random.fold_in(jax.random.fold_in(rng, 6), dim), (blocks,), jnp.float32, smallest / len(pieces), top_value / len(pieces))
        return jnp.repeat(jnp.exp(draws), extent[dim] // blocks).reshape((-1,) + (1,) * (len(extent) - dim - 1))

    factor_of = one(*pieces[0])
    for cut in pieces[1:]:
        factor_of = factor_of * one(*cut)
    return factor_of


def bell_draw(rng, dims, deviation, bound, pieces=(), kind=jnp.bfloat16):
    entries = jax.random.normal(rng, dims, jnp.float32) * deviation
    if len(pieces) > 0:
        entries = block_scale(rng, dims, pieces, -0.22, 0.18) * entries
    return jnp.clip(entries, min=-bound, max=bound).astype(kind)


def setup_inputs(seed: int = 0) -> dict:
    keys = jax.random.split(jax.random.key(seed), 12)
    return {
        "features": draw_features(jax.random.fold_in(keys[11], 71), 0),
        "cotangent": bell_draw(keys[1], (IMAGES, SIDE, SIDE, LOC + GLO), 1.0, 6.0, ((0, 32),)),
        "holes": draw_holes(jax.random.fold_in(keys[11], 71), 0),
        "w_ll": bell_draw(keys[3], (LAYERS, 9 * LOC, LOC), (9 * (LOC + GLO)) ** -0.5, 0.09375, ((1, 8),)),
        "w_gl": bell_draw(keys[4], (LAYERS, 9 * GLO, LOC), (9 * (LOC + GLO)) ** -0.5, 0.09375, ((1, 8),)),
        "w_lg": bell_draw(keys[5], (LAYERS, 9 * LOC, GLO), (9 * LOC) ** -0.5, 0.1875, ((1, 8),)),
        "w_in": bell_draw(keys[6], (LAYERS, GLO, HALF), GLO ** -0.5, 0.3125, ((1, 8),)),
        "w_fu": bell_draw(keys[7], (LAYERS, GLO, GLO), GLO ** -0.5, 0.3125, ((1, 8),)),
        "w_out": bell_draw(keys[8], (LAYERS, HALF, GLO), HALF ** -0.5, 0.4375, ((1, 8),)),
        "gains": jnp.clip(1.0 + 0.1 * jax.random.normal(keys[9], (LAYERS, NORMS), jnp.float32), 0.5, 1.5).astype(jnp.bfloat16),
        "biases": bell_draw(keys[10], (LAYERS, NORMS), 0.5, 2.0, ((1, 8),)),
    }


EPS = 1e-05
HIGH = lax.Precision.HIGHEST

@jax.custom_vjp
def low(v):
    return lax.optimization_barrier(v.astype(jnp.bfloat16)).astype(jnp.float32)

@jax.custom_vjp
def low_back(v):
    return v

def low_keep(v):
    return (low(v), None)

def low_pass(kept, grad):
    return (grad,)

def back_keep(v):
    return (v, None)

def back_low(kept, grad):
    return (low(grad),)
low.defvjp(low_keep, low_pass)
low_back.defvjp(back_keep, back_low)

def gelu(values):
    return jax.nn.gelu(values, approximate=True)

def batch_norm(values, gain, bias):
    mean = lax.optimization_barrier(jnp.mean(values, axis=(0, 1, 2)))
    square = lax.optimization_barrier(jnp.mean(values * values, axis=(0, 1, 2)))
    return gain * (values - mean) * lax.rsqrt(square - mean * mean + EPS) + bias

def conv_three(field, weight):
    kernel = weight.reshape(3, 3, field.shape[-1], weight.shape[-1])
    return lax.conv_general_dilated(field, kernel, (1, 1), ((1, 1), (1, 1)), dimension_numbers=('NHWC', 'HWIO', 'NHWC'), precision=HIGH)

def split_row(row):
    widths = (HALF, GLO, LOC, GLO)
    parts = []
    offset = 0
    for width in widths:
        parts.append(row[offset:offset + width])
        offset = offset + width
    return parts

def ffc_layer(loc_in, glo_in, weights, gain_row, bias_row):
    w_ll, w_gl, w_lg, w_in, w_fu, w_out = weights
    gain_parts = split_row(gain_row)
    bias_parts = split_row(bias_row)

    def first_section(pair):
        loc_one = pair[0][None]
        glo_one = pair[1][None]
        pre_loc = conv_three(loc_one, w_ll) + conv_three(glo_one, w_gl)
        cross = conv_three(loc_one, w_lg)
        pre_spec = jnp.einsum('bhwc,cd->bhwd', glo_one, w_in, precision=HIGH)
        return (pre_loc[0], cross[0], pre_spec[0])
    pre_loc, cross, pre_spec = lax.map(jax.checkpoint(first_section), (loc_in, glo_in))
    pre_loc = low_back(pre_loc)
    pre_spec = low_back(pre_spec)
    spectral = gelu(batch_norm(pre_spec, gain_parts[0], bias_parts[0]))

    def second_section(one_field):
        spectrum = jnp.fft.rfft2(one_field, axes=(0, 1), norm='ortho')
        stacked = low(jnp.concatenate([jnp.real(spectrum), jnp.imag(spectrum)], axis=-1))
        return jnp.einsum('hwc,cd->hwd', stacked, w_fu, precision=HIGH)
    pre_freq = low_back(lax.map(jax.checkpoint(second_section), spectral))
    mixed = gelu(batch_norm(pre_freq, gain_parts[1], bias_parts[1]))

    def third_section(pair):
        one_spec, one_freq = pair
        back = jnp.fft.irfft2(one_freq[..., :HALF] + 1j * one_freq[..., HALF:], s=(SIDE, SIDE), axes=(0, 1), norm='ortho')
        joined = low(one_spec + back)
        return jnp.einsum('hwc,cd->hwd', joined, w_out, precision=HIGH)
    transform = lax.map(jax.checkpoint(third_section), (spectral, mixed))
    pre_glo = low_back(cross + transform)
    out_loc = gelu(batch_norm(pre_loc, gain_parts[2], bias_parts[2]))
    out_glo = gelu(batch_norm(pre_glo, gain_parts[3], bias_parts[3]))
    return (out_loc, out_glo)

def block(start, w_ll, w_gl, w_lg, w_in, w_fu, w_out, gains, biases):
    loc_in = start[..., :LOC]
    glo_in = start[..., LOC:]
    for layer in range(LAYERS):
        weights = (w_ll[layer], w_gl[layer], w_lg[layer], w_in[layer], w_fu[layer], w_out[layer])
        loc_in, glo_in = ffc_layer(low(loc_in), low(glo_in), weights, gains[layer], biases[layer])
    return start + jnp.concatenate([loc_in, glo_in], axis=-1)

def reference(features, cotangent, holes, w_ll, w_gl, w_lg, w_in, w_fu, w_out, gains, biases):
    params = tuple((a.astype(jnp.float32) for a in (w_ll, w_gl, w_lg, w_in, w_fu, w_out, gains, biases)))
    start = features.astype(jnp.float32)
    weighting = cotangent.astype(jnp.float32) * (0.25 + holes.astype(jnp.float32))[..., None]
    result, pullback = jax.vjp(block, start, *params)
    grads = pullback(weighting)
    return (result.astype(jnp.bfloat16), grads[0].astype(jnp.bfloat16), grads[1], grads[2], grads[3], grads[4], grads[5], grads[6], grads[7], grads[8])
```

```python
import functools
import math

import jax
import jax.numpy as jnp
import ml_dtypes
import numpy as np
from jax import lax
from jax.experimental import pallas as pl
from jax.experimental.pallas import tpu as pltpu
from jax.sharding import PartitionSpec as P

EPS = 1e-05
K0 = math.sqrt(2.0 / math.pi)
K1 = 0.044715
MESH = pl.DeviceIdType.MESH
F32 = jnp.float32
BF = jnp.bfloat16
SIDE = 64
LOC = 128
GLO = 384
HALF = 192
ALL = LOC + GLO
WIDTHS = (HALF, GLO, LOC, GLO)
POS = SIDE * SIDE
FREQ = SIDE * (SIDE // 2 + 1)


def dft_table():
    a = np.arange(16)[:, None, None, None, None]
    j = np.arange(4)[None, :, None, None, None]
    w = np.arange(64)[None, None, :, None, None]
    k1 = np.arange(4)[None, None, None, :, None]
    l = np.arange(32)[None, None, None, None, :]
    angle = 2 * np.pi / 64 * (((a + 16 * j) * k1 + w * l) % 64)
    main_re = np.cos(angle).reshape(16, 256, 128) / 64
    main_im = -np.sin(angle).reshape(16, 256, 128) / 64
    k = np.arange(64)[None, None, None, :]
    a, j, w = a[..., 0], j[..., 0], w[..., 0]
    angle = 2 * np.pi / 64 * (((a + 16 * j) * k + 32 * w) % 64)
    ext_re = np.cos(angle).reshape(16, 256, 64) / 64
    ext_im = -np.sin(angle).reshape(16, 256, 64) / 64
    return np.concatenate([main_re, main_im, ext_re, ext_im], axis=-1).astype(ml_dtypes.bfloat16)


def dot(a, b, ca=1, cb=0):
    return lax.dot_general(a, b, (((ca,), (cb,)), ((), ())), preferred_element_type=F32)


def gelu_value(y):
    half = 0.5 * y
    return half + half * jnp.tanh(y * (K0 + K0 * K1 * (y * y)))


def gelu_both(y):
    y2 = y * y
    t = jnp.tanh(y * (K0 + K0 * K1 * y2))
    half = 0.5 * y
    slope = 0.5 + 0.5 * t + half * (1.0 - t * t) * (K0 + 3.0 * K0 * K1 * y2)
    return half + half * t, slope


def gelu_slope(y):
    return gelu_both(y)[1]


def cmul(z, c, s):
    return (z[0] * c - z[1] * s, z[0] * s + z[1] * c)


def dft4(z, sign):
    (ar, ai), (br, bi), (cr, ci), (dr, di) = z
    pr, pi, qr, qi = ar + cr, ai + ci, ar - cr, ai - ci
    rr, ri, sr, si = br + dr, bi + di, br - dr, bi - di
    tr, ti = (si, -sr) if sign < 0 else (-si, sr)
    return [(pr + rr, pi + ri), (qr + tr, qi + ti), (pr - rr, pi - ri), (qr - tr, qi - ti)]


def dft16(z, sign):
    cols = []
    for n2 in range(4):
        part = dft4([z[4 * n1 + n2] for n1 in range(4)], sign)
        for k1 in range(1, 4):
            e = n2 * k1
            if e == 0:
                continue
            if e == 4:
                re, im = part[k1]
                part[k1] = (im, -re) if sign < 0 else (-im, re)
            else:
                ang = sign * 2 * math.pi * e / 16
                part[k1] = cmul(part[k1], math.cos(ang), math.sin(ang))
        cols.append(part)
    out = [None] * 16
    for k1 in range(4):
        part = dft4([cols[n2][k1] for n2 in range(4)], sign)
        for k2 in range(4):
            out[k1 + 4 * k2] = part[k2]
    return out


def dyf_pos(t):
    if t < 12:
        return 2304 + 384 * (t // 3), 128 + 128 * (t % 3)
    u = t - 12
    return 1152 + 384 * (u // 2), 256 + 128 * (u % 2)


def rows8(x):
    acc = x[0:8]
    for r in range(8, x.shape[0], 8):
        acc = acc + x[r : r + 8]
    return acc


def lane_pair(x):
    return x[:, 0:128] + x[:, 128:256]


class Ring:
    def __init__(self, dps, reps):
        self.D, self.R = dps, reps
        self.N = dps * reps
        self.dp = lax.axis_index("dp")
        self.rp = lax.axis_index("rep")
        self.me = self.dp * reps + self.rp
        self.core = lax.rem(self.rp, 2)
        self.x = lax.div(self.rp, 2)

    def dev(self, i):
        return (lax.div(i, self.R), lax.rem(i, self.R))

    def barrier(self):
        sem = pltpu.get_barrier_semaphore()

        def body(d, c):
            peer = lax.rem(self.me + d, self.N)
            pl.semaphore_signal(sem, inc=1, device_id=self.dev(peer), device_id_type=MESH)
            return c

        lax.fori_loop(1, self.N, body, 0)
        pl.semaphore_wait(sem, self.N - 1)

    def send(self, src, dst, ss, rs, device):
        pltpu.make_async_remote_copy(
            src_ref=src, dst_ref=dst, send_sem=ss, recv_sem=rs, device_id=device, device_id_type=MESH
        ).start()

    def sibling(self):
        return (self.dp, self.rp + 1 - 2 * self.core)

    def across(self):
        return (self.dp, lax.rem(self.rp + 2, 4))


def await_bytes(ref, sem):
    pltpu.make_async_copy(ref, ref, sem).wait()


def kernel(dps, reps, fused, *refs):
    it = iter(refs)
    feat_h, cot_h, holes, tab_h = next(it), next(it), next(it), next(it)
    if fused:
        w_ll, w_gl, w_lg, w_in, w_fu, w_out, gain_in, bias_in = (next(it) for _ in range(8))
    else:
        WCAT, WGLN, WINT, WFU, WFUT, WOUT, GBI = (next(it) for _ in range(7))
    block_out, input_grad, norm_out = next(it), next(it), next(it)
    if fused:
        flat_out = next(it)
    else:
        out_ll, out_gl, out_lg, out_in, out_fu, out_out = (next(it) for _ in range(6))
    F, WF, Z3, D3, PX, DY, PS, ST, PF, Y, J, DC, A = (next(it) for _ in range(13))
    EXA, EXB, DYX, ACC, ACF, COLS, COLF, ROWP, GFU, GOUT, GIN = (next(it) for _ in range(11))
    ARB, ar_s, ar_r, COTB, OUTB, cot_sem, out_sem, in_sem, WGL = (next(it) for _ in range(9))
    if fused:
        WCAT, WINT, WFU, WFUT, WOUT = (next(it) for _ in range(5))
        WI, GBB, WFO, WB, OWNI, OWNF, OWNB, g_sem = (next(it) for _ in range(8))
        RB, RF, RI = ([next(it) for _ in range(4)] for _ in range(3))
        GI, rs_sem = next(it), next(it)
    ring = Ring(dps, reps)
    D, R, N = ring.D, ring.R, ring.N
    me, dp, rp = ring.me, ring.dp, ring.rp
    count = float(POS * N)
    fcount = float(FREQ * N)

    copy_f = pltpu.make_async_copy(feat_h.at[:, :, LOC:ALL], F.at[1:65], in_sem.at[0])
    copy_f.start()
    copy_l = pltpu.make_async_copy(feat_h.at[:, :, 0:LOC], Z3.at[1:65, :, 128:256], in_sem.at[1])
    copy_l.start()
    copy_a = pltpu.make_async_copy(tab_h, A, in_sem.at[2])
    copy_a.start()

    def ar_start(k):
        b = k % 2

        def body(d, c):
            peer = lax.rem(me + d, N)
            ring.send(ARB.at[b, me], ARB.at[b, me], ar_s.at[k], ar_r.at[k], ring.dev(peer))
            return c

        lax.fori_loop(1, N, body, 0)

    def ar_wait(k):
        b = k % 2
        await_bytes(ARB.at[b, pl.ds(0, N - 1)], ar_r.at[k])
        await_bytes(ARB.at[b, pl.ds(0, N - 1)], ar_s.at[k])
        return jnp.sum(ARB[b], axis=0)

    q_f, q_b = 64, 256
    if fused:
        OWNI[0:48, :] = w_in[:, 0:128]
        OWNI[48:96, :] = jnp.concatenate([w_in[:, 128:192], jnp.zeros((48, 64), BF)], axis=1)
        for j in range(3):
            OWNF[48 * j : 48 * j + 48, :] = w_fu[:, 128 * j : 128 * j + 128]
            part = w_out[:, 128 * j : 128 * j + 128].astype(F32)
            part = jnp.concatenate([part, jnp.zeros((8, 128), F32)], axis=0)
            OWNF[144 + 32 * j : 176 + 32 * j, :] = part.astype(BF)
            OWNB[576 + 144 * j : 720 + 144 * j, :] = w_lg[:, 128 * j : 128 * j + 128]
        OWNF[240:256, :] = jnp.zeros((16, 128), BF)
        OWNB[0:432, :] = w_gl[...]
        OWNB[432:576, :] = w_ll[...]
        OWNB[1008:1024, :] = jnp.zeros((16, 128), BF)
        own = gain_in.shape[1]
        both = jnp.concatenate([gain_in[...], bias_in[...]], axis=0).astype(F32)
        both = jnp.concatenate([both, jnp.zeros((2, 1152 - own), F32)], axis=1)
        both = jnp.concatenate([both, jnp.zeros((6, 1152), F32)], axis=0)
        both = pltpu.roll(both, own * dp, axis=1)
        GBB[dp] = jnp.zeros((24, 128), F32)
        for j in range(9):
            GBB[dp, j : j + 1, :] = both[0:1, 128 * j : 128 * j + 128]
            GBB[dp, 9 + j : 10 + j, :] = both[1:2, 128 * j : 128 * j + 128]
        WI[dp] = OWNI[...]
        WFO[dp, pl.ds(pl.multiple_of(rp * q_f, 16), q_f)] = OWNF[pl.ds(pl.multiple_of(rp * q_f, 16), q_f)]
        WB[dp, pl.ds(pl.multiple_of(rp * q_b, 16), q_b)] = OWNB[pl.ds(pl.multiple_of(rp * q_b, 16), q_b)]

    ring.barrier()

    def quarter(ref, q, index):
        return ref.at[:, pl.ds(pl.multiple_of(index * q, 16), q)]

    def spread(src, dst, ss, rs):
        def body(d, c):
            ring.send(src, dst, ss, rs, (lax.rem(dp + d, D), rp))
            return c

        lax.fori_loop(1, D, body, 0)

    class Gather:
        def __init__(self, own_ref, buf, q, base):
            self.own, self.buf, self.q, self.base = own_ref, buf, q, base

        def sem(self, i):
            return g_sem.at[self.base + i]

        def first(self):
            rows = pl.ds(pl.multiple_of(rp * self.q, 16), self.q)
            spread(self.own.at[rows], self.buf.at[dp, rows], self.sem(0), self.sem(1))

        def second(self):
            await_bytes(self.buf.at[pl.ds(0, D - 1), pl.ds(0, self.q)], self.sem(1))
            part = quarter(self.buf, self.q, rp)
            ring.send(part, part, self.sem(2), self.sem(3), ring.across())
            ring.send(part, part, self.sem(4), self.sem(5), ring.sibling())

        def third(self):
            one = self.buf.at[:, pl.ds(0, self.q)]
            await_bytes(one, self.sem(3))
            part = quarter(self.buf, self.q, lax.rem(rp + 2, 4))
            ring.send(part, part, self.sem(6), self.sem(7), ring.sibling())

        def last(self):
            one = self.buf.at[:, pl.ds(0, self.q)]
            await_bytes(one, self.sem(5))
            await_bytes(one, self.sem(7))
            await_bytes(self.buf.at[pl.ds(0, D - 1), pl.ds(0, self.q)], self.sem(0))
            await_bytes(one, self.sem(2))
            await_bytes(one, self.sem(4))
            await_bytes(one, self.sem(6))

    if fused:
        spread(OWNI, WI.at[dp], g_sem.at[0], g_sem.at[1])
        spread(GBB.at[dp], GBB.at[dp], g_sem.at[2], g_sem.at[3])
        gather_f = Gather(OWNF, WFO, q_f, 4)
        gather_b = Gather(OWNB, WB, q_b, 12)
        gather_f.first()
        gather_b.first()

    edge_row = jnp.zeros((SIDE, 384), BF)
    for ref in (F, Z3, D3):
        ref[0] = edge_row
        ref[65] = edge_row
    DC[0] = jnp.zeros((SIDE, ALL), BF)
    DC[65] = jnp.zeros((SIDE, ALL), BF)

    def make_wf(h, c):
        row = 0.25 + holes[pl.ds(h, 1), :].astype(F32)
        row = jnp.concatenate([row, row], axis=1)
        WF[h] = (jnp.broadcast_to(row, (128, 128)).T)[0:64].astype(BF)
        return c

    lax.fori_loop(0, SIDE, make_wf, 0)

    def shifted(x, lanes_mask_first, by):
        moved = pltpu.roll(x, by % x.shape[0], axis=0)
        at = lax.rem(lax.broadcasted_iota(jnp.int32, x.shape, 0), SIDE)
        return jnp.where(at == lanes_mask_first, 0.0, moved)

    copy_l.wait()

    def make_z3(h, c):
        x = Z3[h + 1, :, 128:256].astype(F32)
        Z3[h + 1, :, 0:128] = shifted(x, 0, 1).astype(BF)
        Z3[h + 1, :, 256:384] = shifted(x, 63, -1).astype(BF)
        return c

    lax.fori_loop(0, SIDE, make_z3, 0)
    copy_f.wait()

    if fused:
        await_bytes(WI.at[pl.ds(0, D - 1)], g_sem.at[1])
        first = jnp.concatenate([WI[s, 0:48] for s in range(D)], axis=0).astype(F32)
        WINT[0:128, :] = first.T.astype(BF)
        first = jnp.concatenate([WI[s, 48:96] for s in range(D)], axis=0).astype(F32)
        WINT[128:192, :] = (first.T)[0:64].astype(BF)

    def tile(ref, h0, lo, hi):
        return jnp.concatenate([ref[h0 + 16 * j + 1, :, lo:hi] for j in range(4)], axis=0)

    ACC[...] = jnp.zeros_like(ACC)

    def input_proj(h0, c):
        ps = dot(WINT[...], tile(F, h0, 0, GLO), 1, 1)
        PS[h0] = ps
        ACC[0:HALF] += lane_pair(ps)
        ACC[HALF : 2 * HALF] += lane_pair(ps * ps)
        return c

    lax.fori_loop(0, 16, input_proj, 0)

    def row_of(lo, hi):
        parts = []
        for r in range(lo, hi, 128):
            n = min(128, hi - r)
            x = ACF[r : r + n] if hi > 384 or lo >= 384 else ACC[r : r + n]
            parts.append(x)
        return parts

    def to_row(x):
        n = x.shape[0]
        if n < 128:
            x = jnp.concatenate([x, jnp.zeros((128 - n, 128), F32)], axis=0)
        return jnp.sum(x.T, axis=0, keepdims=True)

    def put_rows(k, at, rows):
        b = k % 2
        for i, row in enumerate(rows):
            ARB[b, me, at + i : at + i + 1, :] = row

    def put_zero(k, at):
        ARB[k % 2, me, at:8, :] = jnp.zeros((8 - at, 128), F32)

    def spec_rows():
        return [to_row(ACC[0:128]), to_row(ACC[128:192]), to_row(ACC[192:320]), to_row(ACC[320:384])]

    put_rows(0, 0, spec_rows())
    put_zero(0, 4)
    ar_start(0)

    if fused:
        gather_f.second()
        await_bytes(GBB.at[pl.ds(0, D - 1)], g_sem.at[3])
        gb = GBB[0]
        for s in range(1, D):
            gb = gb + GBB[s]
    else:
        gb = GBI[...]
    wide = []
    for kind in range(2):
        row = jnp.concatenate([gb[9 * kind + j : 9 * kind + j + 1, :] for j in range(9)], axis=1)
        wide.append(jnp.broadcast_to(row, (8, 1152)))

    def piece(kind, offset, width):
        return pltpu.roll(wide[kind], (1152 - offset) % 1152, axis=1)[0:1, 0:width]

    def col(row):
        return jnp.broadcast_to(row, (128, 128)).T

    for kind, at in ((0, 2), (1, 3)):
        spec = piece(kind, 0, 256)
        COLS[at, 0:128] = col(spec[:, 0:128])
        COLS[at, 128:192] = col(spec[:, 128:256])[0:64]
        freq = piece(kind, 192, 384)
        for j in range(3):
            COLF[at, 128 * j : 128 * j + 128] = col(freq[:, 128 * j : 128 * j + 128])
        ROWP[at : at + 1, 0:128] = piece(kind, 576, 128)
        ROWP[at : at + 1, 128:512] = piece(kind, 704, 384)

    def moments(total, square, n):
        mean = total / n
        scale = lax.rsqrt(square / n - mean * mean + EPS)
        return scale, mean * scale

    if fused:
        gather_b.second()
        gather_f.third()

    copy_a.wait()
    tot = ar_wait(0)
    for r, (lo, n) in enumerate(((0, 128), (128, 64))):
        scale, ms = moments(tot[r : r + 1], tot[r + 2 : r + 3], count)
        COLS[0, lo : lo + n] = col(scale)[0:n]
        COLS[1, lo : lo + n] = col(ms)[0:n]
    COLS[6] = COLS[0] * COLS[2]

    def two(x):
        return jnp.concatenate([x, x], axis=1)

    EXA[...] = jnp.zeros_like(EXA)

    def spec_front(h0, c):
        rows = pl.ds(pl.multiple_of(h0 * HALF, 8), HALF)
        xh = PS[h0] * two(COLS[0]) - two(COLS[1])
        sp = gelu_value(xh * two(COLS[2]) + two(COLS[3]))
        DY[rows, 0:256] = sp
        res = dot(sp.astype(BF), A[h0])
        DY[rows, 256:512] = res[:, 0:256]
        EXA[...] += res[:, 256:384]
        return c

    lax.fori_loop(0, 16, spec_front, 0)
    low_half = lax.broadcasted_iota(jnp.int32, (HALF, 128), 1) < 64

    def split_ext(x):
        re = jnp.where(low_half, x, 0.0)
        im = jnp.where(low_half, pltpu.roll(x, 64, axis=1), 0.0)
        return re, im

    def join_ext(re, im):
        return jnp.where(low_half, re, pltpu.roll(im, 64, axis=1))

    ext_re, ext_im = split_ext(EXA[...])
    ST[16, 0:HALF] = ext_re.astype(BF)
    ST[16, HALF : 2 * HALF] = ext_im.astype(BF)

    def grab(ref, g, base):
        z = []
        for a in range(16):
            rows = pl.ds(pl.multiple_of(a * HALF + g * 8, 8), 8)
            z.append((ref[rows, base : base + 128], ref[rows, base + 128 : base + 256]))
        return z

    def fwd_fft(i, c):
        halves = [dft16(grab(DY, 2 * i + s, 256), -1) for s in range(2)]
        for k in range(16):
            for comp in range(2):
                both = jnp.concatenate([halves[0][k][comp], halves[1][k][comp]], axis=0)
                ST[k, pl.ds(pl.multiple_of(comp * HALF + i * 16, 16), 16)] = both.astype(BF)
        return c

    lax.fori_loop(0, 12, fwd_fft, 0)

    if fused:
        gather_b.third()
        gather_f.last()
        for j in range(3):
            fu = jnp.concatenate([WFO[s, 48 * j : 48 * j + 48] for s in range(D)], axis=0)
            WFU[:, 128 * j : 128 * j + 128] = fu
            WFUT[128 * j : 128 * j + 128, :] = fu.astype(F32).T.astype(BF)
            wo = jnp.concatenate(
                [WFO[s, 144 + 32 * j : 176 + 32 * j].astype(F32)[0:24] for s in range(D)], axis=0
            )
            WOUT[:, 128 * j : 128 * j + 128] = wo.astype(BF)
    ACF[...] = jnp.zeros_like(ACF)

    def unit(t, c):
        pf = dot(WFUT[...], jnp.concatenate([ST[2 * t], ST[2 * t + 1]], axis=1))
        PF[2 * t] = pf[:, 0:128]
        PF[2 * t + 1] = pf[:, 128:256]
        ACF[0:384] += lane_pair(pf)
        ACF[384:768] += lane_pair(pf * pf)
        return c

    lax.fori_loop(0, 8, unit, 0)
    pf = dot(WFUT[...], ST[16])
    PF[16] = pf
    ACF[0:384] += pf
    ACF[384:768] += pf * pf

    def freq_rows():
        return [to_row(ACF[128 * j : 128 * j + 128]) for j in range(6)]

    put_rows(1, 0, freq_rows())
    put_zero(1, 6)
    ar_start(1)

    if fused:
        gather_b.last()
        for s in range(D):
            WCAT[144 * s : 144 * s + 144, 0:128] = WB[s, 432:576]
            for j in range(3):
                WCAT[144 * s : 144 * s + 144, 128 + 128 * j : 256 + 128 * j] = WB[s, 576 + 144 * j : 720 + 144 * j]

    def gl_runs():
        runs = []
        share = 3456 // D
        row = 0
        while row < 3456:
            n = min(384 - row % 384, share - row % share)
            runs.append((row // 384, row % 384, row // share, row % share, n))
            row += n
        return runs

    if fused:
        for tap, c0, s, r0, n in gl_runs():
            WGL[tap // 3, c0 : c0 + n, 128 * (tap % 3) : 128 * (tap % 3) + 128] = WB[s, r0 : r0 + n]
    else:
        for tap in range(9):
            WGL[tap // 3, :, 128 * (tap % 3) : 128 * (tap % 3) + 128] = WGLN[384 * tap : 384 * tap + 384]

    ROWP[8:16, :] = jnp.zeros((8, ALL), F32)
    ACCR = ROWP

    def slab(ref, i, off, n):
        return ref[pl.ds(8 * i + off, 8), :, 0:n].reshape(512, n)

    def conv_fwd(i, c):
        rows = pl.ds(pl.multiple_of(512 * i, 512), 512)
        lhs = jnp.concatenate([slab(Z3, i, a, 384) for a in range(3)], axis=1)
        res = dot(lhs, WCAT[...])
        PX[rows, 128:512] = res[:, 128:512]
        lhs = jnp.concatenate([slab(F, i, a, 384) for a in range(3)], axis=1)
        gl = dot(lhs, WGL[...].reshape(1152, 384))
        total = res[:, 0:128] + gl[:, 128:256] + shifted(gl[:, 0:128], 0, 1) + shifted(gl[:, 256:384], 63, -1)
        PX[rows, 0:128] = total
        ACCR[8:16, 0:128] += rows8(total)
        ACCR[8:16, 128:256] += rows8(total * total)
        return c

    lax.fori_loop(0, 8, conv_fwd, 0)
    put_rows(2, 0, [jnp.sum(ACCR[8:16, 128 * j : 128 * j + 128], axis=0, keepdims=True) for j in range(2)])
    put_zero(2, 2)

    tot = ar_wait(1)
    ar_start(2)
    for j in range(3):
        scale, ms = moments(tot[j : j + 1], tot[j + 3 : j + 4], fcount)
        COLF[0, 128 * j : 128 * j + 128] = col(scale)
        COLF[1, 128 * j : 128 * j + 128] = col(ms)
    COLF[6] = COLF[0] * COLF[2]
    lane = lax.broadcasted_iota(jnp.int32, (8, 128), 1)
    doubled = jnp.where(lax.rem(lane, 32) == 0, 1.0, 2.0).astype(F32)

    def freq_act(v, rows):
        xh = v * COLF[0, rows] - COLF[1, rows]
        return xh, xh * COLF[2, rows] + COLF[3, rows]

    def inv_fft(i, c):
        halves = []
        for s in range(2):
            z = []
            rr = pl.ds(pl.multiple_of(16 * i + 8 * s, 8), 8)
            ri = pl.ds(pl.multiple_of(HALF + 16 * i + 8 * s, 8), 8)
            for k in range(16):
                re = gelu_value(freq_act(PF[k, rr], rr)[1]) * doubled
                im = gelu_value(freq_act(PF[k, ri], ri)[1]) * doubled
                z.append((re, im))
            halves.append(dft16(z, 1))
        for a in range(16):
            for comp in range(2):
                both = jnp.concatenate([halves[0][a][comp], halves[1][a][comp]], axis=0)
                Y[a, pl.ds(pl.multiple_of(i * 16, 16), 16), 128 * comp : 128 * comp + 128] = both.astype(BF)
        return c

    lax.fori_loop(0, 12, inv_fft, 0)
    mixed = gelu_value((PF[16] * COLF[0] - COLF[1]) * COLF[2] + COLF[3])
    EXB[...] = join_ext(mixed[0:HALF], mixed[HALF : 2 * HALF]).astype(BF)
    ROWP[8:16, :] = jnp.zeros((8, ALL), F32)
    ROWP[16:24, :] = jnp.zeros((8, ALL), F32)

    def join(h0, c):
        rows = pl.ds(pl.multiple_of(h0 * HALF, 8), HALF)
        back = dot(jnp.concatenate([Y[h0], EXB[...]], axis=1), A[h0], 1, 1)
        joined = (DY[rows, 0:256] + back).astype(BF)
        J[h0] = joined
        pg = dot(joined, WOUT[...], 0, 0)
        for j in range(4):
            at = pl.ds(pl.multiple_of((h0 + 16 * j) * SIDE, SIDE), SIDE)
            v = PX[at, 128:512] + pg[64 * j : 64 * j + 64]
            PX[at, 128:512] = v
            ROWP[8:16, 128:512] += rows8(v)
            ROWP[16:24, 128:512] += rows8(v * v)
        return c

    lax.fori_loop(0, 16, join, 0)

    def put_norm_rows(k, lo, tiles):
        for j in range(tiles):
            at = lo + 128 * j
            put_rows(k, j, [jnp.sum(ROWP[8:16, at : at + 128], axis=0, keepdims=True)])
            put_rows(k, tiles + j, [jnp.sum(ROWP[16:24, at : at + 128], axis=0, keepdims=True)])
        put_zero(k, 2 * tiles)

    put_norm_rows(3, 128, 3)
    tot = ar_wait(2)
    ar_start(3)
    scale, ms = moments(tot[0:1], tot[1:2], count)
    ROWP[0:1, 0:128] = scale
    ROWP[1:2, 0:128] = ms

    def cot_copy(i, lo, hi):
        return pltpu.make_async_copy(
            cot_h.at[pl.ds(8 * i, 8), :, lo:hi], COTB.at[lax.rem(i, 2), :, :, lo:hi], cot_sem.at[lax.rem(i, 2)]
        )

    def out_copy(dst, i, lo, hi):
        return pltpu.make_async_copy(
            OUTB.at[lax.rem(i, 2), :, :, lo:hi], dst.at[pl.ds(8 * i, 8), :, lo:hi], out_sem.at[lax.rem(i, 2)]
        )

    def out_norm(lo, hi):
        cot_copy(0, lo, hi).start()
        ROWP[8:16, lo:hi] = jnp.zeros((8, hi - lo), F32)
        ROWP[16:24, lo:hi] = jnp.zeros((8, hi - lo), F32)

        def chunk(i, c):
            slot = lax.rem(i, 2)
            cot_copy(i, lo, hi).wait()

            @pl.when(i < 7)
            def _():
                cot_copy(i + 1, lo, hi).start()

            @pl.when(i > 1)
            def _():
                out_copy(block_out, i - 2, lo, hi).wait()

            def one(hh, c2):
                h = 8 * i + hh
                for r in (0, 32):
                    at = pl.ds(pl.multiple_of(h * SIDE + r, 32), 32)
                    wf = WF[h, r : r + 32].astype(F32)
                    for l0 in range(lo, hi, 128):
                        ls = slice(l0, l0 + 128)
                        xh = PX[at, ls] * ROWP[0:1, ls] - ROWP[1:2, ls]
                        value, slope = gelu_both(xh * ROWP[2:3, ls] + ROWP[3:4, ls])
                        dy = slope * (COTB[slot, hh, r : r + 32, ls].astype(F32) * wf)
                        DY[at, ls] = dy
                        if l0 == 0:
                            base = Z3[h + 1, r : r + 32, 128:256]
                        else:
                            base = F[h + 1, r : r + 32, l0 - 128 : l0]
                        OUTB[slot, hh, r : r + 32, ls] = (base.astype(F32) + value).astype(BF)
                        ROWP[8:16, ls] += rows8(dy)
                        ROWP[16:24, ls] += rows8(dy * xh)
                return c2

            lax.fori_loop(0, 8, one, 0)
            out_copy(block_out, i, lo, hi).start()
            return c

        lax.fori_loop(0, 8, chunk, 0)
        out_copy(block_out, 6, lo, hi).wait()
        out_copy(block_out, 7, lo, hi).wait()

    out_norm(0, 128)
    put_norm_rows(4, 0, 1)
    tot = ar_wait(3)
    ar_start(4)
    for j in range(3):
        scale, ms = moments(tot[j : j + 1], tot[j + 3 : j + 4], count)
        ROWP[0:1, 128 + 128 * j : 256 + 128 * j] = scale
        ROWP[1:2, 128 + 128 * j : 256 + 128 * j] = ms
    out_norm(128, 512)
    put_norm_rows(5, 128, 3)
    tot = ar_wait(4)
    ar_start(5)

    def set_back(tot, lo, tiles, out_at):
        for j in range(tiles):
            ls = slice(lo + 128 * j, lo + 128 * j + 128)
            ROWP[4:5, ls] = tot[j : j + 1] / count
            ROWP[5:6, ls] = tot[tiles + j : tiles + j + 1] / count
            ROWP[6:7, ls] = ROWP[0:1, ls] * ROWP[2:3, ls]
            norm_out[out_at + j : out_at + j + 1, :] = tot[tiles + j : tiles + j + 1]
            norm_out[16 + out_at + j : 17 + out_at + j, :] = tot[j : j + 1]

    def norm_back(lo, hi):
        def one(h, c):
            for r in (0, 32):
                at = pl.ds(pl.multiple_of(h * SIDE + r, 32), 32)
                for l0 in range(lo, hi, 128):
                    ls = slice(l0, l0 + 128)
                    xh = PX[at, ls] * ROWP[0:1, ls] - ROWP[1:2, ls]
                    d = ROWP[6:7, ls] * (DY[at, ls] - ROWP[4:5, ls] - xh * ROWP[5:6, ls])
                    DC[h + 1, r : r + 32, ls] = d.astype(BF)
            return c

        lax.fori_loop(0, SIDE, one, 0)

    set_back(tot, 0, 1, 5)
    norm_back(0, 128)

    def make_d3(h, c):
        x = DC[h + 1, :, 0:128].astype(F32)
        D3[h + 1, :, 0:128] = shifted(x, 63, -1).astype(BF)
        D3[h + 1, :, 128:256] = DC[h + 1, :, 0:128]
        D3[h + 1, :, 256:384] = shifted(x, 0, 1).astype(BF)
        return c

    lax.fori_loop(0, SIDE, make_d3, 0)

    for r in range(0, 3456, 384):
        DY[r : r + 384, 0:128] = jnp.zeros((384, 128), F32)

    def wgrad_gl(i, c):
        zt = slab(F, i, 1, 384).T
        for a in range(3):
            res = dot(zt, slab(D3, i, 2 - a, 384))
            for b in range(3):
                r = 384 * (3 * a + b)
                DY[r : r + 384, 0:128] += res[:, 128 * b : 128 * b + 128]
        return c

    lax.fori_loop(0, 8, wgrad_gl, 0)
    tot = ar_wait(5)
    set_back(tot, 128, 3, 6)
    norm_back(128, 512)

    EXA[...] = jnp.zeros_like(EXA)
    GOUT[...] = jnp.zeros_like(GOUT)

    def join_back(h0, c):
        rows = pl.ds(pl.multiple_of(h0 * HALF, 8), HALF)
        dg = tile(DC, h0, 128, 512)
        dj = dot(WOUT[...], dg, 1, 1)
        PX[rows, 0:256] = dj
        GOUT[...] += dot(J[h0], dg)
        res = dot(dj.astype(BF), A[h0])
        PX[rows, 256:512] = res[:, 0:256]
        EXA[...] += res[:, 256:384]
        return c

    lax.fori_loop(0, 16, join_back, 0)

    def freq_back(g, c):
        z = dft16(grab(PX, g, 256), -1)
        for comp in range(2):
            rows = pl.ds(pl.multiple_of(comp * HALF + 8 * g, 8), 8)
            s0 = jnp.zeros((8, 128), F32)
            s1 = jnp.zeros((8, 128), F32)
            for k in range(16):
                xh, y = freq_act(PF[k, rows], rows)
                dy = gelu_slope(y) * (z[k][comp] * doubled)
                r0, l0 = dyf_pos(k)
                DY[pl.ds(pl.multiple_of(r0 + comp * HALF + 8 * g, 8), 8), l0 : l0 + 128] = dy
                s0 = s0 + dy
                s1 = s1 + dy * xh
            ACF[rows] = s0
            ACF[pl.ds(pl.multiple_of(384 + comp * HALF + 8 * g, 8), 8)] = s1
        return c

    lax.fori_loop(0, 24, freq_back, 0)
    ext_re, ext_im = split_ext(EXA[...])
    xh = PF[16] * COLF[0] - COLF[1]
    dy = gelu_slope(xh * COLF[2] + COLF[3]) * jnp.concatenate([ext_re, ext_im], axis=0)
    DYX[...] = dy
    ACF[0:384] += dy
    ACF[384:768] += dy * xh
    put_rows(6, 0, freq_rows())
    put_zero(6, 6)
    ar_start(6)

    for r in range(0, 1152, 384):
        DY[r : r + 384, 128:512] = jnp.zeros((384, 384), F32)
        DY[1152 + r : 1536 + r, 128:256] = jnp.zeros((384, 128), F32)

    def wgrad_loc(i, c):
        zt = slab(Z3, i, 1, 384).T
        for a in range(3):
            res = dot(zt, slab(DC, i, 2 - a, 512))
            DY[1152 + 384 * a : 1536 + 384 * a, 128:256] += res[:, 0:128]
            DY[384 * a : 384 * a + 384, 128:512] += res[:, 128:512]
        return c

    lax.fori_loop(0, 8, wgrad_loc, 0)

    class Scatter:
        def __init__(self, buf, scratch, q, base):
            self.buf, self.q, self.base = buf, q, base
            self.one, self.two, self.three, self.four = scratch
            self.slot = 2 * ring.core + ring.x

        def sem(self, i):
            return rs_sem.at[self.base + i]

        def rows(self, index, n):
            return pl.ds(pl.multiple_of(index * self.q, 16), n * self.q)

        def first(self):
            there = self.buf.at[:, self.rows(2 * (1 - ring.core), 2)]
            ring.send(there, self.one, self.sem(0), self.sem(1), ring.sibling())

        def second(self):
            await_bytes(self.one, self.sem(1))
            q = self.q

            def add(s, c):
                for half in range(2):
                    at = self.rows(2 * ring.core + half, 1)
                    mine = self.buf[s, at].astype(F32) + self.one[s, half * q : half * q + q].astype(F32)
                    self.buf[s, at] = mine.astype(BF)
                return c

            lax.fori_loop(0, D, add, 0)
            there = self.buf.at[:, self.rows(2 * ring.core + 1 - ring.x, 1)]
            ring.send(there, self.two, self.sem(2), self.sem(3), ring.across())

        def third(self):
            await_bytes(self.two, self.sem(3))
            at = self.rows(self.slot, 1)

            def add(s, c):
                mine = self.buf[s, at].astype(F32) + self.two[s].astype(F32)
                self.buf[s, at] = mine.astype(BF)
                return c

            lax.fori_loop(0, D, add, 0)

            def body(d, c):
                s = lax.rem(dp + d, D)
                ring.send(self.buf.at[s, at], self.three.at[dp], self.sem(4), self.sem(5), (s, rp))
                return c

            lax.fori_loop(1, D, body, 0)
            self.three[dp] = self.buf[dp, at]

        def fourth(self):
            await_bytes(self.three.at[pl.ds(0, D - 1)], self.sem(5))
            total = self.three[0].astype(F32)
            for s in range(1, D):
                total = total + self.three[s].astype(F32)
            self.four[self.slot] = total.astype(BF)
            for d in range(1, 4):
                ring.send(
                    self.four.at[self.slot], self.four.at[self.slot], self.sem(6), self.sem(7), (dp, lax.rem(rp + d, 4))
                )

        def last(self):
            await_bytes(self.four.at[pl.ds(0, 3)], self.sem(7))
            await_bytes(self.one, self.sem(0))
            await_bytes(self.two, self.sem(2))
            await_bytes(self.three.at[pl.ds(0, D - 1)], self.sem(4))
            await_bytes(self.four.at[pl.ds(0, 3)], self.sem(6))

    if fused:
        for s in range(D):
            for tap, c0, shard, r0, n in gl_runs():
                if shard == s:
                    r = 384 * tap + c0
                    WB[s, r0 : r0 + n] = DY[r : r + n, 0:128].astype(BF)
            WB[s, 432:576] = DY[1152 + 144 * s : 1296 + 144 * s, 128:256].astype(BF)
            for j in range(3):
                ls = slice(128 + 128 * j, 256 + 128 * j)
                WB[s, 576 + 144 * j : 720 + 144 * j] = DY[144 * s : 144 * s + 144, ls].astype(BF)
            WB[s, 1008:1024] = jnp.zeros((16, 128), BF)
        scatter_b = Scatter(WB, RB, q_b, 0)
        scatter_f = Scatter(WFO, RF, q_f, 8)
        scatter_i = Scatter(GI, RI, 32, 16)
        scatter_b.first()
    else:
        out_gl[...] = DY[0:3456, 0:128]
        out_ll[...] = DY[1152:2304, 128:256]
        out_lg[...] = DY[0:1152, 128:512]

    tot = ar_wait(6)
    for j in range(3):
        COLF[4, 128 * j : 128 * j + 128] = col(tot[j : j + 1] / fcount)
        COLF[5, 128 * j : 128 * j + 128] = col(tot[j + 3 : j + 4] / fcount)
        norm_out[2 + j : 3 + j, :] = tot[j + 3 : j + 4]
        norm_out[18 + j : 19 + j, :] = tot[j : j + 1]
    GFU[...] = jnp.zeros_like(GFU)

    def dpf_tile(k, dy):
        xh = PF[k] * COLF[0] - COLF[1]
        return (COLF[6] * (dy - COLF[4] - xh * COLF[5])).astype(BF)

    for t in range(8):
        spots = [dyf_pos(2 * t), dyf_pos(2 * t + 1)]
        parts = [dpf_tile(2 * t + e, DY[r : r + 384, l : l + 128]) for e, (r, l) in enumerate(spots)]
        dpf = jnp.concatenate(parts, axis=1)
        GFU[...] += dot(jnp.concatenate([ST[2 * t], ST[2 * t + 1]], axis=1), dpf, 1, 1)
        ds = dot(WFU[...], dpf)
        for e, (r, l) in enumerate(spots):
            DY[r : r + 384, l : l + 128] = ds[:, 128 * e : 128 * e + 128]
    dpf = dpf_tile(16, DYX[...])
    GFU[...] += dot(ST[16], dpf, 1, 1)
    ds = dot(WFU[...], dpf)
    EXB[...] = join_ext(ds[0:HALF], ds[HALF : 2 * HALF]).astype(BF)
    if fused:
        scatter_b.second()

    def adj_fft(i, c):
        halves = []
        for s in range(2):
            z = []
            for k in range(16):
                r0, l0 = dyf_pos(k)
                z.append(
                    tuple(
                        DY[pl.ds(pl.multiple_of(r0 + comp * HALF + 16 * i + 8 * s, 8), 8), l0 : l0 + 128]
                        for comp in range(2)
                    )
                )
            halves.append(dft16(z, 1))
        for a in range(16):
            for comp in range(2):
                both = jnp.concatenate([halves[0][a][comp], halves[1][a][comp]], axis=0)
                Y[a, pl.ds(pl.multiple_of(i * 16, 16), 16), 128 * comp : 128 * comp + 128] = both.astype(BF)
        return c

    lax.fori_loop(0, 12, adj_fft, 0)
    ACC[...] = jnp.zeros_like(ACC)

    def spec_back(h0, c):
        rows = pl.ds(pl.multiple_of(h0 * HALF, 8), HALF)
        back = dot(jnp.concatenate([Y[h0], EXB[...]], axis=1), A[h0], 1, 1)
        xh = PS[h0] * two(COLS[0]) - two(COLS[1])
        dy = gelu_slope(xh * two(COLS[2]) + two(COLS[3])) * (PX[rows, 0:256] + back)
        DY[rows, 256:512] = dy
        ACC[0:HALF] += lane_pair(dy)
        ACC[HALF : 2 * HALF] += lane_pair(dy * xh)
        return c

    lax.fori_loop(0, 16, spec_back, 0)
    put_rows(7, 0, spec_rows())
    put_zero(7, 4)
    ar_start(7)
    if fused:
        for s in range(D):
            for j in range(3):
                ls = slice(128 * j, 128 * j + 128)
                WFO[s, 48 * j : 48 * j + 48] = GFU[48 * s : 48 * s + 48, ls].astype(BF)
                part = jnp.concatenate([GOUT[24 * s : 24 * s + 24, ls], jnp.zeros((8, 128), F32)], axis=0)
                WFO[s, 144 + 32 * j : 176 + 32 * j] = part.astype(BF)
            WFO[s, 240:256] = jnp.zeros((16, 128), BF)
        scatter_f.first()
        scatter_b.third()
    else:
        out_fu[...] = GFU[...]
        out_out[...] = GOUT[...]

    def dgrad(i, c):
        rows = pl.ds(pl.multiple_of(512 * i, 512), 512)
        lhs = jnp.concatenate([slab(DC, i, 2 - a, 512) for a in range(3)], axis=1)
        rhs = jnp.concatenate([WCAT[384 * a : 384 * a + 384] for a in range(3)], axis=1)
        res = dot(lhs, rhs, 1, 1)
        PX[rows, 0:128] = res[:, 128:256] + shifted(res[:, 0:128], 63, -1) + shifted(res[:, 256:384], 0, 1)
        lhs = jnp.concatenate([slab(D3, i, 2 - a, 384) for a in range(3)], axis=1)
        rhs = jnp.concatenate([WGL[a] for a in range(3)], axis=1)
        PX[rows, 128:512] = dot(lhs, rhs, 1, 1)
        return c

    lax.fori_loop(0, 8, dgrad, 0)
    if fused:
        scatter_b.fourth()
        scatter_f.second()

    tot = ar_wait(7)
    for r, (lo, n) in enumerate(((0, 128), (128, 64))):
        COLS[4, lo : lo + n] = col(tot[r : r + 1] / count)[0:n]
        COLS[5, lo : lo + n] = col(tot[r + 2 : r + 3] / count)[0:n]
        norm_out[r : r + 1, :] = tot[r + 2 : r + 3]
        norm_out[16 + r : 17 + r, :] = tot[r : r + 1]
    norm_out[9:16, :] = jnp.zeros((7, 128), F32)
    norm_out[25:32, :] = jnp.zeros((7, 128), F32)
    GIN[...] = jnp.zeros_like(GIN)

    def spec_grad(h0, c):
        rows = pl.ds(pl.multiple_of(h0 * HALF, 8), HALF)
        xh = PS[h0] * two(COLS[0]) - two(COLS[1])
        d = two(COLS[6]) * (DY[rows, 256:512] - two(COLS[4]) - xh * two(COLS[5]))
        d = d.astype(BF)
        J[h0] = d
        GIN[...] += dot(d, tile(F, h0, 0, GLO))
        return c

    lax.fori_loop(0, 16, spec_grad, 0)
    if fused:
        gin = jnp.concatenate([GIN[...], jnp.zeros((64, 384), F32)], axis=0).T
        for s in range(D):
            GI[s, 0:48] = gin[48 * s : 48 * s + 48, 0:128].astype(BF)
            GI[s, 48:96] = gin[48 * s : 48 * s + 48, 128:256].astype(BF)
            GI[s, 96:128] = jnp.zeros((32, 128), BF)
        scatter_i.first()
        scatter_f.third()
    else:
        out_in[...] = GIN[...]

    def spec_field(h0, c):
        dg = dot(J[h0], WINT[...], 0, 0)
        for j in range(4):
            at = pl.ds(pl.multiple_of((h0 + 16 * j) * SIDE, SIDE), SIDE)
            PX[at, 128:512] += dg[64 * j : 64 * j + 64]
        return c

    lax.fori_loop(0, 16, spec_field, 0)
    if fused:
        scatter_i.second()

    cot_copy(0, 0, ALL).start()

    def finish(i, c):
        slot = lax.rem(i, 2)
        cot_copy(i, 0, ALL).wait()

        @pl.when(i < 7)
        def _():
            cot_copy(i + 1, 0, ALL).start()

        @pl.when(i > 1)
        def _():
            out_copy(input_grad, i - 2, 0, ALL).wait()

        def one(hh, c2):
            h = 8 * i + hh
            for r in (0, 32):
                at = pl.ds(pl.multiple_of(h * SIDE + r, 32), 32)
                wf = WF[h, r : r + 32].astype(F32)
                for l0 in range(0, 512, 128):
                    ls = slice(l0, l0 + 128)
                    g = PX[at, ls] + COTB[slot, hh, r : r + 32, ls].astype(F32) * wf
                    OUTB[slot, hh, r : r + 32, ls] = g.astype(BF)
            return c2

        lax.fori_loop(0, 8, one, 0)
        out_copy(input_grad, i, 0, ALL).start()
        return c

    lax.fori_loop(0, 8, finish, 0)
    if fused:
        scatter_i.third()
        scatter_f.fourth()
        scatter_i.fourth()
        scatter_b.last()
        scatter_f.last()
        scatter_i.last()
        for at, q, four in ((0, q_b, RB[3]), (1024, q_f, RF[3]), (1280, 32, RI[3])):
            for r in range(4):
                flat_out[at + r * q : at + r * q + q, :] = four[r].astype(F32)
        await_bytes(WI.at[pl.ds(0, D - 1)], g_sem.at[0])
        await_bytes(GBB.at[pl.ds(0, D - 1)], g_sem.at[2])
    out_copy(input_grad, 6, 0, ALL).wait()
    out_copy(input_grad, 7, 0, ALL).wait()


def run_block(features, cotangent, holes, weights, gains, biases, fused):
    dps, reps = lax.axis_size("dp"), lax.axis_size("rep")
    N = dps * reps
    any_spec = pl.BlockSpec(memory_space=pl.ANY)
    vmem = pl.BlockSpec(memory_space=pltpu.VMEM)
    table = jnp.asarray(dft_table())
    args = [features, cotangent, holes, table] + list(weights) + list(gains)
    if fused:
        args = args + list(biases)
    out_shape = [
        jax.ShapeDtypeStruct((SIDE, SIDE, ALL), BF),
        jax.ShapeDtypeStruct((SIDE, SIDE, ALL), BF),
        jax.ShapeDtypeStruct((32, 128), F32),
    ]
    if fused:
        out_shape.append(jax.ShapeDtypeStruct((1408, 128), F32))
    else:
        for shape in ((1152, 128), (3456, 128), (1152, 384), (192, 384), (384, 384), (192, 384)):
            out_shape.append(jax.ShapeDtypeStruct(shape, F32))
    V = pltpu.VMEM
    dma = pltpu.SemaphoreType.DMA
    scratch = [
        V((66, SIDE, 384), BF),
        V((SIDE, SIDE, 128), BF),
        V((66, SIDE, 384), BF),
        V((66, SIDE, 384), BF),
        V((POS, ALL), F32),
        V((POS, ALL), F32),
        V((16, HALF, 256), F32),
        V((17, 384, 128), BF),
        V((17, 384, 128), F32),
        V((16, HALF, 256), BF),
        V((16, HALF, 256), BF),
        V((66, SIDE, ALL), BF),
        V((16, 256, 384), BF),
        V((HALF, 128), F32),
        V((HALF, 128), BF),
        V((384, 128), F32),
        V((384, 128), F32),
        V((768, 128), F32),
        V((7, HALF, 128), F32),
        V((7, 384, 128), F32),
        V((24, ALL), F32),
        V((384, 384), F32),
        V((HALF, 384), F32),
        V((HALF, 384), F32),
        V((2, N, 8, 128), F32),
        dma((8,)),
        dma((8,)),
        V((2, 8, SIDE, ALL), BF),
        V((2, 8, SIDE, ALL), BF),
        dma((2,)),
        dma((2,)),
        dma((3,)),
        V((3, 384, 384), BF),
    ]
    if fused:
        scratch += [
            V((1152, ALL), BF),
            V((HALF, 384), BF),
            V((384, 384), BF),
            V((384, 384), BF),
            V((HALF, 384), BF),
            V((dps, 96, 128), BF),
            V((dps, 24, 128), F32),
            V((dps, 256, 128), BF),
            V((dps, 1024, 128), BF),
            V((96, 128), BF),
            V((256, 128), BF),
            V((1024, 128), BF),
            dma((20,)),
        ]
        for q in (256, 64, 32):
            scratch += [V((dps, 2 * q, 128), BF), V((dps, q, 128), BF), V((dps, q, 128), BF), V((4, q, 128), BF)]
        scratch += [V((dps, 128, 128), BF), dma((24,))]
    return pl.pallas_call(
        functools.partial(kernel, dps, reps, fused),
        out_shape=out_shape,
        in_specs=[any_spec, any_spec, vmem, any_spec] + [vmem] * (len(args) - 4),
        out_specs=[any_spec, any_spec] + [vmem] * (len(out_shape) - 2),
        scratch_shapes=scratch,
        compiler_params=pltpu.CompilerParams(
            collective_id=0, has_side_effects=True, vmem_limit_bytes=64 * 1024 * 1024 - 65536
        ),
        cost_estimate=pl.CostEstimate(flops=40_000_000_000, bytes_accessed=30_000_000, transcendentals=10_000_000),
    )(*args)


def on_device(features, cotangent, holes, w_ll, w_gl, w_lg, w_in, w_fu, w_out, gains, biases):
    dps, reps = lax.axis_size("dp"), lax.axis_size("rep")
    share = gains.shape[1]
    first = lax.axis_index("dp") * share
    shards = (w_ll, w_gl, w_lg, w_in, w_fu, w_out)
    rows = [w.shape[1] for w in shards]
    fused = dps == 8 and reps == 4
    if fused:
        weights = [w[0] for w in shards]
        block_out, input_grad, norms, flat = run_block(
            features[0], cotangent[0], holes[0], weights, [gains], [biases], True
        )
        cut = lambda at, n: flat[at : at + n]
        grads = [
            cut(432, 144),
            cut(0, 432),
            jnp.concatenate([cut(576 + 144 * j, 144) for j in range(3)], axis=1),
            jnp.concatenate([cut(1280, 48), cut(1328, 48)[:, 0:64]], axis=1),
            jnp.concatenate([cut(1024 + 48 * j, 48) for j in range(3)], axis=1),
            jnp.concatenate([cut(1168 + 32 * j, 24) for j in range(3)], axis=1),
        ]
        grads = [g[None] for g in grads]
    else:
        full = [lax.all_gather(w, "dp", axis=1, tiled=True)[0] for w in shards]
        table = jnp.concatenate([gains, biases], axis=0).astype(F32)
        table = lax.all_gather(table, "dp", axis=1, tiled=True)
        table = jnp.pad(table, ((0, 0), (0, 1152 - table.shape[1]))).reshape(18, 128)
        table = jnp.pad(table, ((0, 6), (0, 0)))
        weights = [jnp.concatenate([full[0], full[2]], axis=1), full[1], full[3].T, full[4], full[4].T, full[5]]
        block_out, input_grad, norms, g_ll, g_gl, g_lg, g_in, g_fu, g_out = run_block(
            features[0], cotangent[0], holes[0], weights, [table], None, False
        )
        grads = []
        for g in (g_ll, g_gl, g_lg, g_in.T, g_fu, g_out):
            g = lax.psum(g[None], "rep")
            grads.append(lax.psum_scatter(g, "dp", scatter_dimension=1, tiled=True))
    norm_rows = []
    for at in (0, 16):
        part = norms[at : at + 9].reshape(1, 1152)
        part = jnp.concatenate([part[:, 0:192], part[:, 256:1152]], axis=1)
        norm_rows.append(lax.dynamic_slice_in_dim(part, first, share, 1))
    return (block_out[None], input_grad[None], *grads, *norm_rows)


def solution(mesh):
    whole = P(("dp", "rep"), None, None, None)
    rows = P(None, "dp", None)
    in_specs = (whole, whole, P(("dp", "rep"), None, None)) + (rows,) * 6 + (P(None, "dp"),) * 2
    out_specs = (whole, whole) + (rows,) * 6 + (P(None, "dp"),) * 2
    return jax.shard_map(on_device, mesh=mesh, in_specs=in_specs, out_specs=out_specs, check_vma=False)
```

```python
import functools
import math

import jax
import jax.numpy as jnp
import ml_dtypes
import numpy as np
from jax import lax
from jax.experimental import pallas as pl
from jax.experimental.pallas import tpu as pltpu
from jax.sharding import PartitionSpec as P

EPS = 1e-05
K0 = math.sqrt(2.0 / math.pi)
K1 = 0.044715
MESH = pl.DeviceIdType.MESH
F32 = jnp.float32
BF = jnp.bfloat16
SIDE = 64
LOC = 128
GLO = 384
HALF = 192
ALL = LOC + GLO
WIDTHS = (HALF, GLO, LOC, GLO)
POS = SIDE * SIDE
FREQ = SIDE * (SIDE // 2 + 1)


def dft_table():
    a = np.arange(16)[:, None, None, None, None]
    j = np.arange(4)[None, :, None, None, None]
    w = np.arange(64)[None, None, :, None, None]
    k1 = np.arange(4)[None, None, None, :, None]
    l = np.arange(32)[None, None, None, None, :]
    angle = 2 * np.pi / 64 * (((a + 16 * j) * k1 + w * l) % 64)
    main_re = np.cos(angle).reshape(16, 256, 128) / 64
    main_im = -np.sin(angle).reshape(16, 256, 128) / 64
    k = np.arange(64)[None, None, None, :]
    a, j, w = a[..., 0], j[..., 0], w[..., 0]
    angle = 2 * np.pi / 64 * (((a + 16 * j) * k + 32 * w) % 64)
    ext_re = np.cos(angle).reshape(16, 256, 64) / 64
    ext_im = -np.sin(angle).reshape(16, 256, 64) / 64
    return np.concatenate([main_re, main_im, ext_re, ext_im], axis=-1).astype(ml_dtypes.bfloat16)


def dot(a, b, ca=1, cb=0):
    return lax.dot_general(a, b, (((ca,), (cb,)), ((), ())), preferred_element_type=F32)


def gate(y):
    y2 = y * y
    return y2, 0.5 + 0.5 * jnp.tanh(y * (K0 + K0 * K1 * y2))


def gelu_value(y):
    return y * gate(y)[1]


def gelu_both(y):
    y2, s = gate(y)
    value = y * s
    return value, s + value * (1.0 - s) * (2.0 * K0 + 6.0 * K0 * K1 * y2)


def gelu_slope(y):
    return gelu_both(y)[1]


def cmul(z, c, s):
    return (z[0] * c - z[1] * s, z[0] * s + z[1] * c)


def dft4(z, sign):
    (ar, ai), (br, bi), (cr, ci), (dr, di) = z
    pr, pi, qr, qi = ar + cr, ai + ci, ar - cr, ai - ci
    rr, ri, sr, si = br + dr, bi + di, br - dr, bi - di
    tr, ti = (si, -sr) if sign < 0 else (-si, sr)
    return [(pr + rr, pi + ri), (qr + tr, qi + ti), (pr - rr, pi - ri), (qr - tr, qi - ti)]


def dft16(z, sign):
    cols = []
    for n2 in range(4):
        part = dft4([z[4 * n1 + n2] for n1 in range(4)], sign)
        for k1 in range(1, 4):
            e = n2 * k1
            if e == 0:
                continue
            if e == 4:
                re, im = part[k1]
                part[k1] = (im, -re) if sign < 0 else (-im, re)
            else:
                ang = sign * 2 * math.pi * e / 16
                part[k1] = cmul(part[k1], math.cos(ang), math.sin(ang))
        cols.append(part)
    out = [None] * 16
    for k1 in range(4):
        part = dft4([cols[n2][k1] for n2 in range(4)], sign)
        for k2 in range(4):
            out[k1 + 4 * k2] = part[k2]
    return out


def dyf_pos(t):
    if t < 12:
        return 2304 + 384 * (t // 3), 128 + 128 * (t % 3)
    u = t - 12
    return 1152 + 384 * (u // 2), 256 + 128 * (u % 2)


def rows8(x):
    acc = x[0:8]
    for r in range(8, x.shape[0], 8):
        acc = acc + x[r : r + 8]
    return acc


def lane_pair(x):
    return x[:, 0:128] + x[:, 128:256]


def await_bytes(ref, sem):
    pltpu.make_async_copy(ref, ref, sem).wait()


class Ring:
    def __init__(self, dps, reps):
        self.D, self.R = dps, reps
        self.N = dps * reps
        self.dp = lax.axis_index("dp")
        self.rp = lax.axis_index("rep")
        self.me = self.dp * reps + self.rp
        self.core = lax.rem(self.rp, 2)
        self.x = lax.div(self.rp, 2)
        self.y = lax.rem(self.dp, 2)
        self.z = lax.div(self.dp, 2)

    def dev(self, i):
        return (lax.div(i, self.R), lax.rem(i, self.R))

    def barrier(self):
        sem = pltpu.get_barrier_semaphore()

        def body(d, c):
            peer = lax.rem(self.me + d, self.N)
            pl.semaphore_signal(sem, inc=1, device_id=self.dev(peer), device_id_type=MESH)
            return c

        lax.fori_loop(1, self.N, body, 0)
        pl.semaphore_wait(sem, self.N - 1)

    def send(self, src, dst, ss, rs, device):
        pltpu.make_async_remote_copy(
            src_ref=src, dst_ref=dst, send_sem=ss, recv_sem=rs, device_id=device, device_id_type=MESH
        ).start()

    def sibling(self):
        return (self.dp, self.rp + 1 - 2 * self.core)

    def across(self):
        return (self.dp, lax.rem(self.rp + 2, 4))

    def beside(self):
        return (self.dp + 1 - 2 * self.y, self.rp)


class Gather:
    def __init__(self, ring, own, buf, sems, base):
        self.ring, self.own, self.buf, self.sems, self.base = ring, own, buf, sems, base
        self.q = own.shape[0] // 4

    def sem(self, i):
        return self.sems.at[self.base + i]

    def rows(self, i):
        return pl.ds(pl.multiple_of(i * self.q, 16), self.q)

    def place(self):
        rows = self.rows(self.ring.rp)
        self.buf[self.ring.z, self.ring.y, rows] = self.own[rows]

    def along_z(self):
        g = self.ring
        rows = self.rows(g.rp)
        for d in range(1, 4):
            there = (2 * lax.rem(g.z + d, 4) + g.y, g.rp)
            g.send(self.own.at[rows], self.buf.at[g.z, g.y, rows], self.sem(0), self.sem(1), there)

    def along_y(self):
        g = self.ring
        await_bytes(self.buf.at[pl.ds(0, 3), 0, pl.ds(0, self.q)], self.sem(1))
        part = self.buf.at[:, g.y, self.rows(g.rp)]
        g.send(part, part, self.sem(2), self.sem(3), g.beside())

    def along_x(self):
        g = self.ring
        await_bytes(self.buf.at[:, 0, pl.ds(0, self.q)], self.sem(3))
        part = self.buf.at[:, :, self.rows(g.rp)]
        g.send(part, part, self.sem(4), self.sem(5), g.across())
        g.send(part, part, self.sem(6), self.sem(7), g.sibling())

    def between(self):
        g = self.ring
        await_bytes(self.buf.at[:, :, pl.ds(0, self.q)], self.sem(5))
        part = self.buf.at[:, :, self.rows(lax.rem(g.rp + 2, 4))]
        g.send(part, part, self.sem(8), self.sem(9), g.sibling())

    def last(self):
        one = self.buf.at[:, :, pl.ds(0, self.q)]
        for i in (7, 9, 4, 6, 8):
            await_bytes(one, self.sem(i))
        await_bytes(self.buf.at[pl.ds(0, 3), 0, pl.ds(0, self.q)], self.sem(0))
        await_bytes(self.buf.at[:, 0, pl.ds(0, self.q)], self.sem(2))


class Scatter:
    def __init__(self, ring, buf, scratch, sems, base):
        self.ring, self.buf, self.sems, self.base = ring, buf, sems, base
        self.one, self.two, self.three, self.four, self.done = scratch
        self.q = buf.shape[2] // 4
        self.slot = 2 * ring.core + ring.x

    def sem(self, i):
        return self.sems.at[self.base + i]

    def rows(self, index, n):
        return pl.ds(pl.multiple_of(index * self.q, 16), n * self.q)

    def between(self):
        g = self.ring
        there = self.buf.at[:, :, self.rows(2 * (1 - g.core), 2)]
        g.send(there, self.one, self.sem(0), self.sem(1), g.sibling())

    def add(self, zi, yi, at, other):
        self.buf[zi, yi, at] = (self.buf[zi, yi, at].astype(F32) + other.astype(F32)).astype(BF)

    def along_x(self):
        g = self.ring
        await_bytes(self.one, self.sem(1))

        def body(s, c):
            zi, yi = lax.div(s, 2), lax.rem(s, 2)
            self.add(zi, yi, self.rows(2 * g.core, 2), self.one[zi, yi])
            return c

        lax.fori_loop(0, 8, body, 0)
        there = self.buf.at[:, :, self.rows(2 * g.core + 1 - g.x, 1)]
        g.send(there, self.two, self.sem(2), self.sem(3), g.across())

    def along_y(self):
        g = self.ring
        await_bytes(self.two, self.sem(3))
        at = self.rows(self.slot, 1)

        def body(s, c):
            zi, yi = lax.div(s, 2), lax.rem(s, 2)
            self.add(zi, yi, at, self.two[zi, yi])
            return c

        lax.fori_loop(0, 8, body, 0)
        g.send(self.buf.at[:, 1 - g.y, at], self.three, self.sem(4), self.sem(5), g.beside())

    def along_z(self):
        g = self.ring
        await_bytes(self.three, self.sem(5))
        at = self.rows(self.slot, 1)
        for k in range(4):
            self.add(k, g.y, at, self.three[k])
        for d in range(1, 4):
            zz = lax.rem(g.z + d, 4)
            g.send(self.buf.at[zz, g.y, at], self.four.at[g.z], self.sem(6), self.sem(7), (2 * zz + g.y, g.rp))
        self.four[g.z] = self.buf[g.z, g.y, at]

    def to_copies(self):
        g = self.ring
        await_bytes(self.four.at[pl.ds(0, 3)], self.sem(7))
        total = self.four[0].astype(F32)
        for k in range(1, 4):
            total = total + self.four[k].astype(F32)
        self.done[self.slot] = total.astype(BF)
        mine = self.done.at[self.slot]
        for d in range(1, 4):
            g.send(mine, mine, self.sem(8), self.sem(9), (g.dp, lax.rem(g.rp + d, 4)))

    def last(self):
        three = self.done.at[pl.ds(0, 3)]
        await_bytes(three, self.sem(9))
        await_bytes(self.one, self.sem(0))
        await_bytes(self.two, self.sem(2))
        await_bytes(self.three, self.sem(4))
        await_bytes(self.four.at[pl.ds(0, 3)], self.sem(6))
        await_bytes(three, self.sem(8))


AR_ROWS = (4, 6, 2, 6, 2, 6, 6, 4)
CHUNKS = (448, 576, 256, 128)
STARTS = (0, 448, 1024, 1280)


def mask_tile(row):
    at0 = lax.broadcasted_iota(jnp.int32, (SIDE, SIDE), 0)
    at1 = lax.broadcasted_iota(jnp.int32, (SIDE, SIDE), 1)
    diag = jnp.where(at0 == at1, jnp.broadcast_to(row, (SIDE, SIDE)), 0.0)
    return dot(diag.astype(BF), jnp.ones((SIDE, 128), BF))


def shifted(x, edge, by):
    moved = pltpu.roll(x, by % x.shape[0], axis=0)
    at = lax.rem(lax.broadcasted_iota(jnp.int32, x.shape, 0), SIDE)
    return jnp.where(at == edge, 0.0, moved)


def gl_runs(shards):
    runs = []
    share = 9 * GLO // shards
    row = 0
    while row < 9 * GLO:
        n = min(GLO - row % GLO, share - row % share)
        runs.append((row // GLO, row % GLO, row // share, row % share, n))
        row += n
    return runs


def col(row):
    return jnp.broadcast_to(row, (128, 128)).T


def two(x):
    return jnp.concatenate([x, x], axis=1)


def to_row(x):
    n = x.shape[0]
    if n < 128:
        x = jnp.concatenate([x, jnp.zeros((128 - n, 128), F32)], axis=0)
    return jnp.sum(x.T, axis=0, keepdims=True)


def moments(total, square, n):
    mean = total / n
    scale = lax.rsqrt(square / n - mean * mean + EPS)
    return scale, mean * scale


def kernel(dps, reps, fused, *refs):
    it = iter(refs)

    def take(n):
        return [next(it) for _ in range(n)]

    feat_h, cot_h, holes, tab_h = take(4)
    if fused:
        w_ll, w_gl, w_lg, w_in, w_fu, w_out, gain_in, bias_in = take(8)
    else:
        WCAT, WGLN, WINT, WFU, WFUT, WOUT, GBI = take(7)
    block_out, field_out, norm_out = take(3)
    if fused:
        (flat_out,) = take(1)
    else:
        out_ll, out_gl, out_lg, out_in, out_fu, out_out = take(6)
    F, WF, Z3, D3, PX, DY, PS, ST, PF, Y, J, DC, A, COT = take(14)
    EXA, EXB, DYX, ACC, ACF, COLS, COLF, ROWP, GBR, GOUT, WGL = take(11)
    ARB = take(8)
    ar_s, ar_r, io_sem = take(3)
    if fused:
        WCAT, WINT, WFU, WFUT, WOUT, WI, GBB, OWNI, g_sem, rs_sem = take(10)
        OWN, WB, RS = take(3), take(4), [take(5) for _ in range(4)]
    ring = Ring(dps, reps)
    D, R, N = ring.D, ring.R, ring.N
    me, dp, rp = ring.me, ring.dp, ring.rp
    count = float(POS * N)
    fcount = float(FREQ * N)

    copy_l = pltpu.make_async_copy(feat_h.at[:, :, 0:LOC], Z3.at[1:65, :, 128:256], io_sem.at[0])
    copy_l.start()
    copy_f = pltpu.make_async_copy(feat_h.at[:, :, LOC:ALL], F.at[1:65], io_sem.at[1])
    copy_f.start()
    copy_a = pltpu.make_async_copy(tab_h, A, io_sem.at[2])
    copy_a.start()
    copy_c = pltpu.make_async_copy(cot_h, COT, io_sem.at[3])
    copy_c.start()

    def put(src, dst):
        copy = pltpu.make_async_copy(src, dst, io_sem.at[7])
        copy.start()
        copy.wait()

    def ar_start(k):
        def body(d, c):
            peer = lax.rem(me + d, N)
            ring.send(ARB[k].at[me], ARB[k].at[me], ar_s.at[k], ar_r.at[k], ring.dev(peer))
            return c

        lax.fori_loop(1, N, body, 0)

    def ar_wait(k):
        await_bytes(ARB[k].at[pl.ds(0, N - 1)], ar_r.at[k])
        await_bytes(ARB[k].at[pl.ds(0, N - 1)], ar_s.at[k])
        return jnp.sum(ARB[k][...], axis=0)

    def put_rows(k, at, rows):
        for i, row in enumerate(rows):
            ARB[k][me, at + i : at + i + 1, :] = row

    if fused:
        O1, O2, OF = OWN
        OWNI[0:48, :] = w_in[:, 0:128]
        OWNI[48:96, :] = jnp.concatenate([w_in[:, 128:192], jnp.zeros((48, 64), BF)], axis=1)
        own = gain_in.shape[1]
        for kind, ref in ((0, gain_in), (1, bias_in)):
            row = jnp.concatenate([ref[...].astype(F32), jnp.zeros((1, 256 - own), F32)], axis=1)
            for j in range(2):
                GBB[dp, 2 * kind + j : 2 * kind + j + 1, :] = row[:, 128 * j : 128 * j + 128]
        WI[dp] = OWNI[...]
        for j in range(3):
            OF[48 * j : 48 * j + 48, :] = w_fu[:, 128 * j : 128 * j + 128]
            part = w_out[:, 128 * j : 128 * j + 128].astype(F32)
            part = jnp.concatenate([part, jnp.zeros((8, 128), F32)], axis=0)
            OF[144 + 32 * j : 176 + 32 * j, :] = part.astype(BF)
            O2[144 + 144 * j : 288 + 144 * j, :] = w_lg[:, 128 * j : 128 * j + 128]
        OF[240:256, :] = jnp.zeros((16, 128), BF)
        O2[0:144, :] = w_ll[...]
        O1[0:432, :] = w_gl[...]
        O1[432:448, :] = jnp.zeros((16, 128), BF)
        W1, W2, WFO, GI = WB
        gather_1 = Gather(ring, O1, W1, g_sem, 4)
        gather_2 = Gather(ring, O2, W2, g_sem, 14)
        gather_f = Gather(ring, OF, WFO, g_sem, 24)
        for g in (gather_f, gather_2, gather_1):
            g.place()

    ring.barrier()

    def spread(src, dst, ss, rs):
        def body(d, c):
            ring.send(src, dst, ss, rs, (lax.rem(dp + d, D), rp))
            return c

        lax.fori_loop(1, D, body, 0)

    if fused:
        spread(OWNI, WI.at[dp], g_sem.at[0], g_sem.at[1])
        gather_f.along_z()
        spread(GBB.at[dp], GBB.at[dp], g_sem.at[2], g_sem.at[3])
        gather_2.along_z()
        gather_1.along_z()

    edge_row = jnp.zeros((SIDE, 384), BF)
    for ref in (F, Z3, D3):
        ref[0] = edge_row
        ref[65] = edge_row
    DC[0] = jnp.zeros((SIDE, ALL), BF)
    DC[65] = jnp.zeros((SIDE, ALL), BF)

    def make_wf(i, c):
        for e in range(4):
            WF[4 * i + e] = mask_tile(0.25 + holes[pl.ds(4 * i + e, 1), :].astype(F32)).astype(BF)
        return c

    lax.fori_loop(0, 16, make_wf, 0)
    copy_l.wait()

    def make_z3(i, c):
        for e in range(2):
            h = 2 * i + e + 1
            x = Z3[h, :, 128:256].astype(F32)
            Z3[h, :, 0:128] = shifted(x, 0, 1).astype(BF)
            Z3[h, :, 256:384] = shifted(x, 63, -1).astype(BF)
        return c

    lax.fori_loop(0, 32, make_z3, 0)
    copy_f.wait()

    if fused:
        await_bytes(WI.at[pl.ds(0, D - 1)], g_sem.at[1])
        first = jnp.concatenate([WI[s, 0:48] for s in range(D)], axis=0).astype(F32)
        WINT[0:128, :] = first.T.astype(BF)
        first = jnp.concatenate([WI[s, 48:96] for s in range(D)], axis=0).astype(F32)
        WINT[128:192, :] = (first.T)[0:64].astype(BF)

    def tile(ref, h0, lo, hi):
        return jnp.concatenate([ref[h0 + 16 * j + 1, :, lo:hi] for j in range(4)], axis=0)

    def rows_of(h0):
        return pl.ds(pl.multiple_of(h0 * HALF, 8), HALF)

    ACC[...] = jnp.zeros_like(ACC)

    def input_proj(i, c):
        w = WINT[...]
        res = [dot(w, tile(F, 4 * i + e, 0, GLO), 1, 1) for e in range(4)]
        for e in range(4):
            PS[4 * i + e] = res[e]
        ACC[0:HALF] += sum(lane_pair(ps) for ps in res)
        ACC[HALF : 2 * HALF] += sum(lane_pair(ps * ps) for ps in res)
        return c

    lax.fori_loop(0, 4, input_proj, 0)

    def spec_rows():
        return [to_row(ACC[0:128]), to_row(ACC[128:192]), to_row(ACC[192:320]), to_row(ACC[320:384])]

    put_rows(0, 0, spec_rows())
    ar_start(0)

    if fused:
        gather_f.along_y()
        await_bytes(GBB.at[pl.ds(0, D - 1)], g_sem.at[3])
        wide = []
        for kind in range(2):
            parts = []
            for s in range(D):
                parts.append(GBB[s, 2 * kind : 2 * kind + 1, :])
                parts.append(GBB[s, 2 * kind + 1 : 2 * kind + 2, 0 : own - 128])
            row = jnp.concatenate(parts + [jnp.ones((1, 1152 - own * D), F32)], axis=1)
            wide.append(jnp.broadcast_to(row, (8, 1152)))
    else:
        wide = []
        for kind in range(2):
            row = jnp.concatenate([GBI[9 * kind + j : 9 * kind + j + 1, :] for j in range(9)], axis=1)
            wide.append(jnp.broadcast_to(row, (8, 1152)))

    def piece(kind, offset, width):
        return pltpu.roll(wide[kind], (1152 - offset) % 1152, axis=1)[0:1, 0:width]

    for kind in range(2):
        at = 2 + kind
        spec = piece(kind, 0, 256)
        freq = piece(kind, HALF, 384)
        glo = piece(kind, HALF + GLO + LOC, 384)
        COLS[at, 0:128] = col(spec[:, 0:128])
        COLS[at, 128:192] = col(spec[:, 128:256])[0:64]
        for j in range(2):
            GBR[kind, j : j + 1, :] = spec[:, 128 * j : 128 * j + 128]
        for j in range(3):
            COLF[at, 128 * j : 128 * j + 128] = col(freq[:, 128 * j : 128 * j + 128])
            GBR[kind, 2 + j : 3 + j, :] = freq[:, 128 * j : 128 * j + 128]
            GBR[kind, 6 + j : 7 + j, :] = glo[:, 128 * j : 128 * j + 128]
        loc = piece(kind, HALF + GLO, 128)
        GBR[kind, 5:6, :] = loc
        ROWP[at : at + 1, 0:128] = loc
        ROWP[at : at + 1, 128:512] = glo

    def fold(ref):
        ref[4] = ref[0] * ref[2]
        ref[5] = ref[3] - ref[1] * ref[2]

    if fused:
        gather_2.along_y()
        gather_f.along_x()
        gather_1.along_y()

    copy_a.wait()
    tot = ar_wait(0)
    for r, (lo, n) in enumerate(((0, 128), (128, 64))):
        scale, ms = moments(tot[r : r + 1], tot[r + 2 : r + 3], count)
        COLS[0, lo : lo + n] = col(scale)[0:n]
        COLS[1, lo : lo + n] = col(ms)[0:n]
    fold(COLS)

    EXA[...] = jnp.zeros_like(EXA)

    def spec_front(i, c):
        gain, bias = two(COLS[4]), two(COLS[5])
        ext = None
        for e in range(4):
            h0 = 4 * i + e
            sp = gelu_value(PS[h0] * gain + bias)
            DY[rows_of(h0), 0:256] = sp
            res = dot(sp.astype(BF), A[h0])
            DY[rows_of(h0), 256:512] = res[:, 0:256]
            ext = res[:, 256:384] if ext is None else ext + res[:, 256:384]
        EXA[...] += ext
        return c

    lax.fori_loop(0, 4, spec_front, 0)
    if fused:
        gather_2.along_x()
        gather_f.between()
    low_half = lax.broadcasted_iota(jnp.int32, (HALF, 128), 1) < 64

    def split_ext(x):
        re = jnp.where(low_half, x, 0.0)
        im = jnp.where(low_half, pltpu.roll(x, 64, axis=1), 0.0)
        return re, im

    def join_ext(re, im):
        return jnp.where(low_half, re, pltpu.roll(im, 64, axis=1))

    ext_re, ext_im = split_ext(EXA[...])
    ST[16, 0:HALF] = ext_re.astype(BF)
    ST[16, HALF : 2 * HALF] = ext_im.astype(BF)

    def grab(ref, g, base):
        z = []
        for a in range(16):
            rows = pl.ds(pl.multiple_of(a * HALF + g * 8, 8), 8)
            z.append((ref[rows, base : base + 128], ref[rows, base + 128 : base + 256]))
        return z

    def fwd_fft(i, c):
        halves = [dft16(grab(DY, 2 * i + s, 256), -1) for s in range(2)]
        for k in range(16):
            for comp in range(2):
                both = jnp.concatenate([halves[0][k][comp], halves[1][k][comp]], axis=0)
                ST[k, pl.ds(pl.multiple_of(comp * HALF + i * 16, 16), 16)] = both.astype(BF)
        return c

    lax.fori_loop(0, 12, fwd_fft, 0)

    if fused:
        gather_1.along_x()
        gather_2.between()
        gather_f.last()
        for j in range(3):
            parts = [WFO[s // 2, s % 2, 48 * j : 48 * j + 48] for s in range(D)]
            fu = jnp.concatenate(parts, axis=0)
            WFU[:, 128 * j : 128 * j + 128] = fu
            WFUT[128 * j : 128 * j + 128, :] = fu.astype(F32).T.astype(BF)
            parts = [WFO[s // 2, s % 2, 144 + 32 * j : 176 + 32 * j].astype(F32)[0:24] for s in range(D)]
            WOUT[:, 128 * j : 128 * j + 128] = jnp.concatenate(parts, axis=0).astype(BF)

    def unit(ts):
        w = WFUT[...]
        s0 = s1 = None
        for t in ts:
            pf = dot(w, jnp.concatenate([ST[2 * t], ST[2 * t + 1]], axis=1))
            PF[2 * t] = pf[:, 0:128]
            PF[2 * t + 1] = pf[:, 128:256]
            s0 = lane_pair(pf) if s0 is None else s0 + lane_pair(pf)
            s1 = lane_pair(pf * pf) if s1 is None else s1 + lane_pair(pf * pf)
        return s0, s1

    pf = dot(WFUT[...], ST[16])
    PF[16] = pf
    ACF[0:384] = pf
    ACF[384:768] = pf * pf

    def unit_step(i, c):
        s0, s1 = unit([4 * i + e for e in range(4)])
        ACF[0:384] += s0
        ACF[384:768] += s1
        return c

    lax.fori_loop(0, 2, unit_step, 0)

    def freq_rows():
        return [to_row(ACF[128 * j : 128 * j + 128]) for j in range(6)]

    put_rows(1, 0, freq_rows())
    ar_start(1)

    if fused:
        gather_1.between()
        gather_2.last()
        for s in range(D):
            for j in range(4):
                WCAT[144 * s : 144 * s + 144, 128 * j : 128 * j + 128] = W2[s // 2, s % 2, 144 * j : 144 * j + 144]

    def slab(ref, i, off, lo, hi, n=8):
        return ref[pl.ds(n * i + off, n), :, lo:hi].reshape(n * SIDE, hi - lo)

    def block_rows(i):
        return pl.ds(pl.multiple_of(512 * i, 512), 512)

    def conv_loc(i, c):
        lhs = jnp.concatenate([slab(Z3, i, a, 0, 384) for a in range(3)], axis=1)
        PX[block_rows(i), :] = dot(lhs, WCAT[...])
        return c

    lax.fori_loop(0, 8, conv_loc, 0)

    tot = ar_wait(1)
    for j in range(3):
        scale, ms = moments(tot[j : j + 1], tot[j + 3 : j + 4], fcount)
        COLF[0, 128 * j : 128 * j + 128] = col(scale)
        COLF[1, 128 * j : 128 * j + 128] = col(ms)
    fold(COLF)
    lane = lax.broadcasted_iota(jnp.int32, (8, 128), 1)
    doubled = jnp.where(lax.rem(lane, 32) == 0, 1.0, 2.0).astype(F32)

    def freq_act(v, rows):
        return v * COLF[4, rows] + COLF[5, rows]

    def inv_fft(i, c):
        halves = []
        for s in range(2):
            z = []
            rr = pl.ds(pl.multiple_of(16 * i + 8 * s, 8), 8)
            ri = pl.ds(pl.multiple_of(HALF + 16 * i + 8 * s, 8), 8)
            for k in range(16):
                re = gelu_value(freq_act(PF[k, rr], rr)) * doubled
                im = gelu_value(freq_act(PF[k, ri], ri)) * doubled
                z.append((re, im))
            halves.append(dft16(z, 1))
        for a in range(16):
            for comp in range(2):
                both = jnp.concatenate([halves[0][a][comp], halves[1][a][comp]], axis=0)
                Y[a, pl.ds(pl.multiple_of(i * 16, 16), 16), 128 * comp : 128 * comp + 128] = both.astype(BF)
        return c

    lax.fori_loop(0, 12, inv_fft, 0)
    mixed = gelu_value(PF[16] * COLF[4] + COLF[5])
    EXB[...] = join_ext(mixed[0:HALF], mixed[HALF : 2 * HALF]).astype(BF)
    ROWP[8:24, :] = jnp.zeros((16, ALL), F32)

    def slab_rows(h0, j):
        return pl.ds(pl.multiple_of((h0 + 16 * j) * SIDE, SIDE), SIDE)

    def join(i, c):
        ext, w = EXB[...], WOUT[...]
        s0 = s1 = None
        for e in range(4):
            h0 = 4 * i + e
            back = dot(jnp.concatenate([Y[h0], ext], axis=1), A[h0], 1, 1)
            joined = (DY[rows_of(h0), 0:256] + back).astype(BF)
            J[h0] = joined
            pg = dot(joined, w, 0, 0)
            for j in range(4):
                v = PX[slab_rows(h0, j), 128:512] + pg[64 * j : 64 * j + 64]
                PX[slab_rows(h0, j), 128:512] = v
                s0 = rows8(v) if s0 is None else s0 + rows8(v)
                s1 = rows8(v * v) if s1 is None else s1 + rows8(v * v)
        ROWP[8:16, 128:512] += s0
        ROWP[16:24, 128:512] += s1
        return c

    lax.fori_loop(0, 4, join, 0)

    def put_norm_rows(k, lo, tiles):
        for j in range(tiles):
            at = lo + 128 * j
            put_rows(k, j, [jnp.sum(ROWP[8:16, at : at + 128], axis=0, keepdims=True)])
            put_rows(k, tiles + j, [jnp.sum(ROWP[16:24, at : at + 128], axis=0, keepdims=True)])

    put_norm_rows(3, 128, 3)
    ar_start(3)

    if fused:
        gather_1.last()
        for tap, c0, s, r0, n in gl_runs(D):
            WGL[tap // 3, c0 : c0 + n, 128 * (tap % 3) : 128 * (tap % 3) + 128] = W1[s // 2, s % 2, r0 : r0 + n]
    else:
        for tap in range(9):
            WGL[tap // 3, 0:384, 128 * (tap % 3) : 128 * (tap % 3) + 128] = WGLN[384 * tap : 384 * tap + 384]
    for tap in range(9):
        WGL[tap // 3, 384:512, 128 * (tap % 3) : 128 * (tap % 3) + 128] = WCAT[128 * tap : 128 * tap + 128, 0:128]

    def conv_glo(i, c):
        lhs = jnp.concatenate([slab(F, i, a, 0, 384) for a in range(3)], axis=1)
        gl = dot(lhs, jnp.concatenate([WGL[a, 0:384] for a in range(3)], axis=0))
        total = PX[block_rows(i), 0:128] + gl[:, 128:256] + shifted(gl[:, 0:128], 0, 1) + shifted(gl[:, 256:384], 63, -1)
        PX[block_rows(i), 0:128] = total
        ROWP[8:16, 0:128] += rows8(total)
        ROWP[16:24, 0:128] += rows8(total * total)
        return c

    lax.fori_loop(0, 8, conv_glo, 0)
    put_norm_rows(2, 0, 1)
    ar_start(2)

    def set_norm(tot, lo, tiles):
        for j in range(tiles):
            ls = slice(lo + 128 * j, lo + 128 * j + 128)
            scale, ms = moments(tot[j : j + 1], tot[tiles + j : tiles + j + 1], count)
            ROWP[0:1, ls] = scale
            ROWP[1:2, ls] = ms
            ROWP[4:5, ls] = scale * ROWP[2:3, ls]
            ROWP[5:6, ls] = ROWP[3:4, ls] - ms * ROWP[2:3, ls]

    def out_norm(lo, hi, sem):
        ROWP[8:24, lo:hi] = jnp.zeros((16, hi - lo), F32)

        def chunk(i, c):
            def one(hh, c2):
                h = 16 * i + hh
                for l0 in range(lo, hi, 128):
                    ls = slice(l0, l0 + 128)
                    s0 = s1 = None
                    for r in (0, 32):
                        at = pl.ds(pl.multiple_of(h * SIDE + r, 32), 32)
                        y = PX[at, ls] * ROWP[4:5, ls] + ROWP[5:6, ls]
                        value, slope = gelu_both(y)
                        dy = slope * (COT[h, r : r + 32, ls].astype(F32) * WF[h, r : r + 32].astype(F32))
                        DY[at, ls] = dy
                        if l0 == 0:
                            base = Z3[h + 1, r : r + 32, 128:256]
                        else:
                            base = F[h + 1, r : r + 32, l0 - 128 : l0]
                        DC[h + 1, r : r + 32, ls] = (base.astype(F32) + value).astype(BF)
                        s0 = rows8(dy) if s0 is None else s0 + rows8(dy)
                        s1 = rows8(dy * y) if s1 is None else s1 + rows8(dy * y)
                    ROWP[8:16, ls] += s0
                    ROWP[16:24, ls] += s1
                return c2

            lax.fori_loop(0, 16, one, 0)
            pltpu.make_async_copy(
                DC.at[pl.ds(16 * i + 1, 16), :, lo:hi], block_out.at[pl.ds(16 * i, 16), :, lo:hi], sem
            ).start()
            return c

        lax.fori_loop(0, 4, chunk, 0)

    copy_c.wait()
    set_norm(ar_wait(3), 128, 3)
    out_norm(128, 512, io_sem.at[4])
    put_norm_rows(5, 128, 3)
    ar_start(5)
    set_norm(ar_wait(2), 0, 1)
    out_norm(0, 128, io_sem.at[5])
    put_norm_rows(4, 0, 1)
    ar_start(4)

    def back_sums(tot, tiles, at):
        out = []
        for j in range(tiles):
            s1 = tot[j : j + 1]
            s2 = (tot[tiles + j : tiles + j + 1] - GBR[1, at + j : at + j + 1, :] * s1) / GBR[0, at + j : at + j + 1, :]
            norm_out[at + j : at + j + 1, :] = s2
            norm_out[16 + at + j : 17 + at + j, :] = s1
            out.append((s1, s2))
        return out

    norm_out[9:16, :] = jnp.zeros((7, 128), F32)
    norm_out[25:32, :] = jnp.zeros((7, 128), F32)

    def set_back(tot, lo, tiles, at):
        for j, (s1, s2) in enumerate(back_sums(tot, tiles, at)):
            ls = slice(lo + 128 * j, lo + 128 * j + 128)
            ROWP[6:7, ls] = ROWP[4:5, ls] * ROWP[0:1, ls] * (s2 / count)
            ROWP[7:8, ls] = ROWP[4:5, ls] * (ROWP[1:2, ls] * (s2 / count) - s1 / count)

    def norm_back(lo, hi, sem):
        pltpu.make_async_copy(DC.at[1:65, :, lo:hi], block_out.at[:, :, lo:hi], sem).wait()

        def one(h, c):
            for l0 in range(lo, hi, 128):
                ls = slice(l0, l0 + 128)
                for r in (0, 32):
                    at = pl.ds(pl.multiple_of(h * SIDE + r, 32), 32)
                    d = ROWP[4:5, ls] * DY[at, ls] - ROWP[6:7, ls] * PX[at, ls] + ROWP[7:8, ls]
                    DC[h + 1, r : r + 32, ls] = d.astype(BF)
            return c

        lax.fori_loop(0, SIDE, one, 0)

    set_back(ar_wait(5), 128, 3, 6)
    norm_back(128, 512, io_sem.at[4])

    EXA[...] = jnp.zeros_like(EXA)
    GOUT[...] = jnp.zeros_like(GOUT)

    def join_back(i, c):
        w = WOUT[...]
        dgs = []
        ext = None
        for e in range(4):
            h0 = 4 * i + e
            dg = tile(DC, h0, 128, 512)
            dgs.append(dg)
            dj = dot(w, dg, 1, 1)
            PX[rows_of(h0), 0:256] = dj
            res = dot(dj.astype(BF), A[h0])
            PX[rows_of(h0), 256:512] = res[:, 0:256]
            ext = res[:, 256:384] if ext is None else ext + res[:, 256:384]
        EXA[...] += ext
        lhs = jnp.concatenate([J[4 * i + e] for e in range(4)], axis=1)
        GOUT[...] += dot(lhs, jnp.concatenate(dgs, axis=0))
        return c

    set_back(ar_wait(4), 0, 1, 5)
    norm_back(0, 128, io_sem.at[5])
    lax.fori_loop(0, 4, join_back, 0)

    def freq_back(g, c):
        z = dft16(grab(PX, g, 256), -1)
        for comp in range(2):
            rows = pl.ds(pl.multiple_of(comp * HALF + 8 * g, 8), 8)
            s0 = s1 = None
            for k in range(16):
                y = freq_act(PF[k, rows], rows)
                dy = gelu_slope(y) * (z[k][comp] * doubled)
                r0, l0 = dyf_pos(k)
                DY[pl.ds(pl.multiple_of(r0 + comp * HALF + 8 * g, 8), 8), l0 : l0 + 128] = dy
                s0 = dy if s0 is None else s0 + dy
                s1 = dy * y if s1 is None else s1 + dy * y
            ACF[rows] = s0
            ACF[pl.ds(pl.multiple_of(384 + comp * HALF + 8 * g, 8), 8)] = s1
        return c

    lax.fori_loop(0, 24, freq_back, 0)
    ext_re, ext_im = split_ext(EXA[...])
    y = PF[16] * COLF[4] + COLF[5]
    dy = gelu_slope(y) * jnp.concatenate([ext_re, ext_im], axis=0)
    DYX[...] = dy
    ACF[0:384] += dy
    ACF[384:768] += dy * y
    put_rows(6, 0, freq_rows())
    ar_start(6)

    def make_d3(i, c):
        for e in range(2):
            h = 2 * i + e + 1
            x = DC[h, :, 0:128]
            D3[h, :, 0:128] = shifted(x.astype(F32), 63, -1).astype(BF)
            D3[h, :, 128:256] = x
            D3[h, :, 256:384] = shifted(x.astype(F32), 0, 1).astype(BF)
        return c

    lax.fori_loop(0, 32, make_d3, 0)

    def wgrad_glo(i, first):
        zt = slab(F, i, 1, 0, 384, 16).T
        res = dot(zt, jnp.concatenate([slab(D3, i, 2 - a, 0, 384, 16) for a in range(3)], axis=1))
        for tap in range(9):
            r = 384 * tap
            part = res[:, 128 * tap : 128 * tap + 128]
            DY[r : r + 384, 0:128] = part if first else DY[r : r + 384, 0:128] + part

    def wgrad_loc(i, first):
        zt = slab(Z3, i, 1, 0, 384, 16).T
        for a in range(3):
            res = dot(zt, slab(DC, i, 2 - a, 0, 512, 16))
            r = 384 * a
            if first:
                DY[1152 + r : 1536 + r, 128:256] = res[:, 0:128]
                DY[r : r + 384, 128:512] = res[:, 128:512]
            else:
                DY[1152 + r : 1536 + r, 128:256] += res[:, 0:128]
                DY[r : r + 384, 128:512] += res[:, 128:512]

    def rest(f):
        def body(i, c):
            f(i, False)
            return c

        f(0, True)
        lax.fori_loop(1, 4, body, 0)

    rest(wgrad_glo)
    if fused:
        for tap, c0, s, r0, n in gl_runs(D):
            r = 384 * tap + c0
            W1[s // 2, s % 2, r0 : r0 + n] = DY[r : r + n, 0:128].astype(BF)
        for s in range(D):
            W1[s // 2, s % 2, 432:448] = jnp.zeros((16, 128), BF)
        scatter_1 = Scatter(ring, W1, RS[0], rs_sem, 0)
        scatter_2 = Scatter(ring, W2, RS[1], rs_sem, 10)
        scatter_f = Scatter(ring, WFO, RS[2], rs_sem, 20)
        scatter_i = Scatter(ring, GI, RS[3], rs_sem, 30)
        scatter_1.between()
    rest(wgrad_loc)
    if fused:
        scatter_1.along_x()
        for s in range(D):
            W2[s // 2, s % 2, 0:144] = DY[1152 + 144 * s : 1296 + 144 * s, 128:256].astype(BF)
            for j in range(3):
                ls = slice(128 + 128 * j, 256 + 128 * j)
                W2[s // 2, s % 2, 144 + 144 * j : 288 + 144 * j] = DY[144 * s : 144 * s + 144, ls].astype(BF)
        scatter_2.between()
    else:
        put(DY.at[0:3456, 0:128], out_gl)
        put(DY.at[1152:2304, 128:256], out_ll)
        put(DY.at[0:1152, 128:512], out_lg)

    tot = ar_wait(6)
    for j, (s1, s2) in enumerate(back_sums(tot, 3, 2)):
        at = slice(128 * j, 128 * j + 128)
        COLF[6, at] = COLF[4, at] * COLF[0, at] * col(s2 / fcount)
        COLF[7, at] = COLF[4, at] * (COLF[1, at] * col(s2 / fcount) - col(s1 / fcount))

    def gfu_at(j, lo=0, n=384):
        return (slice(384 * (j // 2) + lo, 384 * (j // 2) + lo + n), slice(256 + 128 * (j % 2), 384 + 128 * (j % 2)))

    def dpf_tile(k, dy):
        return (COLF[4] * dy - COLF[6] * PF[k] + COLF[7]).astype(BF)

    dpf = dpf_tile(16, DYX[...])
    res = dot(ST[16], dpf, 1, 1)
    for j in range(3):
        PX[gfu_at(j)] = res[:, 128 * j : 128 * j + 128]
    ds = dot(WFU[...], dpf)
    EXB[...] = join_ext(ds[0:HALF], ds[HALF : 2 * HALF]).astype(BF)
    for t in range(4):
        spots = [dyf_pos(4 * t + e) for e in range(4)]
        parts = [dpf_tile(4 * t + e, DY[r : r + 384, l : l + 128]) for e, (r, l) in enumerate(spots)]
        dpf = jnp.concatenate(parts, axis=1)
        res = dot(jnp.concatenate([ST[4 * t + e] for e in range(4)], axis=1), dpf, 1, 1)
        for j in range(3):
            PX[gfu_at(j)] += res[:, 128 * j : 128 * j + 128]
        ds = dot(WFU[...], dpf)
        for e, (r, l) in enumerate(spots):
            DY[r : r + 384, l : l + 128] = ds[:, 128 * e : 128 * e + 128]
    if fused:
        scatter_1.along_y()
        scatter_2.along_x()
        for s in range(D):
            for j in range(3):
                ls = slice(128 * j, 128 * j + 128)
                WFO[s // 2, s % 2, 48 * j : 48 * j + 48] = PX[gfu_at(j, 48 * s, 48)].astype(BF)
                part = jnp.concatenate([GOUT[24 * s : 24 * s + 24, ls], jnp.zeros((8, 128), F32)], axis=0)
                WFO[s // 2, s % 2, 144 + 32 * j : 176 + 32 * j] = part.astype(BF)
            WFO[s // 2, s % 2, 240:256] = jnp.zeros((16, 128), BF)
        scatter_f.between()
    else:
        for j in range(3):
            put(PX.at[gfu_at(j)], out_fu.at[:, 128 * j : 128 * j + 128])
        put(GOUT, out_out)

    def adj_fft(i, c):
        halves = []
        for s in range(2):
            z = []
            for k in range(16):
                r0, l0 = dyf_pos(k)
                pair = []
                for comp in range(2):
                    at = pl.ds(pl.multiple_of(r0 + comp * HALF + 16 * i + 8 * s, 8), 8)
                    pair.append(DY[at, l0 : l0 + 128])
                z.append(tuple(pair))
            halves.append(dft16(z, 1))
        for a in range(16):
            for comp in range(2):
                both = jnp.concatenate([halves[0][a][comp], halves[1][a][comp]], axis=0)
                Y[a, pl.ds(pl.multiple_of(i * 16, 16), 16), 128 * comp : 128 * comp + 128] = both.astype(BF)
        return c

    lax.fori_loop(0, 12, adj_fft, 0)
    if fused:
        scatter_1.along_z()
        scatter_f.along_x()
    ACC[...] = jnp.zeros_like(ACC)

    def spec_back(i, c):
        gain, bias, ext = two(COLS[4]), two(COLS[5]), EXB[...]
        s0 = s1 = None
        for e in range(4):
            h0 = 4 * i + e
            back = dot(jnp.concatenate([Y[h0], ext], axis=1), A[h0], 1, 1)
            y = PS[h0] * gain + bias
            dy = gelu_slope(y) * (PX[rows_of(h0), 0:256] + back)
            DY[rows_of(h0), 256:512] = dy
            s0 = lane_pair(dy) if s0 is None else s0 + lane_pair(dy)
            s1 = lane_pair(dy * y) if s1 is None else s1 + lane_pair(dy * y)
        ACC[0:HALF] += s0
        ACC[HALF : 2 * HALF] += s1
        return c

    lax.fori_loop(0, 4, spec_back, 0)
    put_rows(7, 0, spec_rows())
    ar_start(7)
    if fused:
        scatter_2.along_y()
        scatter_1.to_copies()

    def dgrad(i, c):
        lhs = jnp.concatenate([slab(DC, i, 2 - a, 128, 512) for a in range(3)], axis=1)
        rhs = jnp.concatenate([WCAT[384 * a : 384 * a + 384, 128:512] for a in range(3)], axis=1)
        res = dot(lhs, rhs, 1, 1)
        lhs = jnp.concatenate([slab(D3, i, 2 - a, 0, 384) for a in range(3)], axis=1)
        both = dot(lhs, jnp.concatenate([WGL[a] for a in range(3)], axis=1), 1, 1)
        PX[block_rows(i), 128:512] = both[:, 0:384]
        loc = both[:, 384:512] + res[:, 128:256] + shifted(res[:, 0:128], 63, -1) + shifted(res[:, 256:384], 0, 1)
        DC[pl.ds(8 * i + 1, 8), :, 0:128] = loc.astype(BF).reshape(8, SIDE, 128)
        return c

    lax.fori_loop(0, 4, dgrad, 0)
    if fused:
        scatter_2.along_z()
        scatter_f.along_y()

    tot = ar_wait(7)
    for r, (s1, s2) in enumerate(back_sums(tot, 2, 0)):
        n = 128 - 64 * r
        at = slice(128 * r, 128 * r + n)
        COLS[6, at] = COLS[4, at] * COLS[0, at] * col(s2 / count)[0:n]
        COLS[7, at] = COLS[4, at] * (COLS[1, at] * col(s2 / count)[0:n] - col(s1 / count)[0:n])
    GOUT[...] = jnp.zeros_like(GOUT)

    def spec_grad(i, c):
        f4, f6, f7 = two(COLS[4]), two(COLS[6]), two(COLS[7])
        ds = []
        for e in range(4):
            h0 = 4 * i + e
            d = (f4 * DY[rows_of(h0), 256:512] - f6 * PS[h0] + f7).astype(BF)
            J[h0] = d
            ds.append(d)
        rhs = jnp.concatenate([tile(F, 4 * i + e, 0, GLO) for e in range(4)], axis=0)
        GOUT[...] += dot(jnp.concatenate(ds, axis=1), rhs)
        return c

    lax.fori_loop(0, 4, spec_grad, 0)
    if fused:
        gin = jnp.concatenate([GOUT[...], jnp.zeros((64, 384), F32)], axis=0).T
        for s in range(D):
            GI[s // 2, s % 2, 0:48] = gin[48 * s : 48 * s + 48, 0:128].astype(BF)
            GI[s // 2, s % 2, 48:96] = gin[48 * s : 48 * s + 48, 128:256].astype(BF)
            GI[s // 2, s % 2, 96:128] = jnp.zeros((32, 128), BF)
        scatter_i.between()
        scatter_f.along_z()
    else:
        put(GOUT, out_in)
    lax.fori_loop(4, 6, dgrad, 0)
    if fused:
        scatter_i.along_x()
        scatter_2.to_copies()
    lax.fori_loop(6, 8, dgrad, 0)
    if fused:
        scatter_i.along_y()
        scatter_f.to_copies()

    def field_copy(h):
        return pltpu.make_async_copy(DC.at[pl.ds(h + 1, 4)], field_out.at[pl.ds(h, 4)], io_sem.at[6])

    def spec_field(i, c):
        w = WINT[...]
        for e in range(4):
            h0 = 4 * i + e
            dg = dot(J[h0], w, 0, 0)
            for j in range(4):
                total = PX[slab_rows(h0, j), 128:512] + dg[64 * j : 64 * j + 64]
                DC[h0 + 16 * j + 1, :, 128:512] = total.astype(BF)
        for j in range(4):
            field_copy(4 * i + 16 * j).start()
        return c

    lax.fori_loop(0, 2, spec_field, 0)
    if fused:
        scatter_i.along_z()
    lax.fori_loop(2, 4, spec_field, 0)
    if fused:
        scatter_i.to_copies()
        for n, sc in enumerate((scatter_1, scatter_2, scatter_f, scatter_i)):
            sc.last()
            for r in range(4):
                at = STARTS[n] + r * sc.q
                flat_out[at : at + sc.q, :] = sc.done[r]
        await_bytes(WI.at[pl.ds(0, D - 1)], g_sem.at[0])
        await_bytes(GBB.at[pl.ds(0, D - 1)], g_sem.at[2])
    pltpu.make_async_copy(DC.at[1:65], field_out, io_sem.at[6]).wait()


def run_block(features, cotangent, holes, weights, gains, biases, fused):
    dps, reps = lax.axis_size("dp"), lax.axis_size("rep")
    N = dps * reps
    any_spec = pl.BlockSpec(memory_space=pl.ANY)
    vmem = pl.BlockSpec(memory_space=pltpu.VMEM)
    table = jnp.asarray(dft_table())
    args = [features, cotangent, holes, table] + list(weights) + list(gains)
    if fused:
        args = args + list(biases)
    out_shape = [
        jax.ShapeDtypeStruct((SIDE, SIDE, ALL), BF),
        jax.ShapeDtypeStruct((SIDE, SIDE, ALL), BF),
        jax.ShapeDtypeStruct((32, 128), F32),
    ]
    if fused:
        out_shape.append(jax.ShapeDtypeStruct((1408, 128), BF))
    else:
        for shape in ((1152, 128), (3456, 128), (1152, 384), (192, 384), (384, 384), (192, 384)):
            out_shape.append(jax.ShapeDtypeStruct(shape, F32))
    V = pltpu.VMEM
    dma = pltpu.SemaphoreType.DMA
    scratch = [
        V((66, SIDE, 384), BF),
        V((SIDE, SIDE, 128), BF),
        V((66, SIDE, 384), BF),
        V((66, SIDE, 384), BF),
        V((POS, ALL), F32),
        V((POS, ALL), F32),
        V((16, HALF, 256), F32),
        V((17, 384, 128), BF),
        V((17, 384, 128), F32),
        V((16, HALF, 256), BF),
        V((16, HALF, 256), BF),
        V((66, SIDE, ALL), BF),
        V((16, 256, 384), BF),
        V((SIDE, SIDE, ALL), BF),
        V((HALF, 128), F32),
        V((HALF, 128), BF),
        V((384, 128), F32),
        V((384, 128), F32),
        V((768, 128), F32),
        V((8, HALF, 128), F32),
        V((8, 384, 128), F32),
        V((24, ALL), F32),
        V((2, 16, 128), F32),
        V((HALF, 384), F32),
        V((3, ALL, 384), BF),
    ]
    scratch += [V((N, n, 128), F32) for n in AR_ROWS]
    scratch += [dma((8,)), dma((8,)), dma((8,))]
    if fused:
        scratch += [
            V((1152, ALL), BF),
            V((HALF, 384), BF),
            V((384, 384), BF),
            V((384, 384), BF),
            V((HALF, 384), BF),
            V((dps, 96, 128), BF),
            V((dps, 4, 128), F32),
            V((96, 128), BF),
            dma((34,)),
            dma((40,)),
        ]
        scratch += [V((n, 128), BF) for n in CHUNKS[:3]]
        scratch += [V((4, 2, n, 128), BF) for n in CHUNKS]
        for n in CHUNKS:
            q = n // 4
            scratch += [V((4, 2, 2 * q, 128), BF), V((4, 2, q, 128), BF)] + [V((4, q, 128), BF)] * 3
    return pl.pallas_call(
        functools.partial(kernel, dps, reps, fused),
        out_shape=out_shape,
        in_specs=[any_spec, any_spec, vmem, any_spec] + [vmem] * (len(args) - 4),
        out_specs=[any_spec, any_spec, vmem] + ([vmem] if fused else [any_spec] * 6),
        scratch_shapes=scratch,
        compiler_params=pltpu.CompilerParams(
            collective_id=0, has_side_effects=True, vmem_limit_bytes=64 * 1024 * 1024 - 65536
        ),
        cost_estimate=pl.CostEstimate(flops=40_000_000_000, bytes_accessed=30_000_000, transcendentals=10_000_000),
    )(*args)


def finish_kernel(share, fused, *refs):
    it = iter(refs)
    cot, field, block, holes, norms = (next(it) for _ in range(5))
    flat = next(it) if fused else None
    o_block, o_input = next(it), next(it)
    grads = [next(it) for _ in range(6)] if fused else []
    o_gain, o_bias = next(it), next(it)
    o_block[...] = block[...]
    for h in range(8):
        wf = mask_tile(0.25 + holes[h : h + 1, :].astype(F32))
        for l0 in range(0, ALL, 128):
            ls = slice(l0, l0 + 128)
            o_input[h, :, ls] = (cot[h, :, ls].astype(F32) * wf + field[h, :, ls].astype(F32)).astype(BF)

    @pl.when(pl.program_id(0) == 0)
    def _():
        if fused:
            g_ll, g_gl, g_lg, g_in, g_fu, g_out = grads
            g_gl[0] = flat[0:432].astype(F32)
            g_ll[0] = flat[448:592].astype(F32)
            for j in range(3):
                ls = slice(128 * j, 128 * j + 128)
                g_lg[0, :, ls] = flat[592 + 144 * j : 736 + 144 * j].astype(F32)
                g_fu[0, :, ls] = flat[1024 + 48 * j : 1072 + 48 * j].astype(F32)
                g_out[0, :, ls] = flat[1168 + 32 * j : 1200 + 32 * j].astype(F32)[0:24]
            g_in[0, :, 0:128] = flat[1280:1328].astype(F32)
            g_in[0, :, 128:192] = flat[1328:1376].astype(F32)[:, 0:64]
        first = share * lax.axis_index("dp")
        lane = lax.broadcasted_iota(jnp.int32, (8, 1152), 1)
        for at, ref in ((0, o_gain), (16, o_bias)):
            row = jnp.concatenate([norms[at + j : at + j + 1, :] for j in range(9)], axis=1)
            row = jnp.broadcast_to(row, (8, 1152))
            row = jnp.where(lane < HALF, row, pltpu.roll(row, 1152 - 64, axis=1))
            row = pltpu.roll(row, lax.rem(1152 - first, 1152), axis=1)
            ref[...] = row[0:1, 0:share]


def finish(cotangent, field, block, holes, norms, flat, share, shapes):
    fused = flat is not None
    maps = pl.BlockSpec((8, SIDE, ALL), lambda i: (i, 0, 0))

    def whole(shape):
        return pl.BlockSpec(shape, lambda i, n=len(shape): (0,) * n)

    args = [cotangent, field, block, holes, norms] + ([flat] if fused else [])
    in_specs = [maps, maps, maps, pl.BlockSpec((8, SIDE), lambda i: (i, 0))]
    in_specs += [whole(a.shape) for a in args[4:]]
    out_shape = [jax.ShapeDtypeStruct((SIDE, SIDE, ALL), BF)] * 2
    out_specs = [maps, maps]
    small = (list(shapes) if fused else []) + [(1, share), (1, share)]
    out_shape += [jax.ShapeDtypeStruct(shape, F32) for shape in small]
    out_specs += [whole(shape) for shape in small]
    return pl.pallas_call(
        functools.partial(finish_kernel, share, fused),
        grid=(8,),
        out_shape=out_shape,
        in_specs=in_specs,
        out_specs=out_specs,
        compiler_params=pltpu.CompilerParams(vmem_limit_bytes=64 * 1024 * 1024 - 65536),
    )(*args)


def on_device(features, cotangent, holes, w_ll, w_gl, w_lg, w_in, w_fu, w_out, gains, biases):
    dps, reps = lax.axis_size("dp"), lax.axis_size("rep")
    share = gains.shape[1]
    shards = (w_ll, w_gl, w_lg, w_in, w_fu, w_out)
    if dps == 8 and reps == 4:
        weights = [w[0] for w in shards]
        block, field, norms, flat = run_block(features[0], cotangent[0], holes[0], weights, [gains], [biases], True)
        block_out, input_grad, *small = finish(
            cotangent[0], field, block, holes[0], norms, flat, share, [w.shape for w in shards]
        )
        return (block_out[None], input_grad[None], *small)
    full = [lax.all_gather(w, "dp", axis=1, tiled=True)[0] for w in shards]
    table = jnp.concatenate([gains, biases], axis=0).astype(F32)
    table = lax.all_gather(table, "dp", axis=1, tiled=True)
    table = jnp.pad(table, ((0, 0), (0, 1152 - table.shape[1])), constant_values=1.0).reshape(18, 128)
    table = jnp.pad(table, ((0, 6), (0, 0)))
    weights = [jnp.concatenate([full[0], full[2]], axis=1), full[1], full[3].T, full[4], full[4].T, full[5]]
    block, field, norms, g_ll, g_gl, g_lg, g_in, g_fu, g_out = run_block(
        features[0], cotangent[0], holes[0], weights, [table], None, False
    )
    grads = []
    for g in (g_ll, g_gl, g_lg, g_in.T, g_fu, g_out):
        g = lax.psum(g[None], "rep")
        grads.append(lax.psum_scatter(g, "dp", scatter_dimension=1, tiled=True))
    block_out, input_grad, *small = finish(cotangent[0], field, block, holes[0], norms, None, share, ())
    return (block_out[None], input_grad[None], *grads, *small)


def solution(mesh):
    whole = P(("dp", "rep"), None, None, None)
    rows = P(None, "dp", None)
    in_specs = (whole, whole, P(("dp", "rep"), None, None)) + (rows,) * 6 + (P(None, "dp"),) * 2
    out_specs = (whole, whole) + (rows,) * 6 + (P(None, "dp"),) * 2
    return jax.shard_map(on_device, mesh=mesh, in_specs=in_specs, out_specs=out_specs, check_vma=False)
```

```python
import functools
import math

import jax
import jax.numpy as jnp
import ml_dtypes
import numpy as np
from jax import lax
from jax.experimental import pallas as pl
from jax.experimental.pallas import tpu as pltpu
from jax.sharding import PartitionSpec as P

EPS = 1e-05
K0 = math.sqrt(2.0 / math.pi)
K1 = 0.044715
MESH = pl.DeviceIdType.MESH
F32 = jnp.float32
BF = jnp.bfloat16
SIDE = 64
LOC = 128
GLO = 384
HALF = 192
ALL = LOC + GLO
WIDTHS = (HALF, GLO, LOC, GLO)
POS = SIDE * SIDE
FREQ = SIDE * (SIDE // 2 + 1)


def dft_table():
    a = np.arange(16)[:, None, None, None, None]
    j = np.arange(4)[None, :, None, None, None]
    w = np.arange(64)[None, None, :, None, None]
    k1 = np.arange(4)[None, None, None, :, None]
    l = np.arange(32)[None, None, None, None, :]
    angle = 2 * np.pi / 64 * (((a + 16 * j) * k1 + w * l) % 64)
    main_re = np.cos(angle).reshape(16, 256, 128) / 64
    main_im = -np.sin(angle).reshape(16, 256, 128) / 64
    k = np.arange(64)[None, None, None, :]
    a, j, w = a[..., 0], j[..., 0], w[..., 0]
    angle = 2 * np.pi / 64 * (((a + 16 * j) * k + 32 * w) % 64)
    ext_re = np.cos(angle).reshape(16, 256, 64) / 64
    ext_im = -np.sin(angle).reshape(16, 256, 64) / 64
    return np.concatenate([main_re, main_im, ext_re, ext_im], axis=-1).astype(ml_dtypes.bfloat16)


def dot(a, b, ca=1, cb=0):
    return lax.dot_general(a, b, (((ca,), (cb,)), ((), ())), preferred_element_type=F32)


def gate(y):
    y2 = y * y
    return y2, 0.5 + 0.5 * jnp.tanh(y * (K0 + K0 * K1 * y2))


def gelu_value(y):
    return y * gate(y)[1]


def gelu_both(y):
    y2, s = gate(y)
    value = y * s
    return value, s + value * (1.0 - s) * (2.0 * K0 + 6.0 * K0 * K1 * y2)


def gelu_slope(y):
    return gelu_both(y)[1]


def cmul(z, c, s):
    return (z[0] * c - z[1] * s, z[0] * s + z[1] * c)


def dft4(z, sign):
    (ar, ai), (br, bi), (cr, ci), (dr, di) = z
    pr, pi, qr, qi = ar + cr, ai + ci, ar - cr, ai - ci
    rr, ri, sr, si = br + dr, bi + di, br - dr, bi - di
    tr, ti = (si, -sr) if sign < 0 else (-si, sr)
    return [(pr + rr, pi + ri), (qr + tr, qi + ti), (pr - rr, pi - ri), (qr - tr, qi - ti)]


def dft16(z, sign):
    cols = []
    for n2 in range(4):
        part = dft4([z[4 * n1 + n2] for n1 in range(4)], sign)
        for k1 in range(1, 4):
            e = n2 * k1
            if e == 0:
                continue
            if e == 4:
                re, im = part[k1]
                part[k1] = (im, -re) if sign < 0 else (-im, re)
            else:
                ang = sign * 2 * math.pi * e / 16
                part[k1] = cmul(part[k1], math.cos(ang), math.sin(ang))
        cols.append(part)
    out = [None] * 16
    for k1 in range(4):
        part = dft4([cols[n2][k1] for n2 in range(4)], sign)
        for k2 in range(4):
            out[k1 + 4 * k2] = part[k2]
    return out


def dyf_pos(t):
    if t < 12:
        return 2304 + 384 * (t // 3), 128 + 128 * (t % 3)
    u = t - 12
    return 1152 + 384 * (u // 2), 256 + 128 * (u % 2)


def rows8(x):
    acc = x[0:8]
    for r in range(8, x.shape[0], 8):
        acc = acc + x[r : r + 8]
    return acc


def lane_pair(x):
    return x[:, 0:128] + x[:, 128:256]


def await_bytes(ref, sem):
    pltpu.make_async_copy(ref, ref, sem).wait()


class Ring:
    def __init__(self, dps, reps):
        self.D, self.R = dps, reps
        self.N = dps * reps
        self.dp = lax.axis_index("dp")
        self.rp = lax.axis_index("rep")
        self.me = self.dp * reps + self.rp
        self.core = lax.rem(self.rp, 2)
        self.x = lax.div(self.rp, 2)
        self.y = lax.rem(self.dp, 2)
        self.z = lax.div(self.dp, 2)

    def dev(self, i):
        return (lax.div(i, self.R), lax.rem(i, self.R))

    def barrier(self):
        sem = pltpu.get_barrier_semaphore()

        def body(d, c):
            peer = lax.rem(self.me + d, self.N)
            pl.semaphore_signal(sem, inc=1, device_id=self.dev(peer), device_id_type=MESH)
            return c

        lax.fori_loop(1, self.N, body, 0)
        pl.semaphore_wait(sem, self.N - 1)

    def send(self, src, dst, ss, rs, device):
        pltpu.make_async_remote_copy(
            src_ref=src, dst_ref=dst, send_sem=ss, recv_sem=rs, device_id=device, device_id_type=MESH
        ).start()

    def sibling(self):
        return (self.dp, self.rp + 1 - 2 * self.core)

    def across(self):
        return (self.dp, lax.rem(self.rp + 2, 4))

    def beside(self):
        return (self.dp + 1 - 2 * self.y, self.rp)


class Gather:
    def __init__(self, ring, own, buf, sems, base):
        self.ring, self.own, self.buf, self.sems, self.base = ring, own, buf, sems, base
        self.q = own.shape[0] // 4

    def sem(self, i):
        return self.sems.at[self.base + i]

    def rows(self, i):
        return pl.ds(pl.multiple_of(i * self.q, 16), self.q)

    def place(self):
        rows = self.rows(self.ring.rp)
        self.buf[self.ring.z, self.ring.y, rows] = self.own[rows]

    def along_z(self):
        g = self.ring
        rows = self.rows(g.rp)
        for d in range(1, 4):
            there = (2 * lax.rem(g.z + d, 4) + g.y, g.rp)
            g.send(self.own.at[rows], self.buf.at[g.z, g.y, rows], self.sem(0), self.sem(1), there)

    def along_y(self):
        g = self.ring
        await_bytes(self.buf.at[pl.ds(0, 3), 0, pl.ds(0, self.q)], self.sem(1))
        part = self.buf.at[:, g.y, self.rows(g.rp)]
        g.send(part, part, self.sem(2), self.sem(3), g.beside())

    def along_x(self):
        g = self.ring
        await_bytes(self.buf.at[:, 0, pl.ds(0, self.q)], self.sem(3))
        part = self.buf.at[:, :, self.rows(g.rp)]
        g.send(part, part, self.sem(4), self.sem(5), g.across())
        g.send(part, part, self.sem(6), self.sem(7), g.sibling())

    def between(self):
        g = self.ring
        await_bytes(self.buf.at[:, :, pl.ds(0, self.q)], self.sem(5))
        part = self.buf.at[:, :, self.rows(lax.rem(g.rp + 2, 4))]
        g.send(part, part, self.sem(8), self.sem(9), g.sibling())

    def last(self):
        one = self.buf.at[:, :, pl.ds(0, self.q)]
        for i in (7, 9, 4, 6, 8):
            await_bytes(one, self.sem(i))
        await_bytes(self.buf.at[pl.ds(0, 3), 0, pl.ds(0, self.q)], self.sem(0))
        await_bytes(self.buf.at[:, 0, pl.ds(0, self.q)], self.sem(2))


class Scatter:
    def __init__(self, ring, buf, scratch, sems, base):
        self.ring, self.buf, self.sems, self.base = ring, buf, sems, base
        self.one, self.two, self.three, self.four, self.done = scratch
        self.q = buf.shape[2] // 4
        self.slot = 2 * ring.core + ring.x

    def sem(self, i):
        return self.sems.at[self.base + i]

    def rows(self, index, n):
        return pl.ds(pl.multiple_of(index * self.q, 16), n * self.q)

    def between(self):
        g = self.ring
        there = self.buf.at[:, :, self.rows(2 * (1 - g.core), 2)]
        g.send(there, self.one, self.sem(0), self.sem(1), g.sibling())

    def add(self, zi, yi, at, other):
        self.buf[zi, yi, at] = (self.buf[zi, yi, at].astype(F32) + other.astype(F32)).astype(BF)

    def along_x(self):
        g = self.ring
        await_bytes(self.one, self.sem(1))

        def body(s, c):
            zi, yi = lax.div(s, 2), lax.rem(s, 2)
            self.add(zi, yi, self.rows(2 * g.core, 2), self.one[zi, yi])
            return c

        lax.fori_loop(0, 8, body, 0)
        there = self.buf.at[:, :, self.rows(2 * g.core + 1 - g.x, 1)]
        g.send(there, self.two, self.sem(2), self.sem(3), g.across())

    def along_y(self):
        g = self.ring
        await_bytes(self.two, self.sem(3))
        at = self.rows(self.slot, 1)

        def body(s, c):
            zi, yi = lax.div(s, 2), lax.rem(s, 2)
            self.add(zi, yi, at, self.two[zi, yi])
            return c

        lax.fori_loop(0, 8, body, 0)
        g.send(self.buf.at[:, 1 - g.y, at], self.three, self.sem(4), self.sem(5), g.beside())

    def along_z(self):
        g = self.ring
        await_bytes(self.three, self.sem(5))
        at = self.rows(self.slot, 1)
        for k in range(4):
            self.add(k, g.y, at, self.three[k])
        for d in range(1, 4):
            zz = lax.rem(g.z + d, 4)
            g.send(self.buf.at[zz, g.y, at], self.four.at[g.z], self.sem(6), self.sem(7), (2 * zz + g.y, g.rp))
        self.four[g.z] = self.buf[g.z, g.y, at]

    def to_copies(self):
        g = self.ring
        await_bytes(self.four.at[pl.ds(0, 3)], self.sem(7))
        total = self.four[0].astype(F32)
        for k in range(1, 4):
            total = total + self.four[k].astype(F32)
        self.done[self.slot] = total.astype(BF)
        mine = self.done.at[self.slot]
        for d in range(1, 4):
            g.send(mine, mine, self.sem(8), self.sem(9), (g.dp, lax.rem(g.rp + d, 4)))

    def last(self):
        three = self.done.at[pl.ds(0, 3)]
        await_bytes(three, self.sem(9))
        await_bytes(self.one, self.sem(0))
        await_bytes(self.two, self.sem(2))
        await_bytes(self.three, self.sem(4))
        await_bytes(self.four.at[pl.ds(0, 3)], self.sem(6))
        await_bytes(three, self.sem(8))


class GatherHalf(Gather):
    def __init__(self, ring, own, buf, sems, base):
        super().__init__(ring, own, buf, sems, base)
        self.q = own.shape[0] // 2

    def place(self):
        rows = self.rows(self.ring.core)
        self.buf[self.ring.z, self.ring.y, rows] = self.own[rows]

    def along_z(self):
        g = self.ring
        rows = self.rows(g.core)
        for d in range(1, 4):
            there = (2 * lax.rem(g.z + d, 4) + g.y, g.rp)
            g.send(self.own.at[rows], self.buf.at[g.z, g.y, rows], self.sem(0), self.sem(1), there)

    def along_y(self):
        g = self.ring
        await_bytes(self.buf.at[pl.ds(0, 3), 0, pl.ds(0, self.q)], self.sem(1))
        part = self.buf.at[:, g.y, self.rows(g.core)]
        g.send(part, part, self.sem(2), self.sem(3), g.beside())

    def between(self):
        g = self.ring
        await_bytes(self.buf.at[:, 0, pl.ds(0, self.q)], self.sem(3))
        part = self.buf.at[:, :, self.rows(g.core)]
        g.send(part, part, self.sem(4), self.sem(5), g.sibling())

    def last(self):
        one = self.buf.at[:, :, pl.ds(0, self.q)]
        await_bytes(one, self.sem(5))
        await_bytes(one, self.sem(4))
        await_bytes(self.buf.at[pl.ds(0, 3), 0, pl.ds(0, self.q)], self.sem(0))
        await_bytes(self.buf.at[:, 0, pl.ds(0, self.q)], self.sem(2))


class ScatterHalf:
    def __init__(self, ring, buf, scratch, sems, base):
        self.ring, self.buf, self.sems, self.base = ring, buf, sems, base
        self.one, self.three, self.four, self.part, self.two, self.done = scratch
        self.q = buf.shape[2] // 2

    def sem(self, i):
        return self.sems.at[self.base + i]

    def rows(self, index):
        return pl.ds(pl.multiple_of(index * self.q, 16), self.q)

    def between(self):
        g = self.ring
        g.send(self.buf.at[:, :, self.rows(1 - g.core)], self.one, self.sem(0), self.sem(1), g.sibling())

    def add(self, zi, yi, other):
        at = self.rows(self.ring.core)
        self.buf[zi, yi, at] = (self.buf[zi, yi, at].astype(F32) + other.astype(F32)).astype(BF)

    def along_y(self):
        g = self.ring
        await_bytes(self.one, self.sem(1))

        def body(s, c):
            zi, yi = lax.div(s, 2), lax.rem(s, 2)
            self.add(zi, yi, self.one[zi, yi])
            return c

        lax.fori_loop(0, 8, body, 0)
        there = self.buf.at[:, 1 - g.y, self.rows(g.core)]
        g.send(there, self.three, self.sem(2), self.sem(3), g.beside())

    def along_z(self):
        g = self.ring
        await_bytes(self.three, self.sem(3))
        at = self.rows(g.core)
        for k in range(4):
            self.add(k, g.y, self.three[k])
        for d in range(1, 4):
            zz = lax.rem(g.z + d, 4)
            g.send(self.buf.at[zz, g.y, at], self.four.at[g.z], self.sem(4), self.sem(5), (2 * zz + g.y, g.rp))
        self.four[g.z] = self.buf[g.z, g.y, at]

    def along_x(self):
        g = self.ring
        await_bytes(self.four.at[pl.ds(0, 3)], self.sem(5))
        total = self.four[0].astype(F32)
        for k in range(1, 4):
            total = total + self.four[k].astype(F32)
        self.part[...] = total.astype(BF)
        g.send(self.part, self.two, self.sem(6), self.sem(7), g.across())

    def back(self):
        g = self.ring
        await_bytes(self.two, self.sem(7))
        self.done[g.core] = (self.part[...].astype(F32) + self.two[...].astype(F32)).astype(BF)
        mine = self.done.at[g.core]
        g.send(mine, mine, self.sem(8), self.sem(9), g.sibling())

    def last(self):
        half = self.done.at[0]
        await_bytes(half, self.sem(9))
        await_bytes(self.one, self.sem(0))
        await_bytes(self.three, self.sem(2))
        await_bytes(self.four.at[pl.ds(0, 3)], self.sem(4))
        await_bytes(self.part, self.sem(6))
        await_bytes(half, self.sem(8))


AR_ROWS = (4, 6, 2, 6, 2, 6, 6, 4)
CHUNKS = (448, 576, 256, 128)
STARTS = (0, 448, 1024, 1280)


def mask_tile(row):
    at0 = lax.broadcasted_iota(jnp.int32, (SIDE, SIDE), 0)
    at1 = lax.broadcasted_iota(jnp.int32, (SIDE, SIDE), 1)
    diag = jnp.where(at0 == at1, jnp.broadcast_to(row, (SIDE, SIDE)), 0.0)
    return dot(diag.astype(BF), jnp.ones((SIDE, 128), BF))


def shifted(x, edge, by):
    moved = pltpu.roll(x, by % x.shape[0], axis=0)
    at = lax.rem(lax.broadcasted_iota(jnp.int32, x.shape, 0), SIDE)
    return jnp.where(at == edge, 0.0, moved)


def gl_runs(shards):
    runs = []
    share = 9 * GLO // shards
    row = 0
    while row < 9 * GLO:
        n = min(GLO - row % GLO, share - row % share)
        runs.append((row // GLO, row % GLO, row // share, row % share, n))
        row += n
    return runs


def col(row):
    return jnp.broadcast_to(row, (128, 128)).T


def two(x):
    return jnp.concatenate([x, x], axis=1)


def to_row(x):
    n = x.shape[0]
    if n < 128:
        x = jnp.concatenate([x, jnp.zeros((128 - n, 128), F32)], axis=0)
    return jnp.sum(x.T, axis=0, keepdims=True)


def moments(total, square, n):
    mean = total / n
    scale = lax.rsqrt(square / n - mean * mean + EPS)
    return scale, mean * scale


def kernel(dps, reps, fused, *refs):
    it = iter(refs)

    def take(n):
        return [next(it) for _ in range(n)]

    feat_h, cot_h, holes, tab_h = take(4)
    if fused:
        w_ll, w_gl, w_lg, w_in, w_fu, w_out, gain_in, bias_in = take(8)
    else:
        WCAT, WGLN, WINT, WFU, WFUT, WOUT, GBI = take(7)
    block_out, field_out, norm_out = take(3)
    if fused:
        (flat_out,) = take(1)
    else:
        out_ll, out_gl, out_lg, out_in, out_fu, out_out = take(6)
    F, WF, Z3, D3, PX, DY, PS, ST, PF, Y, J, DC, A, COT = take(14)
    EXA, EXB, DYX, ACC, ACF, COLS, COLF, ROWP, GBR, GOUT, WGL = take(11)
    ARB = take(8)
    ar_s, ar_r, io_sem = take(3)
    if fused:
        WCAT, WINT, WFU, WFUT, WOUT, WI, GBB, OWNI, g_sem, rs_sem = take(10)
        OWN, WB, RS = take(3), take(4), [take(n) for n in (6, 5, 5, 5)]
    ring = Ring(dps, reps)
    D, R, N = ring.D, ring.R, ring.N
    me, dp, rp = ring.me, ring.dp, ring.rp
    count = float(POS * N)
    fcount = float(FREQ * N)

    copy_l = pltpu.make_async_copy(feat_h.at[:, :, 0:LOC], Z3.at[1:65, :, 128:256], io_sem.at[0])
    copy_l.start()
    copy_f = pltpu.make_async_copy(feat_h.at[:, :, LOC:ALL], F.at[1:65], io_sem.at[1])
    copy_f.start()
    copy_a = pltpu.make_async_copy(tab_h, A, io_sem.at[2])
    copy_a.start()
    copy_c = pltpu.make_async_copy(cot_h, COT, io_sem.at[3])
    copy_c.start()

    def put(src, dst):
        copy = pltpu.make_async_copy(src, dst, io_sem.at[7])
        copy.start()
        copy.wait()

    def ar_start(k):
        def body(d, c):
            peer = lax.rem(me + d, N)
            ring.send(ARB[k].at[me], ARB[k].at[me], ar_s.at[k], ar_r.at[k], ring.dev(peer))
            return c

        lax.fori_loop(1, N, body, 0)

    def ar_wait(k):
        await_bytes(ARB[k].at[pl.ds(0, N - 1)], ar_r.at[k])
        await_bytes(ARB[k].at[pl.ds(0, N - 1)], ar_s.at[k])
        return jnp.sum(ARB[k][...], axis=0)

    def put_rows(k, at, rows):
        for i, row in enumerate(rows):
            ARB[k][me, at + i : at + i + 1, :] = row

    if fused:
        O1, O2, OF = OWN
        half = pl.ds(pl.multiple_of(48 * ring.core, 16), 48)
        OWNI[0:48, :] = w_in[:, 0:128]
        OWNI[48:96, :] = jnp.concatenate([w_in[:, 128:192], jnp.zeros((48, 64), BF)], axis=1)
        own = gain_in.shape[1]
        for kind, ref in ((0, gain_in), (1, bias_in)):
            row = jnp.concatenate([ref[...].astype(F32), jnp.zeros((1, 256 - own), F32)], axis=1)
            for j in range(2):
                GBB[dp, 2 * kind + j : 2 * kind + j + 1, :] = row[:, 128 * j : 128 * j + 128]
        WI[dp, half] = OWNI[half]
        for j in range(3):
            OF[48 * j : 48 * j + 48, :] = w_fu[:, 128 * j : 128 * j + 128]
            part = w_out[:, 128 * j : 128 * j + 128].astype(F32)
            part = jnp.concatenate([part, jnp.zeros((8, 128), F32)], axis=0)
            OF[144 + 32 * j : 176 + 32 * j, :] = part.astype(BF)
            O2[144 + 144 * j : 288 + 144 * j, :] = w_lg[:, 128 * j : 128 * j + 128]
        OF[240:256, :] = jnp.zeros((16, 128), BF)
        O2[0:144, :] = w_ll[...]
        O1[0:432, :] = w_gl[...]
        O1[432:448, :] = jnp.zeros((16, 128), BF)
        W1, W2, WFO, GI = WB
        gather_1 = GatherHalf(ring, O1, W1, g_sem, 6)
        gather_2 = Gather(ring, O2, W2, g_sem, 12)
        gather_f = Gather(ring, OF, WFO, g_sem, 22)
        for g in (gather_f, gather_2, gather_1):
            g.place()

    ring.barrier()

    def spread(src, dst, ss, rs):
        def body(d, c):
            ring.send(src, dst, ss, rs, (lax.rem(dp + d, D), rp))
            return c

        lax.fori_loop(1, D, body, 0)

    if fused:
        spread(OWNI.at[half], WI.at[dp, half], g_sem.at[0], g_sem.at[1])
        spread(GBB.at[dp], GBB.at[dp], g_sem.at[4], g_sem.at[5])

    edge_row = jnp.zeros((SIDE, 384), BF)
    for ref in (F, Z3, D3):
        ref[0] = edge_row
        ref[65] = edge_row
    DC[0] = jnp.zeros((SIDE, ALL), BF)
    DC[65] = jnp.zeros((SIDE, ALL), BF)

    def make_wf(i, c):
        for e in range(4):
            WF[4 * i + e] = mask_tile(0.25 + holes[pl.ds(4 * i + e, 1), :].astype(F32)).astype(BF)
        return c

    lax.fori_loop(0, 16, make_wf, 0)
    if fused:
        gather_f.along_z()
        gather_2.along_z()
    copy_l.wait()

    def make_z3(i, c):
        for e in range(2):
            h = 2 * i + e + 1
            x = Z3[h, :, 128:256].astype(F32)
            Z3[h, :, 0:128] = shifted(x, 0, 1).astype(BF)
            Z3[h, :, 256:384] = shifted(x, 63, -1).astype(BF)
        return c

    lax.fori_loop(0, 32, make_z3, 0)
    copy_f.wait()

    if fused:
        await_bytes(WI.at[pl.ds(0, D - 1), pl.ds(0, 48)], g_sem.at[1])
        part = WI.at[:, half]
        ring.send(part, part, g_sem.at[2], g_sem.at[3], ring.sibling())
        await_bytes(part, g_sem.at[3])
        first = jnp.concatenate([WI[s, 0:48] for s in range(D)], axis=0).astype(F32)
        WINT[0:128, :] = first.T.astype(BF)
        first = jnp.concatenate([WI[s, 48:96] for s in range(D)], axis=0).astype(F32)
        WINT[128:192, :] = (first.T)[0:64].astype(BF)

    def tile(ref, h0, lo, hi):
        return jnp.concatenate([ref[h0 + 16 * j + 1, :, lo:hi] for j in range(4)], axis=0)

    def rows_of(h0):
        return pl.ds(pl.multiple_of(h0 * HALF, 8), HALF)

    ACC[...] = jnp.zeros_like(ACC)

    def input_proj(i, c):
        w = WINT[...]
        res = [dot(w, tile(F, 4 * i + e, 0, GLO), 1, 1) for e in range(4)]
        for e in range(4):
            PS[4 * i + e] = res[e]
        ACC[0:HALF] += sum(lane_pair(ps) for ps in res)
        ACC[HALF : 2 * HALF] += sum(lane_pair(ps * ps) for ps in res)
        return c

    lax.fori_loop(0, 4, input_proj, 0)

    def spec_rows():
        return [to_row(ACC[0:128]), to_row(ACC[128:192]), to_row(ACC[192:320]), to_row(ACC[320:384])]

    put_rows(0, 0, spec_rows())
    ar_start(0)

    if fused:
        gather_f.along_y()
        gather_2.along_y()
        await_bytes(GBB.at[pl.ds(0, D - 1)], g_sem.at[5])
        wide = []
        for kind in range(2):
            parts = []
            for s in range(D):
                parts.append(GBB[s, 2 * kind : 2 * kind + 1, :])
                parts.append(GBB[s, 2 * kind + 1 : 2 * kind + 2, 0 : own - 128])
            row = jnp.concatenate(parts + [jnp.ones((1, 1152 - own * D), F32)], axis=1)
            wide.append(jnp.broadcast_to(row, (8, 1152)))
    else:
        wide = []
        for kind in range(2):
            row = jnp.concatenate([GBI[9 * kind + j : 9 * kind + j + 1, :] for j in range(9)], axis=1)
            wide.append(jnp.broadcast_to(row, (8, 1152)))

    def piece(kind, offset, width):
        return pltpu.roll(wide[kind], (1152 - offset) % 1152, axis=1)[0:1, 0:width]

    for kind in range(2):
        at = 2 + kind
        spec = piece(kind, 0, 256)
        freq = piece(kind, HALF, 384)
        glo = piece(kind, HALF + GLO + LOC, 384)
        COLS[at, 0:128] = col(spec[:, 0:128])
        COLS[at, 128:192] = col(spec[:, 128:256])[0:64]
        for j in range(2):
            GBR[kind, j : j + 1, :] = spec[:, 128 * j : 128 * j + 128]
        for j in range(3):
            COLF[at, 128 * j : 128 * j + 128] = col(freq[:, 128 * j : 128 * j + 128])
            GBR[kind, 2 + j : 3 + j, :] = freq[:, 128 * j : 128 * j + 128]
            GBR[kind, 6 + j : 7 + j, :] = glo[:, 128 * j : 128 * j + 128]
        loc = piece(kind, HALF + GLO, 128)
        GBR[kind, 5:6, :] = loc
        ROWP[at : at + 1, 0:128] = loc
        ROWP[at : at + 1, 128:512] = glo

    def fold(ref):
        ref[4] = ref[0] * ref[2]
        ref[5] = ref[3] - ref[1] * ref[2]

    if fused:
        gather_f.along_x()
        gather_2.along_x()
        gather_1.along_z()

    copy_a.wait()
    tot = ar_wait(0)
    for r, (lo, n) in enumerate(((0, 128), (128, 64))):
        scale, ms = moments(tot[r : r + 1], tot[r + 2 : r + 3], count)
        COLS[0, lo : lo + n] = col(scale)[0:n]
        COLS[1, lo : lo + n] = col(ms)[0:n]
    fold(COLS)

    EXA[...] = jnp.zeros_like(EXA)

    def spec_front(i, c):
        gain, bias = two(COLS[4]), two(COLS[5])
        ext = None
        for e in range(4):
            h0 = 4 * i + e
            sp = gelu_value(PS[h0] * gain + bias)
            DY[rows_of(h0), 0:256] = sp
            res = dot(sp.astype(BF), A[h0])
            DY[rows_of(h0), 256:512] = res[:, 0:256]
            ext = res[:, 256:384] if ext is None else ext + res[:, 256:384]
        EXA[...] += ext
        return c

    lax.fori_loop(0, 4, spec_front, 0)
    if fused:
        gather_f.between()
    low_half = lax.broadcasted_iota(jnp.int32, (HALF, 128), 1) < 64

    def split_ext(x):
        re = jnp.where(low_half, x, 0.0)
        im = jnp.where(low_half, pltpu.roll(x, 64, axis=1), 0.0)
        return re, im

    def join_ext(re, im):
        return jnp.where(low_half, re, pltpu.roll(im, 64, axis=1))

    ext_re, ext_im = split_ext(EXA[...])
    ST[16, 0:HALF] = ext_re.astype(BF)
    ST[16, HALF : 2 * HALF] = ext_im.astype(BF)

    def grab(ref, g, base):
        z = []
        for a in range(16):
            rows = pl.ds(pl.multiple_of(a * HALF + g * 8, 8), 8)
            z.append((ref[rows, base : base + 128], ref[rows, base + 128 : base + 256]))
        return z

    def fwd_fft(i, c):
        halves = [dft16(grab(DY, 2 * i + s, 256), -1) for s in range(2)]
        for k in range(16):
            for comp in range(2):
                both = jnp.concatenate([halves[0][k][comp], halves[1][k][comp]], axis=0)
                ST[k, pl.ds(pl.multiple_of(comp * HALF + i * 16, 16), 16)] = both.astype(BF)
        return c

    lax.fori_loop(0, 12, fwd_fft, 0)

    if fused:
        gather_f.last()
        for j in range(3):
            parts = [WFO[s // 2, s % 2, 48 * j : 48 * j + 48] for s in range(D)]
            fu = jnp.concatenate(parts, axis=0)
            WFU[:, 128 * j : 128 * j + 128] = fu
            WFUT[128 * j : 128 * j + 128, :] = fu.astype(F32).T.astype(BF)
            parts = [WFO[s // 2, s % 2, 144 + 32 * j : 176 + 32 * j].astype(F32)[0:24] for s in range(D)]
            WOUT[:, 128 * j : 128 * j + 128] = jnp.concatenate(parts, axis=0).astype(BF)

    def unit(ts):
        w = WFUT[...]
        s0 = s1 = None
        for t in ts:
            pf = dot(w, jnp.concatenate([ST[2 * t], ST[2 * t + 1]], axis=1))
            PF[2 * t] = pf[:, 0:128]
            PF[2 * t + 1] = pf[:, 128:256]
            s0 = lane_pair(pf) if s0 is None else s0 + lane_pair(pf)
            s1 = lane_pair(pf * pf) if s1 is None else s1 + lane_pair(pf * pf)
        return s0, s1

    pf = dot(WFUT[...], ST[16])
    PF[16] = pf
    ACF[0:384] = pf
    ACF[384:768] = pf * pf

    def unit_step(i, c):
        s0, s1 = unit([4 * i + e for e in range(4)])
        ACF[0:384] += s0
        ACF[384:768] += s1
        return c

    lax.fori_loop(0, 2, unit_step, 0)

    def freq_rows():
        return [to_row(ACF[128 * j : 128 * j + 128]) for j in range(6)]

    put_rows(1, 0, freq_rows())
    ar_start(1)

    if fused:
        gather_1.along_y()
        gather_2.between()
        gather_2.last()
        for s in range(D):
            for j in range(4):
                WCAT[144 * s : 144 * s + 144, 128 * j : 128 * j + 128] = W2[s // 2, s % 2, 144 * j : 144 * j + 144]

    def slab(ref, i, off, lo, hi, n=8):
        return ref[pl.ds(n * i + off, n), :, lo:hi].reshape(n * SIDE, hi - lo)

    def block_rows(i):
        return pl.ds(pl.multiple_of(512 * i, 512), 512)

    def conv_loc(i, c):
        lhs = jnp.concatenate([slab(Z3, i, a, 0, 384) for a in range(3)], axis=1)
        PX[block_rows(i), :] = dot(lhs, WCAT[...])
        return c

    lax.fori_loop(0, 8, conv_loc, 0)
    if fused:
        gather_1.between()

    tot = ar_wait(1)
    for j in range(3):
        scale, ms = moments(tot[j : j + 1], tot[j + 3 : j + 4], fcount)
        COLF[0, 128 * j : 128 * j + 128] = col(scale)
        COLF[1, 128 * j : 128 * j + 128] = col(ms)
    fold(COLF)
    lane = lax.broadcasted_iota(jnp.int32, (8, 128), 1)
    doubled = jnp.where(lax.rem(lane, 32) == 0, 1.0, 2.0).astype(F32)

    def freq_act(v, rows):
        return v * COLF[4, rows] + COLF[5, rows]

    def inv_fft(i, c):
        halves = []
        for s in range(2):
            z = []
            rr = pl.ds(pl.multiple_of(16 * i + 8 * s, 8), 8)
            ri = pl.ds(pl.multiple_of(HALF + 16 * i + 8 * s, 8), 8)
            for k in range(16):
                re = gelu_value(freq_act(PF[k, rr], rr)) * doubled
                im = gelu_value(freq_act(PF[k, ri], ri)) * doubled
                z.append((re, im))
            halves.append(dft16(z, 1))
        for a in range(16):
            for comp in range(2):
                both = jnp.concatenate([halves[0][a][comp], halves[1][a][comp]], axis=0)
                Y[a, pl.ds(pl.multiple_of(i * 16, 16), 16), 128 * comp : 128 * comp + 128] = both.astype(BF)
        return c

    lax.fori_loop(0, 12, inv_fft, 0)
    mixed = gelu_value(PF[16] * COLF[4] + COLF[5])
    EXB[...] = join_ext(mixed[0:HALF], mixed[HALF : 2 * HALF]).astype(BF)
    ROWP[8:24, :] = jnp.zeros((16, ALL), F32)

    def slab_rows(h0, j):
        return pl.ds(pl.multiple_of((h0 + 16 * j) * SIDE, SIDE), SIDE)

    def join(i, c):
        ext, w = EXB[...], WOUT[...]
        s0 = s1 = None
        for e in range(4):
            h0 = 4 * i + e
            back = dot(jnp.concatenate([Y[h0], ext], axis=1), A[h0], 1, 1)
            joined = (DY[rows_of(h0), 0:256] + back).astype(BF)
            J[h0] = joined
            pg = dot(joined, w, 0, 0)
            for j in range(4):
                v = PX[slab_rows(h0, j), 128:512] + pg[64 * j : 64 * j + 64]
                PX[slab_rows(h0, j), 128:512] = v
                s0 = rows8(v) if s0 is None else s0 + rows8(v)
                s1 = rows8(v * v) if s1 is None else s1 + rows8(v * v)
        ROWP[8:16, 128:512] += s0
        ROWP[16:24, 128:512] += s1
        return c

    lax.fori_loop(0, 4, join, 0)

    def put_norm_rows(k, lo, tiles):
        for j in range(tiles):
            at = lo + 128 * j
            put_rows(k, j, [jnp.sum(ROWP[8:16, at : at + 128], axis=0, keepdims=True)])
            put_rows(k, tiles + j, [jnp.sum(ROWP[16:24, at : at + 128], axis=0, keepdims=True)])

    put_norm_rows(3, 128, 3)
    ar_start(3)

    if fused:
        gather_1.last()
        for tap, c0, s, r0, n in gl_runs(D):
            WGL[tap // 3, c0 : c0 + n, 128 * (tap % 3) : 128 * (tap % 3) + 128] = W1[s // 2, s % 2, r0 : r0 + n]
    else:
        for tap in range(9):
            WGL[tap // 3, 0:384, 128 * (tap % 3) : 128 * (tap % 3) + 128] = WGLN[384 * tap : 384 * tap + 384]
    for tap in range(9):
        WGL[tap // 3, 384:512, 128 * (tap % 3) : 128 * (tap % 3) + 128] = WCAT[128 * tap : 128 * tap + 128, 0:128]

    def conv_glo(i, c):
        lhs = jnp.concatenate([slab(F, i, a, 0, 384) for a in range(3)], axis=1)
        gl = dot(lhs, jnp.concatenate([WGL[a, 0:384] for a in range(3)], axis=0))
        total = PX[block_rows(i), 0:128] + gl[:, 128:256] + shifted(gl[:, 0:128], 0, 1) + shifted(gl[:, 256:384], 63, -1)
        PX[block_rows(i), 0:128] = total
        ROWP[8:16, 0:128] += rows8(total)
        ROWP[16:24, 0:128] += rows8(total * total)
        return c

    lax.fori_loop(0, 8, conv_glo, 0)
    put_norm_rows(2, 0, 1)
    ar_start(2)

    def set_norm(tot, lo, tiles):
        for j in range(tiles):
            ls = slice(lo + 128 * j, lo + 128 * j + 128)
            scale, ms = moments(tot[j : j + 1], tot[tiles + j : tiles + j + 1], count)
            ROWP[0:1, ls] = scale
            ROWP[1:2, ls] = ms
            ROWP[4:5, ls] = scale * ROWP[2:3, ls]
            ROWP[5:6, ls] = ROWP[3:4, ls] - ms * ROWP[2:3, ls]

    def out_norm(lo, hi, sem):
        ROWP[8:24, lo:hi] = jnp.zeros((16, hi - lo), F32)

        def chunk(i, c):
            def one(hh, c2):
                h = 16 * i + hh
                for l0 in range(lo, hi, 128):
                    ls = slice(l0, l0 + 128)
                    s0 = s1 = None
                    for r in (0, 32):
                        at = pl.ds(pl.multiple_of(h * SIDE + r, 32), 32)
                        y = PX[at, ls] * ROWP[4:5, ls] + ROWP[5:6, ls]
                        value, slope = gelu_both(y)
                        dy = slope * (COT[h, r : r + 32, ls].astype(F32) * WF[h, r : r + 32].astype(F32))
                        DY[at, ls] = dy
                        if l0 == 0:
                            base = Z3[h + 1, r : r + 32, 128:256]
                        else:
                            base = F[h + 1, r : r + 32, l0 - 128 : l0]
                        DC[h + 1, r : r + 32, ls] = (base.astype(F32) + value).astype(BF)
                        s0 = rows8(dy) if s0 is None else s0 + rows8(dy)
                        s1 = rows8(dy * y) if s1 is None else s1 + rows8(dy * y)
                    ROWP[8:16, ls] += s0
                    ROWP[16:24, ls] += s1
                return c2

            lax.fori_loop(0, 16, one, 0)
            pltpu.make_async_copy(
                DC.at[pl.ds(16 * i + 1, 16), :, lo:hi], block_out.at[pl.ds(16 * i, 16), :, lo:hi], sem
            ).start()
            return c

        lax.fori_loop(0, 4, chunk, 0)

    copy_c.wait()
    set_norm(ar_wait(3), 128, 3)
    out_norm(128, 512, io_sem.at[4])
    put_norm_rows(5, 128, 3)
    ar_start(5)
    set_norm(ar_wait(2), 0, 1)
    out_norm(0, 128, io_sem.at[5])
    put_norm_rows(4, 0, 1)
    ar_start(4)

    def back_sums(tot, tiles, at):
        out = []
        for j in range(tiles):
            s1 = tot[j : j + 1]
            s2 = (tot[tiles + j : tiles + j + 1] - GBR[1, at + j : at + j + 1, :] * s1) / GBR[0, at + j : at + j + 1, :]
            norm_out[at + j : at + j + 1, :] = s2
            norm_out[16 + at + j : 17 + at + j, :] = s1
            out.append((s1, s2))
        return out

    norm_out[9:16, :] = jnp.zeros((7, 128), F32)
    norm_out[25:32, :] = jnp.zeros((7, 128), F32)

    def set_back(tot, lo, tiles, at):
        for j, (s1, s2) in enumerate(back_sums(tot, tiles, at)):
            ls = slice(lo + 128 * j, lo + 128 * j + 128)
            ROWP[6:7, ls] = ROWP[4:5, ls] * ROWP[0:1, ls] * (s2 / count)
            ROWP[7:8, ls] = ROWP[4:5, ls] * (ROWP[1:2, ls] * (s2 / count) - s1 / count)

    def norm_back(lo, hi, sem):
        pltpu.make_async_copy(DC.at[1:65, :, lo:hi], block_out.at[:, :, lo:hi], sem).wait()

        def one(h, c):
            for l0 in range(lo, hi, 128):
                ls = slice(l0, l0 + 128)
                for r in (0, 32):
                    at = pl.ds(pl.multiple_of(h * SIDE + r, 32), 32)
                    d = ROWP[4:5, ls] * DY[at, ls] - ROWP[6:7, ls] * PX[at, ls] + ROWP[7:8, ls]
                    DC[h + 1, r : r + 32, ls] = d.astype(BF)
            return c

        lax.fori_loop(0, SIDE, one, 0)

    set_back(ar_wait(5), 128, 3, 6)
    norm_back(128, 512, io_sem.at[4])

    EXA[...] = jnp.zeros_like(EXA)
    GOUT[...] = jnp.zeros_like(GOUT)

    def join_back(i, c):
        w = WOUT[...]
        dgs = []
        ext = None
        for e in range(4):
            h0 = 4 * i + e
            dg = tile(DC, h0, 128, 512)
            dgs.append(dg)
            dj = dot(w, dg, 1, 1)
            PX[rows_of(h0), 0:256] = dj
            res = dot(dj.astype(BF), A[h0])
            PX[rows_of(h0), 256:512] = res[:, 0:256]
            ext = res[:, 256:384] if ext is None else ext + res[:, 256:384]
        EXA[...] += ext
        lhs = jnp.concatenate([J[4 * i + e] for e in range(4)], axis=1)
        GOUT[...] += dot(lhs, jnp.concatenate(dgs, axis=0))
        return c

    set_back(ar_wait(4), 0, 1, 5)
    norm_back(0, 128, io_sem.at[5])
    lax.fori_loop(0, 4, join_back, 0)

    def freq_back(g, c):
        z = dft16(grab(PX, g, 256), -1)
        for comp in range(2):
            rows = pl.ds(pl.multiple_of(comp * HALF + 8 * g, 8), 8)
            s0 = s1 = None
            for k in range(16):
                y = freq_act(PF[k, rows], rows)
                dy = gelu_slope(y) * (z[k][comp] * doubled)
                r0, l0 = dyf_pos(k)
                DY[pl.ds(pl.multiple_of(r0 + comp * HALF + 8 * g, 8), 8), l0 : l0 + 128] = dy
                s0 = dy if s0 is None else s0 + dy
                s1 = dy * y if s1 is None else s1 + dy * y
            ACF[rows] = s0
            ACF[pl.ds(pl.multiple_of(384 + comp * HALF + 8 * g, 8), 8)] = s1
        return c

    lax.fori_loop(0, 24, freq_back, 0)
    ext_re, ext_im = split_ext(EXA[...])
    y = PF[16] * COLF[4] + COLF[5]
    dy = gelu_slope(y) * jnp.concatenate([ext_re, ext_im], axis=0)
    DYX[...] = dy
    ACF[0:384] += dy
    ACF[384:768] += dy * y
    put_rows(6, 0, freq_rows())
    ar_start(6)

    def make_d3(i, c):
        for e in range(2):
            h = 2 * i + e + 1
            x = DC[h, :, 0:128]
            D3[h, :, 0:128] = shifted(x.astype(F32), 63, -1).astype(BF)
            D3[h, :, 128:256] = x
            D3[h, :, 256:384] = shifted(x.astype(F32), 0, 1).astype(BF)
        return c

    lax.fori_loop(0, 32, make_d3, 0)

    def wgrad_glo(i, first):
        zt = slab(F, i, 1, 0, 384, 16).T
        res = dot(zt, jnp.concatenate([slab(D3, i, 2 - a, 0, 384, 16) for a in range(3)], axis=1))
        for tap in range(9):
            r = 384 * tap
            part = res[:, 128 * tap : 128 * tap + 128]
            DY[r : r + 384, 0:128] = part if first else DY[r : r + 384, 0:128] + part

    def wgrad_loc(i, first):
        zt = slab(Z3, i, 1, 0, 384, 16).T
        for a in range(3):
            res = dot(zt, slab(DC, i, 2 - a, 0, 512, 16))
            r = 384 * a
            if first:
                DY[1152 + r : 1536 + r, 128:256] = res[:, 0:128]
                DY[r : r + 384, 128:512] = res[:, 128:512]
            else:
                DY[1152 + r : 1536 + r, 128:256] += res[:, 0:128]
                DY[r : r + 384, 128:512] += res[:, 128:512]

    def rest(f, after_first=None):
        def body(i, c):
            f(i, False)
            return c

        f(0, True)
        if after_first is not None:
            after_first()
        lax.fori_loop(1, 4, body, 0)

    rest(wgrad_glo)
    if fused:
        for tap, c0, s, r0, n in gl_runs(D):
            r = 384 * tap + c0
            W1[s // 2, s % 2, r0 : r0 + n] = DY[r : r + n, 0:128].astype(BF)
        for s in range(D):
            W1[s // 2, s % 2, 432:448] = jnp.zeros((16, 128), BF)
        scatter_1 = ScatterHalf(ring, W1, RS[0], rs_sem, 0)
        scatter_2 = Scatter(ring, W2, RS[1], rs_sem, 10)
        scatter_f = Scatter(ring, WFO, RS[2], rs_sem, 20)
        scatter_i = Scatter(ring, GI, RS[3], rs_sem, 30)
        scatter_1.between()
    rest(wgrad_loc, scatter_1.along_y if fused else None)
    if fused:
        for s in range(D):
            W2[s // 2, s % 2, 0:144] = DY[1152 + 144 * s : 1296 + 144 * s, 128:256].astype(BF)
            for j in range(3):
                ls = slice(128 + 128 * j, 256 + 128 * j)
                W2[s // 2, s % 2, 144 + 144 * j : 288 + 144 * j] = DY[144 * s : 144 * s + 144, ls].astype(BF)
        scatter_2.between()
    else:
        put(DY.at[0:3456, 0:128], out_gl)
        put(DY.at[1152:2304, 128:256], out_ll)
        put(DY.at[0:1152, 128:512], out_lg)

    tot = ar_wait(6)
    for j, (s1, s2) in enumerate(back_sums(tot, 3, 2)):
        at = slice(128 * j, 128 * j + 128)
        COLF[6, at] = COLF[4, at] * COLF[0, at] * col(s2 / fcount)
        COLF[7, at] = COLF[4, at] * (COLF[1, at] * col(s2 / fcount) - col(s1 / fcount))

    def gfu_at(j, lo=0, n=384):
        return (slice(384 * (j // 2) + lo, 384 * (j // 2) + lo + n), slice(256 + 128 * (j % 2), 384 + 128 * (j % 2)))

    def dpf_tile(k, dy):
        return (COLF[4] * dy - COLF[6] * PF[k] + COLF[7]).astype(BF)

    dpf = dpf_tile(16, DYX[...])
    res = dot(ST[16], dpf, 1, 1)
    for j in range(3):
        PX[gfu_at(j)] = res[:, 128 * j : 128 * j + 128]
    ds = dot(WFU[...], dpf)
    EXB[...] = join_ext(ds[0:HALF], ds[HALF : 2 * HALF]).astype(BF)
    for t in range(4):
        spots = [dyf_pos(4 * t + e) for e in range(4)]
        parts = [dpf_tile(4 * t + e, DY[r : r + 384, l : l + 128]) for e, (r, l) in enumerate(spots)]
        dpf = jnp.concatenate(parts, axis=1)
        res = dot(jnp.concatenate([ST[4 * t + e] for e in range(4)], axis=1), dpf, 1, 1)
        for j in range(3):
            PX[gfu_at(j)] += res[:, 128 * j : 128 * j + 128]
        ds = dot(WFU[...], dpf)
        for e, (r, l) in enumerate(spots):
            DY[r : r + 384, l : l + 128] = ds[:, 128 * e : 128 * e + 128]
        if fused and t == 1:
            scatter_1.along_z()
            scatter_2.along_x()
    if fused:
        for s in range(D):
            for j in range(3):
                ls = slice(128 * j, 128 * j + 128)
                WFO[s // 2, s % 2, 48 * j : 48 * j + 48] = PX[gfu_at(j, 48 * s, 48)].astype(BF)
                part = jnp.concatenate([GOUT[24 * s : 24 * s + 24, ls], jnp.zeros((8, 128), F32)], axis=0)
                WFO[s // 2, s % 2, 144 + 32 * j : 176 + 32 * j] = part.astype(BF)
            WFO[s // 2, s % 2, 240:256] = jnp.zeros((16, 128), BF)
        scatter_f.between()
    else:
        for j in range(3):
            put(PX.at[gfu_at(j)], out_fu.at[:, 128 * j : 128 * j + 128])
        put(GOUT, out_out)

    def adj_fft(i, c):
        halves = []
        for s in range(2):
            z = []
            for k in range(16):
                r0, l0 = dyf_pos(k)
                pair = []
                for comp in range(2):
                    at = pl.ds(pl.multiple_of(r0 + comp * HALF + 16 * i + 8 * s, 8), 8)
                    pair.append(DY[at, l0 : l0 + 128])
                z.append(tuple(pair))
            halves.append(dft16(z, 1))
        for a in range(16):
            for comp in range(2):
                both = jnp.concatenate([halves[0][a][comp], halves[1][a][comp]], axis=0)
                Y[a, pl.ds(pl.multiple_of(i * 16, 16), 16), 128 * comp : 128 * comp + 128] = both.astype(BF)
        return c

    lax.fori_loop(0, 12, adj_fft, 0)
    ACC[...] = jnp.zeros_like(ACC)

    def spec_back(i, c):
        gain, bias, ext = two(COLS[4]), two(COLS[5]), EXB[...]
        s0 = s1 = None
        for e in range(4):
            h0 = 4 * i + e
            back = dot(jnp.concatenate([Y[h0], ext], axis=1), A[h0], 1, 1)
            y = PS[h0] * gain + bias
            dy = gelu_slope(y) * (PX[rows_of(h0), 0:256] + back)
            DY[rows_of(h0), 256:512] = dy
            s0 = lane_pair(dy) if s0 is None else s0 + lane_pair(dy)
            s1 = lane_pair(dy * y) if s1 is None else s1 + lane_pair(dy * y)
        ACC[0:HALF] += s0
        ACC[HALF : 2 * HALF] += s1
        return c

    lax.fori_loop(0, 4, spec_back, 0)
    put_rows(7, 0, spec_rows())
    ar_start(7)
    if fused:
        scatter_f.along_x()

    def dgrad(i, c):
        lhs = jnp.concatenate([slab(DC, i, 2 - a, 128, 512) for a in range(3)], axis=1)
        rhs = jnp.concatenate([WCAT[384 * a : 384 * a + 384, 128:512] for a in range(3)], axis=1)
        res = dot(lhs, rhs, 1, 1)
        lhs = jnp.concatenate([slab(D3, i, 2 - a, 0, 384) for a in range(3)], axis=1)
        both = dot(lhs, jnp.concatenate([WGL[a] for a in range(3)], axis=1), 1, 1)
        PX[block_rows(i), 128:512] = both[:, 0:384]
        loc = both[:, 384:512] + res[:, 128:256] + shifted(res[:, 0:128], 63, -1) + shifted(res[:, 256:384], 0, 1)
        loc = loc.reshape(8, SIDE, 128)
        at = pl.ds(8 * i, 8)
        COT[at, :, 0:128] = (loc + COT[at, :, 0:128].astype(F32) * WF[at].astype(F32)).astype(BF)
        return c

    lax.fori_loop(0, 2, dgrad, 0)
    if fused:
        scatter_1.along_x()
    lax.fori_loop(2, 4, dgrad, 0)
    if fused:
        scatter_2.along_y()

    tot = ar_wait(7)
    for r, (s1, s2) in enumerate(back_sums(tot, 2, 0)):
        n = 128 - 64 * r
        at = slice(128 * r, 128 * r + n)
        COLS[6, at] = COLS[4, at] * COLS[0, at] * col(s2 / count)[0:n]
        COLS[7, at] = COLS[4, at] * (COLS[1, at] * col(s2 / count)[0:n] - col(s1 / count)[0:n])
    GOUT[...] = jnp.zeros_like(GOUT)

    def spec_grad(i, c):
        f4, f6, f7 = two(COLS[4]), two(COLS[6]), two(COLS[7])
        ds = []
        for e in range(4):
            h0 = 4 * i + e
            d = (f4 * DY[rows_of(h0), 256:512] - f6 * PS[h0] + f7).astype(BF)
            J[h0] = d
            ds.append(d)
        rhs = jnp.concatenate([tile(F, 4 * i + e, 0, GLO) for e in range(4)], axis=0)
        GOUT[...] += dot(jnp.concatenate(ds, axis=1), rhs)
        return c

    lax.fori_loop(0, 4, spec_grad, 0)
    if fused:
        gin = jnp.concatenate([GOUT[...], jnp.zeros((64, 384), F32)], axis=0).T
        for s in range(D):
            GI[s // 2, s % 2, 0:48] = gin[48 * s : 48 * s + 48, 0:128].astype(BF)
            GI[s // 2, s % 2, 48:96] = gin[48 * s : 48 * s + 48, 128:256].astype(BF)
            GI[s // 2, s % 2, 96:128] = jnp.zeros((32, 128), BF)
        scatter_i.between()
        scatter_1.back()
    else:
        put(GOUT, out_in)
    lax.fori_loop(4, 5, dgrad, 0)
    if fused:
        scatter_i.along_x()
        scatter_2.along_z()
        scatter_f.along_y()
    lax.fori_loop(5, 7, dgrad, 0)
    if fused:
        scatter_i.along_y()
        scatter_f.along_z()
    lax.fori_loop(7, 8, dgrad, 0)

    def field_copy(h):
        return pltpu.make_async_copy(COT.at[pl.ds(h, 4)], field_out.at[pl.ds(h, 4)], io_sem.at[6])

    def spec_field(i, c):
        w = WINT[...]
        for e in range(4):
            h0 = 4 * i + e
            dg = dot(J[h0], w, 0, 0)
            for j in range(4):
                h = h0 + 16 * j
                total = PX[slab_rows(h0, j), 128:512] + dg[64 * j : 64 * j + 64]
                wf = WF[h].astype(F32)
                for l0 in range(0, 384, 128):
                    ls = slice(128 + l0, 256 + l0)
                    COT[h, :, ls] = (total[:, l0 : l0 + 128] + COT[h, :, ls].astype(F32) * wf).astype(BF)
        for j in range(4):
            field_copy(4 * i + 16 * j).start()
        return c

    lax.fori_loop(0, 2, spec_field, 0)
    if fused:
        scatter_i.along_z()
        scatter_2.to_copies()
    lax.fori_loop(2, 4, spec_field, 0)
    if fused:
        scatter_f.to_copies()
        scatter_i.to_copies()
        for n, sc in enumerate((scatter_1, scatter_2, scatter_f, scatter_i)):
            sc.last()
            for r in range(CHUNKS[n] // sc.q):
                at = STARTS[n] + r * sc.q
                pltpu.make_async_copy(sc.done.at[r], flat_out.at[at : at + sc.q], io_sem.at[7]).start()
        await_bytes(WI.at[pl.ds(0, D - 1), pl.ds(0, 48)], g_sem.at[0])
        await_bytes(WI.at[:, half], g_sem.at[2])
        await_bytes(GBB.at[pl.ds(0, D - 1)], g_sem.at[4])
        await_bytes(flat_out, io_sem.at[7])
    pltpu.make_async_copy(COT, field_out, io_sem.at[6]).wait()


def run_block(features, cotangent, holes, weights, gains, biases, fused):
    dps, reps = lax.axis_size("dp"), lax.axis_size("rep")
    N = dps * reps
    any_spec = pl.BlockSpec(memory_space=pl.ANY)
    vmem = pl.BlockSpec(memory_space=pltpu.VMEM)
    table = jnp.asarray(dft_table())
    args = [features, cotangent, holes, table] + list(weights) + list(gains)
    if fused:
        args = args + list(biases)
    out_shape = [
        jax.ShapeDtypeStruct((SIDE, SIDE, ALL), BF),
        jax.ShapeDtypeStruct((SIDE, SIDE, ALL), BF),
        jax.ShapeDtypeStruct((32, 128), F32),
    ]
    if fused:
        out_shape.append(jax.ShapeDtypeStruct((1408, 128), BF))
    else:
        for shape in ((1152, 128), (3456, 128), (1152, 384), (192, 384), (384, 384), (192, 384)):
            out_shape.append(jax.ShapeDtypeStruct(shape, F32))
    V = pltpu.VMEM
    dma = pltpu.SemaphoreType.DMA
    scratch = [
        V((66, SIDE, 384), BF),
        V((SIDE, SIDE, 128), BF),
        V((66, SIDE, 384), BF),
        V((66, SIDE, 384), BF),
        V((POS, ALL), F32),
        V((POS, ALL), F32),
        V((16, HALF, 256), F32),
        V((17, 384, 128), BF),
        V((17, 384, 128), F32),
        V((16, HALF, 256), BF),
        V((16, HALF, 256), BF),
        V((66, SIDE, ALL), BF),
        V((16, 256, 384), BF),
        V((SIDE, SIDE, ALL), BF),
        V((HALF, 128), F32),
        V((HALF, 128), BF),
        V((384, 128), F32),
        V((384, 128), F32),
        V((768, 128), F32),
        V((8, HALF, 128), F32),
        V((8, 384, 128), F32),
        V((24, ALL), F32),
        V((2, 16, 128), F32),
        V((HALF, 384), F32),
        V((3, ALL, 384), BF),
    ]
    scratch += [V((N, n, 128), F32) for n in AR_ROWS]
    scratch += [dma((8,)), dma((8,)), dma((8,))]
    if fused:
        scratch += [
            V((1152, ALL), BF),
            V((HALF, 384), BF),
            V((384, 384), BF),
            V((384, 384), BF),
            V((HALF, 384), BF),
            V((dps, 96, 128), BF),
            V((dps, 4, 128), F32),
            V((96, 128), BF),
            dma((32,)),
            dma((40,)),
        ]
        scratch += [V((n, 128), BF) for n in CHUNKS[:3]]
        scratch += [V((4, 2, n, 128), BF) for n in CHUNKS]
        h = CHUNKS[0] // 2
        scratch += [V((4, 2, h, 128), BF), V((4, h, 128), BF), V((4, h, 128), BF)]
        scratch += [V((h, 128), BF), V((h, 128), BF), V((2, h, 128), BF)]
        for n in CHUNKS[1:]:
            q = n // 4
            scratch += [V((4, 2, 2 * q, 128), BF), V((4, 2, q, 128), BF)] + [V((4, q, 128), BF)] * 3
    return pl.pallas_call(
        functools.partial(kernel, dps, reps, fused),
        out_shape=out_shape,
        in_specs=[any_spec, any_spec, vmem, any_spec] + [vmem] * (len(args) - 4),
        out_specs=[any_spec, any_spec, vmem] + [any_spec] * (1 if fused else 6),
        scratch_shapes=scratch,
        compiler_params=pltpu.CompilerParams(
            collective_id=0, has_side_effects=True, vmem_limit_bytes=64 * 1024 * 1024 - 65536
        ),
        cost_estimate=pl.CostEstimate(flops=40_000_000_000, bytes_accessed=30_000_000, transcendentals=10_000_000),
    )(*args)


COPIES = 4


def finish_kernel(share, fused, *refs):
    it = iter(refs)

    def take(n):
        return [next(it) for _ in range(n)]

    maps = take(2)
    (norms,) = take(1)
    flat = take(1)[0] if fused else None
    outs = take(2)
    grads = take(6) if fused else []
    o_gain, o_bias = take(2)
    buf, in_sem, out_sem = take(3)
    n = SIDE // COPIES
    copies = []
    for i in range(2):
        for c in range(COPIES):
            at = pl.ds(n * c, n)
            back = pltpu.make_async_copy(buf.at[i, at], outs[i].at[at], out_sem.at[i, c])
            copy = pltpu.make_async_copy(maps[i].at[at], buf.at[i, at], in_sem.at[i, c])
            copy.start()
            copies.append((copy, back))
    if fused:
        flat_v, sems = take(2)
        grads_v = take(6)
        copy = pltpu.make_async_copy(flat, flat_v, sems.at[0])
        copy.start()
    for copy_in, copy_out in copies[: len(copies) // 2]:
        copy_in.wait()
        copy_out.start()
    if fused:
        copy.wait()
        g_ll, g_gl, g_lg, g_in, g_fu, g_out = grads_v
        g_gl[0] = flat_v[0:432].astype(F32)
        g_ll[0] = flat_v[448:592].astype(F32)
        for j in range(3):
            ls = slice(128 * j, 128 * j + 128)
            g_lg[0, :, ls] = flat_v[592 + 144 * j : 736 + 144 * j].astype(F32)
            g_fu[0, :, ls] = flat_v[1024 + 48 * j : 1072 + 48 * j].astype(F32)
            g_out[0, :, ls] = flat_v[1168 + 32 * j : 1200 + 32 * j].astype(F32)[0:24]
        g_in[0, :, 0:128] = flat_v[1280:1328].astype(F32)
        g_in[0, :, 128:192] = flat_v[1328:1376].astype(F32)[:, 0:64]
        small = [pltpu.make_async_copy(v, o, sems.at[1 + i]) for i, (v, o) in enumerate(zip(grads_v, grads))]
        for c in small:
            c.start()
    for copy_in, copy_out in copies[len(copies) // 2 :]:
        copy_in.wait()
        copy_out.start()
    first = share * lax.axis_index("dp")
    lane = lax.broadcasted_iota(jnp.int32, (8, 1152), 1)
    for at, ref in ((0, o_gain), (16, o_bias)):
        row = jnp.concatenate([norms[at + j : at + j + 1, :] for j in range(9)], axis=1)
        row = jnp.broadcast_to(row, (8, 1152))
        row = jnp.where(lane < HALF, row, pltpu.roll(row, 1152 - 64, axis=1))
        row = pltpu.roll(row, lax.rem(1152 - first, 1152), axis=1)
        ref[...] = row[0:1, 0:share]
    if fused:
        for c in small:
            c.wait()
    for _, copy_out in copies:
        copy_out.wait()


def finish(block, field, norms, flat, share, shapes):
    fused = flat is not None
    any_spec = pl.BlockSpec(memory_space=pl.ANY)
    vmem = pl.BlockSpec(memory_space=pltpu.VMEM)
    args = [block, field, norms] + ([flat] if fused else [])
    in_specs = [any_spec, any_spec, vmem] + ([any_spec] if fused else [])
    out_shape = [jax.ShapeDtypeStruct((SIDE, SIDE, ALL), BF)] * 2
    out_specs = [any_spec, any_spec]
    dma = pltpu.SemaphoreType.DMA
    scratch = [pltpu.VMEM((2, SIDE, SIDE, ALL), BF), dma((2, COPIES)), dma((2, COPIES))]
    if fused:
        out_shape += [jax.ShapeDtypeStruct(shape, F32) for shape in shapes]
        out_specs += [any_spec] * len(shapes)
        scratch += [pltpu.VMEM(flat.shape, BF), dma((1 + len(shapes),))]
        scratch += [pltpu.VMEM(shape, F32) for shape in shapes]
    out_shape += [jax.ShapeDtypeStruct((1, share), F32)] * 2
    out_specs += [vmem, vmem]
    return pl.pallas_call(
        functools.partial(finish_kernel, share, fused),
        out_shape=out_shape,
        in_specs=in_specs,
        out_specs=out_specs,
        scratch_shapes=scratch,
        compiler_params=pltpu.CompilerParams(vmem_limit_bytes=64 * 1024 * 1024 - 65536),
    )(*args)


def on_device(features, cotangent, holes, w_ll, w_gl, w_lg, w_in, w_fu, w_out, gains, biases):
    dps, reps = lax.axis_size("dp"), lax.axis_size("rep")
    share = gains.shape[1]
    shards = (w_ll, w_gl, w_lg, w_in, w_fu, w_out)
    if dps == 8 and reps == 4:
        weights = [w[0] for w in shards]
        block, field, norms, flat = run_block(features[0], cotangent[0], holes[0], weights, [gains], [biases], True)
        block_out, input_grad, *small = finish(block, field, norms, flat, share, [w.shape for w in shards])
        return (block_out[None], input_grad[None], *small)
    full = [lax.all_gather(w, "dp", axis=1, tiled=True)[0] for w in shards]
    table = jnp.concatenate([gains, biases], axis=0).astype(F32)
    table = lax.all_gather(table, "dp", axis=1, tiled=True)
    table = jnp.pad(table, ((0, 0), (0, 1152 - table.shape[1])), constant_values=1.0).reshape(18, 128)
    table = jnp.pad(table, ((0, 6), (0, 0)))
    weights = [jnp.concatenate([full[0], full[2]], axis=1), full[1], full[3].T, full[4], full[4].T, full[5]]
    block, field, norms, g_ll, g_gl, g_lg, g_in, g_fu, g_out = run_block(
        features[0], cotangent[0], holes[0], weights, [table], None, False
    )
    grads = []
    for g in (g_ll, g_gl, g_lg, g_in.T, g_fu, g_out):
        g = lax.psum(g[None], "rep")
        grads.append(lax.psum_scatter(g, "dp", scatter_dimension=1, tiled=True))
    block_out, input_grad, *small = finish(block, field, norms, None, share, ())
    return (block_out[None], input_grad[None], *grads, *small)


def solution(mesh):
    whole = P(("dp", "rep"), None, None, None)
    rows = P(None, "dp", None)
    in_specs = (whole, whole, P(("dp", "rep"), None, None)) + (rows,) * 6 + (P(None, "dp"),) * 2
    out_specs = (whole, whole) + (rows,) * 6 + (P(None, "dp"),) * 2
    return jax.shard_map(on_device, mesh=mesh, in_specs=in_specs, out_specs=out_specs, check_vma=False)
```

```python
import functools
import math

import jax
import jax.numpy as jnp
import ml_dtypes
import numpy as np
from jax import lax
from jax.experimental import pallas as pl
from jax.experimental.pallas import tpu as pltpu
from jax.sharding import PartitionSpec as P

EPS = 1e-05
K0 = math.sqrt(2.0 / math.pi)
K1 = 0.044715
MESH = pl.DeviceIdType.MESH
F32 = jnp.float32
BF = jnp.bfloat16
SIDE = 64
LOC = 128
GLO = 384
HALF = 192
ALL = LOC + GLO
WIDTHS = (HALF, GLO, LOC, GLO)
POS = SIDE * SIDE
FREQ = SIDE * (SIDE // 2 + 1)


def dft_table():
    a = np.arange(16)[:, None, None, None, None]
    j = np.arange(4)[None, :, None, None, None]
    w = np.arange(64)[None, None, :, None, None]
    k1 = np.arange(4)[None, None, None, :, None]
    l = np.arange(32)[None, None, None, None, :]
    angle = 2 * np.pi / 64 * (((a + 16 * j) * k1 + w * l) % 64)
    main_re = np.cos(angle).reshape(16, 256, 128) / 64
    main_im = -np.sin(angle).reshape(16, 256, 128) / 64
    k = np.arange(64)[None, None, None, :]
    a, j, w = a[..., 0], j[..., 0], w[..., 0]
    angle = 2 * np.pi / 64 * (((a + 16 * j) * k + 32 * w) % 64)
    ext_re = np.cos(angle).reshape(16, 256, 64) / 64
    ext_im = -np.sin(angle).reshape(16, 256, 64) / 64
    return np.concatenate([main_re, main_im, ext_re, ext_im], axis=-1).astype(ml_dtypes.bfloat16)


def dot(a, b, ca=1, cb=0):
    return lax.dot_general(a, b, (((ca,), (cb,)), ((), ())), preferred_element_type=F32)


def gate(y):
    y2 = y * y
    return y2, 0.5 + 0.5 * jnp.tanh(y * (K0 + K0 * K1 * y2))


def gelu_value(y):
    return y * gate(y)[1]


def gelu_both(y):
    y2, s = gate(y)
    value = y * s
    return value, s + value * (1.0 - s) * (2.0 * K0 + 6.0 * K0 * K1 * y2)


def gelu_slope(y):
    return gelu_both(y)[1]


def cmul(z, c, s):
    return (z[0] * c - z[1] * s, z[0] * s + z[1] * c)


def dft4(z, sign):
    (ar, ai), (br, bi), (cr, ci), (dr, di) = z
    pr, pi, qr, qi = ar + cr, ai + ci, ar - cr, ai - ci
    rr, ri, sr, si = br + dr, bi + di, br - dr, bi - di
    tr, ti = (si, -sr) if sign < 0 else (-si, sr)
    return [(pr + rr, pi + ri), (qr + tr, qi + ti), (pr - rr, pi - ri), (qr - tr, qi - ti)]


def dft16(z, sign):
    cols = []
    for n2 in range(4):
        part = dft4([z[4 * n1 + n2] for n1 in range(4)], sign)
        for k1 in range(1, 4):
            e = n2 * k1
            if e == 0:
                continue
            if e == 4:
                re, im = part[k1]
                part[k1] = (im, -re) if sign < 0 else (-im, re)
            else:
                ang = sign * 2 * math.pi * e / 16
                part[k1] = cmul(part[k1], math.cos(ang), math.sin(ang))
        cols.append(part)
    out = [None] * 16
    for k1 in range(4):
        part = dft4([cols[n2][k1] for n2 in range(4)], sign)
        for k2 in range(4):
            out[k1 + 4 * k2] = part[k2]
    return out


def dyf_pos(t):
    if t < 12:
        return 2304 + 384 * (t // 3), 128 + 128 * (t % 3)
    u = t - 12
    return 1152 + 384 * (u // 2), 256 + 128 * (u % 2)


def rows8(x):
    acc = x[0:8]
    for r in range(8, x.shape[0], 8):
        acc = acc + x[r : r + 8]
    return acc


def lane_pair(x):
    return x[:, 0:128] + x[:, 128:256]


def await_bytes(ref, sem):
    pltpu.make_async_copy(ref, ref, sem).wait()


class Ring:
    def __init__(self, dps, reps):
        self.D, self.R = dps, reps
        self.N = dps * reps
        self.dp = lax.axis_index("dp")
        self.rp = lax.axis_index("rep")
        self.me = self.dp * reps + self.rp
        self.core = lax.rem(self.rp, 2)
        self.x = lax.div(self.rp, 2)
        self.y = lax.rem(self.dp, 2)
        self.z = lax.div(self.dp, 2)

    def dev(self, i):
        return (lax.div(i, self.R), lax.rem(i, self.R))

    def barrier(self):
        sem = pltpu.get_barrier_semaphore()

        def body(d, c):
            peer = lax.rem(self.me + d, self.N)
            pl.semaphore_signal(sem, inc=1, device_id=self.dev(peer), device_id_type=MESH)
            return c

        lax.fori_loop(1, self.N, body, 0)
        pl.semaphore_wait(sem, self.N - 1)

    def send(self, src, dst, ss, rs, device):
        pltpu.make_async_remote_copy(
            src_ref=src, dst_ref=dst, send_sem=ss, recv_sem=rs, device_id=device, device_id_type=MESH
        ).start()

    def sibling(self):
        return (self.dp, self.rp + 1 - 2 * self.core)

    def across(self):
        return (self.dp, lax.rem(self.rp + 2, 4))

    def beside(self):
        return (self.dp + 1 - 2 * self.y, self.rp)


class Gather:
    def __init__(self, ring, own, buf, sems, base):
        self.ring, self.own, self.buf, self.sems, self.base = ring, own, buf, sems, base
        self.lo, self.q = 0, own.shape[0] // 4

    def sem(self, i):
        return self.sems.at[self.base + i]

    def rows(self, i):
        return pl.ds(pl.multiple_of(self.lo + i * self.q, 16), self.q)

    def place(self):
        rows = self.rows(self.ring.rp)
        self.buf[self.ring.z, self.ring.y, rows] = self.own[rows]

    def along_z(self):
        g = self.ring
        rows = self.rows(g.rp)
        for d in range(1, 4):
            there = (2 * lax.rem(g.z + d, 4) + g.y, g.rp)
            g.send(self.own.at[rows], self.buf.at[g.z, g.y, rows], self.sem(0), self.sem(1), there)

    def along_y(self):
        g = self.ring
        await_bytes(self.buf.at[pl.ds(0, 3), 0, pl.ds(0, self.q)], self.sem(1))
        part = self.buf.at[:, g.y, self.rows(g.rp)]
        g.send(part, part, self.sem(2), self.sem(3), g.beside())

    def along_x(self):
        g = self.ring
        await_bytes(self.buf.at[:, 0, pl.ds(0, self.q)], self.sem(3))
        part = self.buf.at[:, :, self.rows(g.rp)]
        g.send(part, part, self.sem(4), self.sem(5), g.across())
        g.send(part, part, self.sem(6), self.sem(7), g.sibling())

    def between(self):
        g = self.ring
        await_bytes(self.buf.at[:, :, pl.ds(0, self.q)], self.sem(5))
        part = self.buf.at[:, :, self.rows(lax.rem(g.rp + 2, 4))]
        g.send(part, part, self.sem(8), self.sem(9), g.sibling())

    def last(self):
        one = self.buf.at[:, :, pl.ds(0, self.q)]
        for i in (7, 9, 4, 6, 8):
            await_bytes(one, self.sem(i))
        await_bytes(self.buf.at[pl.ds(0, 3), 0, pl.ds(0, self.q)], self.sem(0))
        await_bytes(self.buf.at[:, 0, pl.ds(0, self.q)], self.sem(2))


class Scatter:
    def __init__(self, ring, buf, scratch, sems, base):
        self.ring, self.buf, self.sems, self.base = ring, buf, sems, base
        self.one, self.two, self.three, self.four, self.done = scratch
        self.q = buf.shape[2] // 4
        self.slot = 2 * ring.core + ring.x

    def sem(self, i):
        return self.sems.at[self.base + i]

    def rows(self, index, n):
        return pl.ds(pl.multiple_of(index * self.q, 16), n * self.q)

    def between(self):
        g = self.ring
        there = self.buf.at[:, :, self.rows(2 * (1 - g.core), 2)]
        g.send(there, self.one, self.sem(0), self.sem(1), g.sibling())

    def add(self, zi, yi, at, other):
        self.buf[zi, yi, at] = (self.buf[zi, yi, at].astype(F32) + other.astype(F32)).astype(BF)

    def along_x(self):
        g = self.ring
        await_bytes(self.one, self.sem(1))

        def body(s, c):
            zi, yi = lax.div(s, 2), lax.rem(s, 2)
            self.add(zi, yi, self.rows(2 * g.core, 2), self.one[zi, yi])
            return c

        lax.fori_loop(0, 8, body, 0)
        there = self.buf.at[:, :, self.rows(2 * g.core + 1 - g.x, 1)]
        g.send(there, self.two, self.sem(2), self.sem(3), g.across())

    def along_y(self):
        g = self.ring
        await_bytes(self.two, self.sem(3))
        at = self.rows(self.slot, 1)

        def body(s, c):
            zi, yi = lax.div(s, 2), lax.rem(s, 2)
            self.add(zi, yi, at, self.two[zi, yi])
            return c

        lax.fori_loop(0, 8, body, 0)
        g.send(self.buf.at[:, 1 - g.y, at], self.three, self.sem(4), self.sem(5), g.beside())

    def along_z(self):
        g = self.ring
        await_bytes(self.three, self.sem(5))
        at = self.rows(self.slot, 1)
        for k in range(4):
            self.add(k, g.y, at, self.three[k])
        for d in range(1, 4):
            zz = lax.rem(g.z + d, 4)
            g.send(self.buf.at[zz, g.y, at], self.four.at[g.z], self.sem(6), self.sem(7), (2 * zz + g.y, g.rp))
        self.four[g.z] = self.buf[g.z, g.y, at]

    def to_copies(self):
        g = self.ring
        await_bytes(self.four.at[pl.ds(0, 3)], self.sem(7))
        total = self.four[0].astype(F32)
        for k in range(1, 4):
            total = total + self.four[k].astype(F32)
        self.done[self.slot] = total.astype(BF)
        mine = self.done.at[self.slot]
        for d in range(1, 4):
            g.send(mine, mine, self.sem(8), self.sem(9), (g.dp, lax.rem(g.rp + d, 4)))

    def last(self):
        three = self.done.at[pl.ds(0, 3)]
        await_bytes(three, self.sem(9))
        await_bytes(self.one, self.sem(0))
        await_bytes(self.two, self.sem(2))
        await_bytes(self.three, self.sem(4))
        await_bytes(self.four.at[pl.ds(0, 3)], self.sem(6))
        await_bytes(three, self.sem(8))


class GatherHalf(Gather):
    def __init__(self, ring, own, buf, sems, base, lo, n):
        super().__init__(ring, own, buf, sems, base)
        self.lo, self.q = lo, n // 2

    def place(self):
        rows = self.rows(self.ring.core)
        self.buf[self.ring.z, self.ring.y, rows] = self.own[rows]

    def along_z(self):
        g = self.ring
        rows = self.rows(g.core)
        for d in range(1, 4):
            there = (2 * lax.rem(g.z + d, 4) + g.y, g.rp)
            g.send(self.own.at[rows], self.buf.at[g.z, g.y, rows], self.sem(0), self.sem(1), there)

    def along_y(self):
        g = self.ring
        await_bytes(self.buf.at[pl.ds(0, 3), 0, pl.ds(0, self.q)], self.sem(1))
        part = self.buf.at[:, g.y, self.rows(g.core)]
        g.send(part, part, self.sem(2), self.sem(3), g.beside())

    def between(self):
        g = self.ring
        await_bytes(self.buf.at[:, 0, pl.ds(0, self.q)], self.sem(3))
        part = self.buf.at[:, :, self.rows(g.core)]
        g.send(part, part, self.sem(4), self.sem(5), g.sibling())

    def last(self):
        one = self.buf.at[:, :, pl.ds(0, self.q)]
        await_bytes(one, self.sem(5))
        await_bytes(one, self.sem(4))
        await_bytes(self.buf.at[pl.ds(0, 3), 0, pl.ds(0, self.q)], self.sem(0))
        await_bytes(self.buf.at[:, 0, pl.ds(0, self.q)], self.sem(2))


class ScatterHalf:
    def __init__(self, ring, buf, scratch, sems, base):
        self.ring, self.buf, self.sems, self.base = ring, buf, sems, base
        self.one, self.three, self.four, self.part, self.two, self.done = scratch
        self.q = buf.shape[2] // 2

    def sem(self, i):
        return self.sems.at[self.base + i]

    def rows(self, index):
        return pl.ds(pl.multiple_of(index * self.q, 16), self.q)

    def between(self):
        g = self.ring
        g.send(self.buf.at[:, :, self.rows(1 - g.core)], self.one, self.sem(0), self.sem(1), g.sibling())

    def add(self, zi, yi, other):
        at = self.rows(self.ring.core)
        self.buf[zi, yi, at] = (self.buf[zi, yi, at].astype(F32) + other.astype(F32)).astype(BF)

    def along_y(self):
        g = self.ring
        await_bytes(self.one, self.sem(1))

        def body(s, c):
            zi, yi = lax.div(s, 2), lax.rem(s, 2)
            self.add(zi, yi, self.one[zi, yi])
            return c

        lax.fori_loop(0, 8, body, 0)
        there = self.buf.at[:, 1 - g.y, self.rows(g.core)]
        g.send(there, self.three, self.sem(2), self.sem(3), g.beside())

    def along_z(self):
        g = self.ring
        await_bytes(self.three, self.sem(3))
        at = self.rows(g.core)
        for k in range(4):
            self.add(k, g.y, self.three[k])
        for d in range(1, 4):
            zz = lax.rem(g.z + d, 4)
            g.send(self.buf.at[zz, g.y, at], self.four.at[g.z], self.sem(4), self.sem(5), (2 * zz + g.y, g.rp))
        self.four[g.z] = self.buf[g.z, g.y, at]

    def along_x(self):
        g = self.ring
        await_bytes(self.four.at[pl.ds(0, 3)], self.sem(5))
        total = self.four[0].astype(F32)
        for k in range(1, 4):
            total = total + self.four[k].astype(F32)
        self.part[...] = total.astype(BF)
        g.send(self.part, self.two, self.sem(6), self.sem(7), g.across())

    def back(self):
        g = self.ring
        await_bytes(self.two, self.sem(7))
        self.done[g.core] = (self.part[...].astype(F32) + self.two[...].astype(F32)).astype(BF)
        mine = self.done.at[g.core]
        g.send(mine, mine, self.sem(8), self.sem(9), g.sibling())

    def last(self):
        half = self.done.at[0]
        await_bytes(half, self.sem(9))
        await_bytes(self.one, self.sem(0))
        await_bytes(self.three, self.sem(2))
        await_bytes(self.four.at[pl.ds(0, 3)], self.sem(4))
        await_bytes(self.part, self.sem(6))
        await_bytes(half, self.sem(8))


class ScatterDirect(ScatterHalf):
    def __init__(self, ring, buf, scratch, sems, base):
        self.ring, self.buf, self.sems, self.base = ring, buf, sems, base
        self.one, self.eight, self.part, self.two, self.done = scratch
        self.q = buf.shape[2] // 2

    def along_yz(self):
        g = self.ring
        await_bytes(self.one, self.sem(1))
        at = self.rows(g.core)
        for zi in range(4):
            for yi in range(2):
                self.add(zi, yi, self.one[zi, yi])

        def body(d, c):
            there = lax.rem(g.dp + d, 8)
            src = self.buf.at[lax.div(there, 2), lax.rem(there, 2), at]
            g.send(src, self.eight.at[g.dp], self.sem(2), self.sem(3), (there, g.rp))
            return c

        lax.fori_loop(1, 8, body, 0)
        self.eight[g.dp] = self.buf[g.z, g.y, at]

    def along_x(self):
        g = self.ring
        await_bytes(self.eight.at[pl.ds(0, 7)], self.sem(3))
        total = self.eight[0].astype(F32)
        for k in range(1, 8):
            total = total + self.eight[k].astype(F32)
        self.part[...] = total.astype(BF)
        g.send(self.part, self.two, self.sem(6), self.sem(7), g.across())

    def last(self):
        half = self.done.at[0]
        await_bytes(half, self.sem(9))
        await_bytes(self.one, self.sem(0))
        await_bytes(self.eight.at[pl.ds(0, 7)], self.sem(2))
        await_bytes(self.part, self.sem(6))
        await_bytes(half, self.sem(8))


AR_ROWS = (4, 6, 2, 6, 2, 6, 6, 4)
CHUNKS = (448, 576, 256, 96)
STARTS = (0, 448, 1024, 1280)


def mask_tile(row):
    at0 = lax.broadcasted_iota(jnp.int32, (SIDE, SIDE), 0)
    at1 = lax.broadcasted_iota(jnp.int32, (SIDE, SIDE), 1)
    diag = jnp.where(at0 == at1, jnp.broadcast_to(row, (SIDE, SIDE)), 0.0)
    return dot(diag.astype(BF), jnp.ones((SIDE, 128), BF))


def shifted(x, edge, by):
    moved = pltpu.roll(x, by % x.shape[0], axis=0)
    at = lax.rem(lax.broadcasted_iota(jnp.int32, x.shape, 0), SIDE)
    return jnp.where(at == edge, 0.0, moved)


def gl_runs(shards):
    runs = []
    share = 9 * GLO // shards
    row = 0
    while row < 9 * GLO:
        n = min(GLO - row % GLO, share - row % share)
        runs.append((row // GLO, row % GLO, row // share, row % share, n))
        row += n
    return runs


def col(row):
    return jnp.broadcast_to(row, (128, 128)).T


def two(x):
    return jnp.concatenate([x, x], axis=1)


def to_row(x):
    n = x.shape[0]
    if n < 128:
        x = jnp.concatenate([x, jnp.zeros((128 - n, 128), F32)], axis=0)
    return jnp.sum(x.T, axis=0, keepdims=True)


def moments(total, square, n):
    mean = total / n
    scale = lax.rsqrt(square / n - mean * mean + EPS)
    return scale, mean * scale


def kernel(dps, reps, fused, *refs):
    it = iter(refs)

    def take(n):
        return [next(it) for _ in range(n)]

    feat_h, cot_h, holes, tab_h = take(4)
    if fused:
        w_ll, w_gl, w_lg, w_in, w_fu, w_out, gain_in, bias_in = take(8)
    else:
        WCAT, WGLN, WINT, WFU, WFUT, WOUT, GBI = take(7)
    block_out, field_out, norm_out = take(3)
    if fused:
        (flat_out,) = take(1)
    else:
        out_ll, out_gl, out_lg, out_in, out_fu, out_out = take(6)
    F, WF, Z3, D3, PX, DY, PS, ST, PF, Y, J, DC, A, COT = take(14)
    EXA, EXB, DYX, ACC, ACF, COLS, COLF, ROWP, GBR, GOUT, WGL = take(11)
    ARB = take(8)
    ar_s, ar_r, io_sem = take(3)
    if fused:
        WCAT, WINT, WFU, WFUT, WOUT, WI, GBB, OWNI, g_sem, rs_sem = take(10)
        OWN, WB, RS = take(3), take(4), [take(n) for n in (6, 5, 5, 5)]
    ring = Ring(dps, reps)
    D, R, N = ring.D, ring.R, ring.N
    me, dp, rp = ring.me, ring.dp, ring.rp
    count = float(POS * N)
    fcount = float(FREQ * N)

    copy_l = pltpu.make_async_copy(feat_h.at[:, :, 0:LOC], Z3.at[1:65, :, 128:256], io_sem.at[0])
    copy_l.start()
    copy_f = pltpu.make_async_copy(feat_h.at[:, :, LOC:ALL], F.at[1:65], io_sem.at[1])
    copy_f.start()
    copy_a = pltpu.make_async_copy(tab_h, A, io_sem.at[2])
    copy_a.start()
    copy_c = pltpu.make_async_copy(cot_h, COT, io_sem.at[3])
    copy_c.start()

    def put(src, dst):
        copy = pltpu.make_async_copy(src, dst, io_sem.at[7])
        copy.start()
        copy.wait()

    def ar_start(k):
        def body(d, c):
            peer = lax.rem(me + d, N)
            ring.send(ARB[k].at[me], ARB[k].at[me], ar_s.at[k], ar_r.at[k], ring.dev(peer))
            return c

        lax.fori_loop(1, N, body, 0)

    def ar_wait(k):
        await_bytes(ARB[k].at[pl.ds(0, N - 1)], ar_r.at[k])
        await_bytes(ARB[k].at[pl.ds(0, N - 1)], ar_s.at[k])
        return jnp.sum(ARB[k][...], axis=0)

    def put_rows(k, at, rows):
        for i, row in enumerate(rows):
            ARB[k][me, at + i : at + i + 1, :] = row

    if fused:
        O1, O2, OF = OWN
        half = pl.ds(pl.multiple_of(48 * ring.core, 16), 48)
        OWNI[0:48, :] = w_in[:, 0:128]
        OWNI[48:96, :] = jnp.concatenate([w_in[:, 128:192], jnp.zeros((48, 64), BF)], axis=1)
        own = gain_in.shape[1]
        for kind, ref in ((0, gain_in), (1, bias_in)):
            row = jnp.concatenate([ref[...].astype(F32), jnp.zeros((1, 256 - own), F32)], axis=1)
            for j in range(2):
                GBB[dp, 2 * kind + j : 2 * kind + j + 1, :] = row[:, 128 * j : 128 * j + 128]
        WI[dp, half] = OWNI[half]
        for j in range(3):
            OF[48 * j : 48 * j + 48, :] = w_fu[:, 128 * j : 128 * j + 128]
            part = w_out[:, 128 * j : 128 * j + 128].astype(F32)
            part = jnp.concatenate([part, jnp.zeros((8, 128), F32)], axis=0)
            OF[144 + 32 * j : 176 + 32 * j, :] = part.astype(BF)
            O2[144 + 144 * j : 288 + 144 * j, :] = w_lg[:, 128 * j : 128 * j + 128]
        OF[240:256, :] = jnp.zeros((16, 128), BF)
        O2[0:144, :] = w_ll[...]
        O1[0:432, :] = w_gl[...]
        O1[432:448, :] = jnp.zeros((16, 128), BF)
        W1, W2, WFO, GI = WB
        gather_1 = Gather(ring, O1, W1, g_sem, 6)
        gather_2a = GatherHalf(ring, O2, W2, g_sem, 26, 0, 288)
        gather_2b = GatherHalf(ring, O2, W2, g_sem, 32, 288, 288)
        gather_f = Gather(ring, OF, WFO, g_sem, 16)
        for g in (gather_f, gather_2a, gather_2b, gather_1):
            g.place()

    ring.barrier()

    def spread(src, dst, ss, rs):
        def body(d, c):
            ring.send(src, dst, ss, rs, (lax.rem(dp + d, D), rp))
            return c

        lax.fori_loop(1, D, body, 0)

    if fused:
        spread(OWNI.at[half], WI.at[dp, half], g_sem.at[0], g_sem.at[1])
        spread(GBB.at[dp], GBB.at[dp], g_sem.at[4], g_sem.at[5])

    edge_row = jnp.zeros((SIDE, 384), BF)
    for ref in (F, Z3, D3):
        ref[0] = edge_row
        ref[65] = edge_row
    DC[0] = jnp.zeros((SIDE, ALL), BF)
    DC[65] = jnp.zeros((SIDE, ALL), BF)

    def make_wf(i, c):
        for e in range(4):
            WF[4 * i + e] = mask_tile(0.25 + holes[pl.ds(4 * i + e, 1), :].astype(F32)).astype(BF)
        return c

    lax.fori_loop(0, 16, make_wf, 0)
    if fused:
        gather_f.along_z()
        gather_2a.along_z()
    copy_l.wait()

    def make_z3(i, c):
        for e in range(2):
            h = 2 * i + e + 1
            x = Z3[h, :, 128:256].astype(F32)
            Z3[h, :, 0:128] = shifted(x, 0, 1).astype(BF)
            Z3[h, :, 256:384] = shifted(x, 63, -1).astype(BF)
        return c

    lax.fori_loop(0, 32, make_z3, 0)
    copy_f.wait()

    if fused:
        await_bytes(WI.at[pl.ds(0, D - 1), pl.ds(0, 48)], g_sem.at[1])
        part = WI.at[:, half]
        ring.send(part, part, g_sem.at[2], g_sem.at[3], ring.sibling())
        await_bytes(part, g_sem.at[3])
        gather_f.along_y()
        first = jnp.concatenate([WI[s, 0:48] for s in range(D)], axis=0).astype(F32)
        WINT[0:128, :] = first.T.astype(BF)
        first = jnp.concatenate([WI[s, 48:96] for s in range(D)], axis=0).astype(F32)
        WINT[128:192, :] = (first.T)[0:64].astype(BF)

    def tile(ref, h0, lo, hi):
        return jnp.concatenate([ref[h0 + 16 * j + 1, :, lo:hi] for j in range(4)], axis=0)

    def rows_of(h0):
        return pl.ds(pl.multiple_of(h0 * HALF, 8), HALF)

    ACC[...] = jnp.zeros_like(ACC)

    def input_proj(i, c):
        w = WINT[...]
        res = [dot(w, tile(F, 4 * i + e, 0, GLO), 1, 1) for e in range(4)]
        for e in range(4):
            PS[4 * i + e] = res[e]
        ACC[0:HALF] += sum(lane_pair(ps) for ps in res)
        ACC[HALF : 2 * HALF] += sum(lane_pair(ps * ps) for ps in res)
        return c

    lax.fori_loop(0, 4, input_proj, 0)

    def spec_rows():
        return [to_row(ACC[0:128]), to_row(ACC[128:192]), to_row(ACC[192:320]), to_row(ACC[320:384])]

    put_rows(0, 0, spec_rows())
    ar_start(0)

    if fused:
        gather_2a.along_y()
        gather_2b.along_z()
        await_bytes(GBB.at[pl.ds(0, D - 1)], g_sem.at[5])
        wide = []
        for kind in range(2):
            parts = []
            for s in range(D):
                parts.append(GBB[s, 2 * kind : 2 * kind + 1, :])
                parts.append(GBB[s, 2 * kind + 1 : 2 * kind + 2, 0 : own - 128])
            row = jnp.concatenate(parts + [jnp.ones((1, 1152 - own * D), F32)], axis=1)
            wide.append(jnp.broadcast_to(row, (8, 1152)))
    else:
        wide = []
        for kind in range(2):
            row = jnp.concatenate([GBI[9 * kind + j : 9 * kind + j + 1, :] for j in range(9)], axis=1)
            wide.append(jnp.broadcast_to(row, (8, 1152)))

    def piece(kind, offset, width):
        return pltpu.roll(wide[kind], (1152 - offset) % 1152, axis=1)[0:1, 0:width]

    for kind in range(2):
        at = 2 + kind
        spec = piece(kind, 0, 256)
        freq = piece(kind, HALF, 384)
        glo = piece(kind, HALF + GLO + LOC, 384)
        COLS[at, 0:128] = col(spec[:, 0:128])
        COLS[at, 128:192] = col(spec[:, 128:256])[0:64]
        for j in range(2):
            GBR[kind, j : j + 1, :] = spec[:, 128 * j : 128 * j + 128]
        for j in range(3):
            COLF[at, 128 * j : 128 * j + 128] = col(freq[:, 128 * j : 128 * j + 128])
            GBR[kind, 2 + j : 3 + j, :] = freq[:, 128 * j : 128 * j + 128]
            GBR[kind, 6 + j : 7 + j, :] = glo[:, 128 * j : 128 * j + 128]
        loc = piece(kind, HALF + GLO, 128)
        GBR[kind, 5:6, :] = loc
        ROWP[at : at + 1, 0:128] = loc
        ROWP[at : at + 1, 128:512] = glo

    def fold(ref):
        ref[4] = ref[0] * ref[2]
        ref[5] = ref[3] - ref[1] * ref[2]

    if fused:
        gather_f.along_x()

    copy_a.wait()
    tot = ar_wait(0)
    if fused:
        gather_2b.along_y()
        gather_1.along_z()
    for r, (lo, n) in enumerate(((0, 128), (128, 64))):
        scale, ms = moments(tot[r : r + 1], tot[r + 2 : r + 3], count)
        COLS[0, lo : lo + n] = col(scale)[0:n]
        COLS[1, lo : lo + n] = col(ms)[0:n]
    fold(COLS)

    EXA[...] = jnp.zeros_like(EXA)

    def spec_front(i, c):
        gain, bias = two(COLS[4]), two(COLS[5])
        ext = None
        for e in range(4):
            h0 = 4 * i + e
            sp = gelu_value(PS[h0] * gain + bias)
            DY[rows_of(h0), 0:256] = sp
            res = dot(sp.astype(BF), A[h0])
            DY[rows_of(h0), 256:512] = res[:, 0:256]
            ext = res[:, 256:384] if ext is None else ext + res[:, 256:384]
        EXA[...] += ext
        return c

    lax.fori_loop(0, 4, spec_front, 0)
    if fused:
        gather_2a.between()
        gather_f.between()
    low_half = lax.broadcasted_iota(jnp.int32, (HALF, 128), 1) < 64

    def split_ext(x):
        re = jnp.where(low_half, x, 0.0)
        im = jnp.where(low_half, pltpu.roll(x, 64, axis=1), 0.0)
        return re, im

    def join_ext(re, im):
        return jnp.where(low_half, re, pltpu.roll(im, 64, axis=1))

    ext_re, ext_im = split_ext(EXA[...])
    ST[16, 0:HALF] = ext_re.astype(BF)
    ST[16, HALF : 2 * HALF] = ext_im.astype(BF)

    def grab(ref, g, base):
        z = []
        for a in range(16):
            rows = pl.ds(pl.multiple_of(a * HALF + g * 8, 8), 8)
            z.append((ref[rows, base : base + 128], ref[rows, base + 128 : base + 256]))
        return z

    def fwd_fft(i, c):
        halves = [dft16(grab(DY, 2 * i + s, 256), -1) for s in range(2)]
        for k in range(16):
            for comp in range(2):
                both = jnp.concatenate([halves[0][k][comp], halves[1][k][comp]], axis=0)
                ST[k, pl.ds(pl.multiple_of(comp * HALF + i * 16, 16), 16)] = both.astype(BF)
        return c

    lax.fori_loop(0, 12, fwd_fft, 0)

    if fused:
        gather_2b.between()
        gather_f.last()
        for j in range(3):
            parts = [WFO[s // 2, s % 2, 48 * j : 48 * j + 48] for s in range(D)]
            fu = jnp.concatenate(parts, axis=0)
            WFU[:, 128 * j : 128 * j + 128] = fu
            WFUT[128 * j : 128 * j + 128, :] = fu.astype(F32).T.astype(BF)
            parts = [WFO[s // 2, s % 2, 144 + 32 * j : 176 + 32 * j].astype(F32)[0:24] for s in range(D)]
            WOUT[:, 128 * j : 128 * j + 128] = jnp.concatenate(parts, axis=0).astype(BF)

    def unit(ts):
        w = WFUT[...]
        s0 = s1 = None
        for t in ts:
            pf = dot(w, jnp.concatenate([ST[2 * t], ST[2 * t + 1]], axis=1))
            PF[2 * t] = pf[:, 0:128]
            PF[2 * t + 1] = pf[:, 128:256]
            s0 = lane_pair(pf) if s0 is None else s0 + lane_pair(pf)
            s1 = lane_pair(pf * pf) if s1 is None else s1 + lane_pair(pf * pf)
        return s0, s1

    pf = dot(WFUT[...], ST[16])
    PF[16] = pf
    ACF[0:384] = pf
    ACF[384:768] = pf * pf

    def unit_step(i, c):
        s0, s1 = unit([4 * i + e for e in range(4)])
        ACF[0:384] += s0
        ACF[384:768] += s1
        return c

    lax.fori_loop(0, 2, unit_step, 0)

    def freq_rows():
        return [to_row(ACF[128 * j : 128 * j + 128]) for j in range(6)]

    put_rows(1, 0, freq_rows())
    ar_start(1)

    if fused:
        gather_1.along_y()
        gather_2a.last()
        gather_2b.last()
        for s in range(D):
            for j in range(4):
                WCAT[144 * s : 144 * s + 144, 128 * j : 128 * j + 128] = W2[s // 2, s % 2, 144 * j : 144 * j + 144]

    def slab(ref, i, off, lo, hi, n=8):
        return ref[pl.ds(n * i + off, n), :, lo:hi].reshape(n * SIDE, hi - lo)

    def block_rows(i):
        return pl.ds(pl.multiple_of(512 * i, 512), 512)

    def conv_loc(i, c):
        lhs = jnp.concatenate([slab(Z3, i, a, 0, 384) for a in range(3)], axis=1)
        PX[block_rows(i), :] = dot(lhs, WCAT[...])
        return c

    lax.fori_loop(0, 8, conv_loc, 0)
    if fused:
        gather_1.along_x()

    tot = ar_wait(1)
    for j in range(3):
        scale, ms = moments(tot[j : j + 1], tot[j + 3 : j + 4], fcount)
        COLF[0, 128 * j : 128 * j + 128] = col(scale)
        COLF[1, 128 * j : 128 * j + 128] = col(ms)
    fold(COLF)
    lane = lax.broadcasted_iota(jnp.int32, (8, 128), 1)
    doubled = jnp.where(lax.rem(lane, 32) == 0, 1.0, 2.0).astype(F32)

    def freq_act(v, rows):
        return v * COLF[4, rows] + COLF[5, rows]

    def inv_fft(i, c):
        halves = []
        for s in range(2):
            z = []
            rr = pl.ds(pl.multiple_of(16 * i + 8 * s, 8), 8)
            ri = pl.ds(pl.multiple_of(HALF + 16 * i + 8 * s, 8), 8)
            for k in range(16):
                re = gelu_value(freq_act(PF[k, rr], rr)) * doubled
                im = gelu_value(freq_act(PF[k, ri], ri)) * doubled
                z.append((re, im))
            halves.append(dft16(z, 1))
        for a in range(16):
            for comp in range(2):
                both = jnp.concatenate([halves[0][a][comp], halves[1][a][comp]], axis=0)
                Y[a, pl.ds(pl.multiple_of(i * 16, 16), 16), 128 * comp : 128 * comp + 128] = both.astype(BF)
        return c

    lax.fori_loop(0, 12, inv_fft, 0)
    mixed = gelu_value(PF[16] * COLF[4] + COLF[5])
    EXB[...] = join_ext(mixed[0:HALF], mixed[HALF : 2 * HALF]).astype(BF)
    ROWP[8:24, :] = jnp.zeros((16, ALL), F32)

    def slab_rows(h0, j):
        return pl.ds(pl.multiple_of((h0 + 16 * j) * SIDE, SIDE), SIDE)

    def join(i, c):
        ext, w = EXB[...], WOUT[...]
        s0 = s1 = None
        for e in range(4):
            h0 = 4 * i + e
            back = dot(jnp.concatenate([Y[h0], ext], axis=1), A[h0], 1, 1)
            joined = (DY[rows_of(h0), 0:256] + back).astype(BF)
            J[h0] = joined
            pg = dot(joined, w, 0, 0)
            for j in range(4):
                v = PX[slab_rows(h0, j), 128:512] + pg[64 * j : 64 * j + 64]
                PX[slab_rows(h0, j), 128:512] = v
                s0 = rows8(v) if s0 is None else s0 + rows8(v)
                s1 = rows8(v * v) if s1 is None else s1 + rows8(v * v)
        ROWP[8:16, 128:512] += s0
        ROWP[16:24, 128:512] += s1
        return c

    lax.fori_loop(0, 4, join, 0)

    def put_norm_rows(k, lo, tiles):
        for j in range(tiles):
            at = lo + 128 * j
            put_rows(k, j, [jnp.sum(ROWP[8:16, at : at + 128], axis=0, keepdims=True)])
            put_rows(k, tiles + j, [jnp.sum(ROWP[16:24, at : at + 128], axis=0, keepdims=True)])

    put_norm_rows(3, 128, 3)
    ar_start(3)

    if fused:
        gather_1.between()
        gather_1.last()
        for tap, c0, s, r0, n in gl_runs(D):
            WGL[tap // 3, c0 : c0 + n, 128 * (tap % 3) : 128 * (tap % 3) + 128] = W1[s // 2, s % 2, r0 : r0 + n]
    else:
        for tap in range(9):
            WGL[tap // 3, 0:384, 128 * (tap % 3) : 128 * (tap % 3) + 128] = WGLN[384 * tap : 384 * tap + 384]
    for tap in range(9):
        WGL[tap // 3, 384:512, 128 * (tap % 3) : 128 * (tap % 3) + 128] = WCAT[128 * tap : 128 * tap + 128, 0:128]

    def conv_glo(i, c):
        lhs = jnp.concatenate([slab(F, i, a, 0, 384) for a in range(3)], axis=1)
        gl = dot(lhs, jnp.concatenate([WGL[a, 0:384] for a in range(3)], axis=0))
        total = PX[block_rows(i), 0:128] + gl[:, 128:256] + shifted(gl[:, 0:128], 0, 1) + shifted(gl[:, 256:384], 63, -1)
        PX[block_rows(i), 0:128] = total
        ROWP[8:16, 0:128] += rows8(total)
        ROWP[16:24, 0:128] += rows8(total * total)
        return c

    lax.fori_loop(0, 8, conv_glo, 0)
    put_norm_rows(2, 0, 1)
    ar_start(2)

    def set_norm(tot, lo, tiles):
        for j in range(tiles):
            ls = slice(lo + 128 * j, lo + 128 * j + 128)
            scale, ms = moments(tot[j : j + 1], tot[tiles + j : tiles + j + 1], count)
            ROWP[0:1, ls] = scale
            ROWP[1:2, ls] = ms
            ROWP[4:5, ls] = scale * ROWP[2:3, ls]
            ROWP[5:6, ls] = ROWP[3:4, ls] - ms * ROWP[2:3, ls]

    def out_norm(lo, hi, sem):
        ROWP[8:24, lo:hi] = jnp.zeros((16, hi - lo), F32)

        def chunk(i, c):
            def one(hh, c2):
                h = 16 * i + hh
                for l0 in range(lo, hi, 128):
                    ls = slice(l0, l0 + 128)
                    s0 = s1 = None
                    for r in (0, 32):
                        at = pl.ds(pl.multiple_of(h * SIDE + r, 32), 32)
                        y = PX[at, ls] * ROWP[4:5, ls] + ROWP[5:6, ls]
                        value, slope = gelu_both(y)
                        dy = slope * (COT[h, r : r + 32, ls].astype(F32) * WF[h, r : r + 32].astype(F32))
                        DY[at, ls] = dy
                        if l0 == 0:
                            base = Z3[h + 1, r : r + 32, 128:256]
                        else:
                            base = F[h + 1, r : r + 32, l0 - 128 : l0]
                        DC[h + 1, r : r + 32, ls] = (base.astype(F32) + value).astype(BF)
                        s0 = rows8(dy) if s0 is None else s0 + rows8(dy)
                        s1 = rows8(dy * y) if s1 is None else s1 + rows8(dy * y)
                    ROWP[8:16, ls] += s0
                    ROWP[16:24, ls] += s1
                return c2

            lax.fori_loop(0, 16, one, 0)
            pltpu.make_async_copy(
                DC.at[pl.ds(16 * i + 1, 16), :, lo:hi], block_out.at[pl.ds(16 * i, 16), :, lo:hi], sem
            ).start()
            return c

        lax.fori_loop(0, 4, chunk, 0)

    copy_c.wait()
    set_norm(ar_wait(3), 128, 3)
    out_norm(128, 512, io_sem.at[4])
    put_norm_rows(5, 128, 3)
    ar_start(5)
    set_norm(ar_wait(2), 0, 1)
    out_norm(0, 128, io_sem.at[5])
    put_norm_rows(4, 0, 1)
    ar_start(4)

    def back_sums(tot, tiles, at):
        out = []
        for j in range(tiles):
            s1 = tot[j : j + 1]
            s2 = (tot[tiles + j : tiles + j + 1] - GBR[1, at + j : at + j + 1, :] * s1) / GBR[0, at + j : at + j + 1, :]
            norm_out[at + j : at + j + 1, :] = s2
            norm_out[16 + at + j : 17 + at + j, :] = s1
            out.append((s1, s2))
        return out

    norm_out[9:16, :] = jnp.zeros((7, 128), F32)
    norm_out[25:32, :] = jnp.zeros((7, 128), F32)

    def set_back(tot, lo, tiles, at):
        for j, (s1, s2) in enumerate(back_sums(tot, tiles, at)):
            ls = slice(lo + 128 * j, lo + 128 * j + 128)
            ROWP[6:7, ls] = ROWP[4:5, ls] * ROWP[0:1, ls] * (s2 / count)
            ROWP[7:8, ls] = ROWP[4:5, ls] * (ROWP[1:2, ls] * (s2 / count) - s1 / count)

    def norm_back(lo, hi, sem):
        pltpu.make_async_copy(DC.at[1:65, :, lo:hi], block_out.at[:, :, lo:hi], sem).wait()

        def one(h, c):
            for l0 in range(lo, hi, 128):
                ls = slice(l0, l0 + 128)
                for r in (0, 32):
                    at = pl.ds(pl.multiple_of(h * SIDE + r, 32), 32)
                    d = ROWP[4:5, ls] * DY[at, ls] - ROWP[6:7, ls] * PX[at, ls] + ROWP[7:8, ls]
                    DC[h + 1, r : r + 32, ls] = d.astype(BF)
            return c

        lax.fori_loop(0, SIDE, one, 0)

    set_back(ar_wait(5), 128, 3, 6)
    norm_back(128, 512, io_sem.at[4])

    EXA[...] = jnp.zeros_like(EXA)
    GOUT[...] = jnp.zeros_like(GOUT)

    def join_back(i, c):
        w = WOUT[...]
        dgs = []
        ext = None
        for e in range(4):
            h0 = 4 * i + e
            dg = tile(DC, h0, 128, 512)
            dgs.append(dg)
            dj = dot(w, dg, 1, 1)
            PX[rows_of(h0), 0:256] = dj
            res = dot(dj.astype(BF), A[h0])
            PX[rows_of(h0), 256:512] = res[:, 0:256]
            ext = res[:, 256:384] if ext is None else ext + res[:, 256:384]
        EXA[...] += ext
        lhs = jnp.concatenate([J[4 * i + e] for e in range(4)], axis=1)
        GOUT[...] += dot(lhs, jnp.concatenate(dgs, axis=0))
        return c

    set_back(ar_wait(4), 0, 1, 5)
    norm_back(0, 128, io_sem.at[5])
    lax.fori_loop(0, 4, join_back, 0)

    def freq_back(g, c):
        z = dft16(grab(PX, g, 256), -1)
        for comp in range(2):
            rows = pl.ds(pl.multiple_of(comp * HALF + 8 * g, 8), 8)
            s0 = s1 = None
            for k in range(16):
                y = freq_act(PF[k, rows], rows)
                dy = gelu_slope(y) * (z[k][comp] * doubled)
                r0, l0 = dyf_pos(k)
                DY[pl.ds(pl.multiple_of(r0 + comp * HALF + 8 * g, 8), 8), l0 : l0 + 128] = dy
                s0 = dy if s0 is None else s0 + dy
                s1 = dy * y if s1 is None else s1 + dy * y
            ACF[rows] = s0
            ACF[pl.ds(pl.multiple_of(384 + comp * HALF + 8 * g, 8), 8)] = s1
        return c

    lax.fori_loop(0, 24, freq_back, 0)
    ext_re, ext_im = split_ext(EXA[...])
    y = PF[16] * COLF[4] + COLF[5]
    dy = gelu_slope(y) * jnp.concatenate([ext_re, ext_im], axis=0)
    DYX[...] = dy
    ACF[0:384] += dy
    ACF[384:768] += dy * y
    put_rows(6, 0, freq_rows())
    ar_start(6)

    def make_d3(i, c):
        for e in range(2):
            h = 2 * i + e + 1
            x = DC[h, :, 0:128]
            D3[h, :, 0:128] = shifted(x.astype(F32), 63, -1).astype(BF)
            D3[h, :, 128:256] = x
            D3[h, :, 256:384] = shifted(x.astype(F32), 0, 1).astype(BF)
        return c

    lax.fori_loop(0, 32, make_d3, 0)

    def wgrad_glo(i, first):
        zt = slab(F, i, 1, 0, 384, 16).T
        res = dot(zt, jnp.concatenate([slab(D3, i, 2 - a, 0, 384, 16) for a in range(3)], axis=1))
        for tap in range(9):
            r = 384 * tap
            part = res[:, 128 * tap : 128 * tap + 128]
            DY[r : r + 384, 0:128] = part if first else DY[r : r + 384, 0:128] + part

    def wgrad_loc(i, first):
        zt = slab(Z3, i, 1, 0, 384, 16).T
        for a in range(3):
            res = dot(zt, slab(DC, i, 2 - a, 0, 512, 16))
            r = 384 * a
            if first:
                DY[1152 + r : 1536 + r, 128:256] = res[:, 0:128]
                DY[r : r + 384, 128:512] = res[:, 128:512]
            else:
                DY[1152 + r : 1536 + r, 128:256] += res[:, 0:128]
                DY[r : r + 384, 128:512] += res[:, 128:512]

    def rest(f, after_first=None):
        def body(i, c):
            f(i, False)
            return c

        f(0, True)
        if after_first is not None:
            after_first()
        lax.fori_loop(1, 4, body, 0)

    rest(wgrad_glo)
    if fused:
        for tap, c0, s, r0, n in gl_runs(D):
            r = 384 * tap + c0
            W1[s // 2, s % 2, r0 : r0 + n] = DY[r : r + n, 0:128].astype(BF)
        for s in range(D):
            W1[s // 2, s % 2, 432:448] = jnp.zeros((16, 128), BF)
        scatter_1 = ScatterHalf(ring, W1, RS[0], rs_sem, 0)
        scatter_2 = Scatter(ring, W2, RS[1], rs_sem, 10)
        scatter_f = Scatter(ring, WFO, RS[2], rs_sem, 20)
        scatter_i = ScatterDirect(ring, GI, RS[3], rs_sem, 30)
        scatter_1.between()
    rest(wgrad_loc, scatter_1.along_y if fused else None)
    if fused:
        for s in range(D):
            W2[s // 2, s % 2, 0:144] = DY[1152 + 144 * s : 1296 + 144 * s, 128:256].astype(BF)
            for j in range(3):
                ls = slice(128 + 128 * j, 256 + 128 * j)
                W2[s // 2, s % 2, 144 + 144 * j : 288 + 144 * j] = DY[144 * s : 144 * s + 144, ls].astype(BF)
        scatter_2.between()
    else:
        put(DY.at[0:3456, 0:128], out_gl)
        put(DY.at[1152:2304, 128:256], out_ll)
        put(DY.at[0:1152, 128:512], out_lg)

    tot = ar_wait(6)
    for j, (s1, s2) in enumerate(back_sums(tot, 3, 2)):
        at = slice(128 * j, 128 * j + 128)
        COLF[6, at] = COLF[4, at] * COLF[0, at] * col(s2 / fcount)
        COLF[7, at] = COLF[4, at] * (COLF[1, at] * col(s2 / fcount) - col(s1 / fcount))

    def gfu_at(j, lo=0, n=384):
        return (slice(384 * (j // 2) + lo, 384 * (j // 2) + lo + n), slice(256 + 128 * (j % 2), 384 + 128 * (j % 2)))

    def dpf_tile(k, dy):
        return (COLF[4] * dy - COLF[6] * PF[k] + COLF[7]).astype(BF)

    dpf = dpf_tile(16, DYX[...])
    res = dot(ST[16], dpf, 1, 1)
    for j in range(3):
        PX[gfu_at(j)] = res[:, 128 * j : 128 * j + 128]
    ds = dot(WFU[...], dpf)
    EXB[...] = join_ext(ds[0:HALF], ds[HALF : 2 * HALF]).astype(BF)
    for t in range(4):
        spots = [dyf_pos(4 * t + e) for e in range(4)]
        parts = [dpf_tile(4 * t + e, DY[r : r + 384, l : l + 128]) for e, (r, l) in enumerate(spots)]
        dpf = jnp.concatenate(parts, axis=1)
        res = dot(jnp.concatenate([ST[4 * t + e] for e in range(4)], axis=1), dpf, 1, 1)
        for j in range(3):
            PX[gfu_at(j)] += res[:, 128 * j : 128 * j + 128]
        ds = dot(WFU[...], dpf)
        for e, (r, l) in enumerate(spots):
            DY[r : r + 384, l : l + 128] = ds[:, 128 * e : 128 * e + 128]
        if fused and t == 1:
            scatter_1.along_z()
            scatter_2.along_x()
    if fused:
        for s in range(D):
            for j in range(3):
                ls = slice(128 * j, 128 * j + 128)
                WFO[s // 2, s % 2, 48 * j : 48 * j + 48] = PX[gfu_at(j, 48 * s, 48)].astype(BF)
                part = jnp.concatenate([GOUT[24 * s : 24 * s + 24, ls], jnp.zeros((8, 128), F32)], axis=0)
                WFO[s // 2, s % 2, 144 + 32 * j : 176 + 32 * j] = part.astype(BF)
            WFO[s // 2, s % 2, 240:256] = jnp.zeros((16, 128), BF)
        scatter_f.between()
    else:
        for j in range(3):
            put(PX.at[gfu_at(j)], out_fu.at[:, 128 * j : 128 * j + 128])
        put(GOUT, out_out)

    def adj_fft(i, c):
        halves = []
        for s in range(2):
            z = []
            for k in range(16):
                r0, l0 = dyf_pos(k)
                pair = []
                for comp in range(2):
                    at = pl.ds(pl.multiple_of(r0 + comp * HALF + 16 * i + 8 * s, 8), 8)
                    pair.append(DY[at, l0 : l0 + 128])
                z.append(tuple(pair))
            halves.append(dft16(z, 1))
        for a in range(16):
            for comp in range(2):
                both = jnp.concatenate([halves[0][a][comp], halves[1][a][comp]], axis=0)
                Y[a, pl.ds(pl.multiple_of(i * 16, 16), 16), 128 * comp : 128 * comp + 128] = both.astype(BF)
        return c

    lax.fori_loop(0, 12, adj_fft, 0)
    if fused:
        scatter_f.along_x()
    ACC[...] = jnp.zeros_like(ACC)

    def spec_back(i, c):
        gain, bias, ext = two(COLS[4]), two(COLS[5]), EXB[...]
        s0 = s1 = None
        for e in range(4):
            h0 = 4 * i + e
            back = dot(jnp.concatenate([Y[h0], ext], axis=1), A[h0], 1, 1)
            y = PS[h0] * gain + bias
            dy = gelu_slope(y) * (PX[rows_of(h0), 0:256] + back)
            DY[rows_of(h0), 256:512] = dy
            s0 = lane_pair(dy) if s0 is None else s0 + lane_pair(dy)
            s1 = lane_pair(dy * y) if s1 is None else s1 + lane_pair(dy * y)
        ACC[0:HALF] += s0
        ACC[HALF : 2 * HALF] += s1
        return c

    lax.fori_loop(0, 4, spec_back, 0)
    put_rows(7, 0, spec_rows())
    ar_start(7)

    def dgrad(i, c):
        lhs = jnp.concatenate([slab(DC, i, 2 - a, 128, 512) for a in range(3)], axis=1)
        rhs = jnp.concatenate([WCAT[384 * a : 384 * a + 384, 128:512] for a in range(3)], axis=1)
        res = dot(lhs, rhs, 1, 1)
        lhs = jnp.concatenate([slab(D3, i, 2 - a, 0, 384) for a in range(3)], axis=1)
        both = dot(lhs, jnp.concatenate([WGL[a] for a in range(3)], axis=1), 1, 1)
        PX[block_rows(i), 128:512] = both[:, 0:384]
        loc = both[:, 384:512] + res[:, 128:256] + shifted(res[:, 0:128], 63, -1) + shifted(res[:, 256:384], 0, 1)
        loc = loc.reshape(8, SIDE, 128)
        at = pl.ds(8 * i, 8)
        COT[at, :, 0:128] = (loc + COT[at, :, 0:128].astype(F32) * WF[at].astype(F32)).astype(BF)
        return c

    lax.fori_loop(0, 1, dgrad, 0)
    if fused:
        scatter_1.along_x()
    lax.fori_loop(1, 3, dgrad, 0)
    if fused:
        scatter_2.along_y()
        scatter_f.along_y()

    tot = ar_wait(7)
    for r, (s1, s2) in enumerate(back_sums(tot, 2, 0)):
        n = 128 - 64 * r
        at = slice(128 * r, 128 * r + n)
        COLS[6, at] = COLS[4, at] * COLS[0, at] * col(s2 / count)[0:n]
        COLS[7, at] = COLS[4, at] * (COLS[1, at] * col(s2 / count)[0:n] - col(s1 / count)[0:n])
    GOUT[...] = jnp.zeros_like(GOUT)

    def spec_grad(i, c):
        f4, f6, f7 = two(COLS[4]), two(COLS[6]), two(COLS[7])
        ds = []
        for e in range(4):
            h0 = 4 * i + e
            d = (f4 * DY[rows_of(h0), 256:512] - f6 * PS[h0] + f7).astype(BF)
            J[h0] = d
            ds.append(d)
        rhs = jnp.concatenate([tile(F, 4 * i + e, 0, GLO) for e in range(4)], axis=0)
        GOUT[...] += dot(jnp.concatenate(ds, axis=1), rhs)
        return c

    lax.fori_loop(0, 4, spec_grad, 0)
    if fused:
        gin = jnp.concatenate([GOUT[...], jnp.zeros((64, 384), F32)], axis=0).T
        for s in range(D):
            GI[s // 2, s % 2, 0:48] = gin[48 * s : 48 * s + 48, 0:128].astype(BF)
            GI[s // 2, s % 2, 48:96] = gin[48 * s : 48 * s + 48, 128:256].astype(BF)
        scatter_i.between()
        scatter_1.back()
    else:
        put(GOUT, out_in)
    lax.fori_loop(3, 4, dgrad, 0)
    if fused:
        scatter_i.along_yz()
        scatter_f.along_z()
    lax.fori_loop(4, 5, dgrad, 0)
    if fused:
        scatter_2.along_z()
    lax.fori_loop(5, 7, dgrad, 0)
    if fused:
        scatter_i.along_x()
        scatter_f.to_copies()
    lax.fori_loop(7, 8, dgrad, 0)
    if fused:
        scatter_2.to_copies()

    def field_copy(h):
        return pltpu.make_async_copy(COT.at[pl.ds(h, 4)], field_out.at[pl.ds(h, 4)], io_sem.at[6])

    def spec_field(i, c):
        w = WINT[...]
        for e in range(4):
            h0 = 4 * i + e
            dg = dot(J[h0], w, 0, 0)
            for j in range(4):
                h = h0 + 16 * j
                total = PX[slab_rows(h0, j), 128:512] + dg[64 * j : 64 * j + 64]
                wf = WF[h].astype(F32)
                for l0 in range(0, 384, 128):
                    ls = slice(128 + l0, 256 + l0)
                    COT[h, :, ls] = (total[:, l0 : l0 + 128] + COT[h, :, ls].astype(F32) * wf).astype(BF)
        for j in range(4):
            field_copy(4 * i + 16 * j).start()
        return c

    lax.fori_loop(0, 2, spec_field, 0)
    if fused:
        scatter_i.back()
    lax.fori_loop(2, 4, spec_field, 0)
    if fused:
        for n, sc in enumerate((scatter_1, scatter_2, scatter_f, scatter_i)):
            sc.last()
            for r in range(CHUNKS[n] // sc.q):
                at = STARTS[n] + r * sc.q
                pltpu.make_async_copy(sc.done.at[r], flat_out.at[at : at + sc.q], io_sem.at[7]).start()
        await_bytes(WI.at[pl.ds(0, D - 1), pl.ds(0, 48)], g_sem.at[0])
        await_bytes(WI.at[:, half], g_sem.at[2])
        await_bytes(GBB.at[pl.ds(0, D - 1)], g_sem.at[4])
        pltpu.make_async_copy(flat_out, flat_out, io_sem.at[7]).wait()
    pltpu.make_async_copy(COT, field_out, io_sem.at[6]).wait()


def run_block(features, cotangent, holes, weights, gains, biases, fused):
    dps, reps = lax.axis_size("dp"), lax.axis_size("rep")
    N = dps * reps
    any_spec = pl.BlockSpec(memory_space=pl.ANY)
    vmem = pl.BlockSpec(memory_space=pltpu.VMEM)
    table = jnp.asarray(dft_table())
    args = [features, cotangent, holes, table] + list(weights) + list(gains)
    if fused:
        args = args + list(biases)
    out_shape = [
        jax.ShapeDtypeStruct((SIDE, SIDE, ALL), BF),
        jax.ShapeDtypeStruct((SIDE, SIDE, ALL), BF),
        jax.ShapeDtypeStruct((32, 128), F32),
    ]
    if fused:
        out_shape.append(jax.ShapeDtypeStruct((sum(CHUNKS), 128), BF))
    else:
        for shape in ((1152, 128), (3456, 128), (1152, 384), (192, 384), (384, 384), (192, 384)):
            out_shape.append(jax.ShapeDtypeStruct(shape, F32))
    V = pltpu.VMEM
    dma = pltpu.SemaphoreType.DMA
    scratch = [
        V((66, SIDE, 384), BF),
        V((SIDE, SIDE, 128), BF),
        V((66, SIDE, 384), BF),
        V((66, SIDE, 384), BF),
        V((POS, ALL), F32),
        V((POS, ALL), F32),
        V((16, HALF, 256), F32),
        V((17, 384, 128), BF),
        V((17, 384, 128), F32),
        V((16, HALF, 256), BF),
        V((16, HALF, 256), BF),
        V((66, SIDE, ALL), BF),
        V((16, 256, 384), BF),
        V((SIDE, SIDE, ALL), BF),
        V((HALF, 128), F32),
        V((HALF, 128), BF),
        V((384, 128), F32),
        V((384, 128), F32),
        V((768, 128), F32),
        V((8, HALF, 128), F32),
        V((8, 384, 128), F32),
        V((24, ALL), F32),
        V((2, 16, 128), F32),
        V((HALF, 384), F32),
        V((3, ALL, 384), BF),
    ]
    scratch += [V((N, n, 128), F32) for n in AR_ROWS]
    scratch += [dma((8,)), dma((8,)), dma((8,))]
    if fused:
        scratch += [
            V((1152, ALL), BF),
            V((HALF, 384), BF),
            V((384, 384), BF),
            V((384, 384), BF),
            V((HALF, 384), BF),
            V((dps, 96, 128), BF),
            V((dps, 4, 128), F32),
            V((96, 128), BF),
            dma((38,)),
            dma((40,)),
        ]
        scratch += [V((n, 128), BF) for n in CHUNKS[:3]]
        scratch += [V((4, 2, n, 128), BF) for n in CHUNKS]
        h = CHUNKS[0] // 2
        scratch += [V((4, 2, h, 128), BF), V((4, h, 128), BF), V((4, h, 128), BF)]
        scratch += [V((h, 128), BF), V((h, 128), BF), V((2, h, 128), BF)]
        for n in CHUNKS[1:3]:
            q = n // 4
            scratch += [V((4, 2, 2 * q, 128), BF), V((4, 2, q, 128), BF)] + [V((4, q, 128), BF)] * 3
        h = CHUNKS[3] // 2
        scratch += [V((4, 2, h, 128), BF), V((8, h, 128), BF)]
        scratch += [V((h, 128), BF), V((h, 128), BF), V((2, h, 128), BF)]
    return pl.pallas_call(
        functools.partial(kernel, dps, reps, fused),
        out_shape=out_shape,
        in_specs=[any_spec, any_spec, vmem, any_spec] + [vmem] * (len(args) - 4),
        out_specs=[any_spec, any_spec, vmem] + [any_spec] * (1 if fused else 6),
        scratch_shapes=scratch,
        compiler_params=pltpu.CompilerParams(
            collective_id=0, has_side_effects=True, vmem_limit_bytes=64 * 1024 * 1024 - 65536
        ),
        cost_estimate=pl.CostEstimate(flops=40_000_000_000, bytes_accessed=30_000_000, transcendentals=10_000_000),
    )(*args)


COPIES = 4


def finish_kernel(share, fused, *refs):
    it = iter(refs)

    def take(n):
        return [next(it) for _ in range(n)]

    maps = take(2)
    (norms,) = take(1)
    flat = take(1)[0] if fused else None
    outs = take(2)
    grads = take(6) if fused else []
    o_gain, o_bias = take(2)
    buf, in_sem, out_sem, norms_v, gain_v, bias_v, row_sem = take(7)
    n = SIDE // COPIES
    norm_copy = pltpu.make_async_copy(norms, norms_v, row_sem.at[0])
    copies = []
    for i in range(2):
        for c in range(COPIES):
            at = pl.ds(n * c, n)
            back = pltpu.make_async_copy(buf.at[i, at], outs[i].at[at], out_sem.at[i, c])
            copy = pltpu.make_async_copy(maps[i].at[at], buf.at[i, at], in_sem.at[i, c])
            copy.start()
            copies.append((copy, back))
    norm_copy.start()
    if fused:
        flat_v, sems = take(2)
        grads_v = take(6)
        copy = pltpu.make_async_copy(flat, flat_v, sems.at[0])
        copy.start()
    for copy_in, copy_out in copies[: len(copies) // 2]:
        copy_in.wait()
        copy_out.start()
    if fused:
        copy.wait()
        g_ll, g_gl, g_lg, g_in, g_fu, g_out = grads_v
        g_gl[0] = flat_v[0:432].astype(F32)
        g_ll[0] = flat_v[448:592].astype(F32)
        for j in range(3):
            ls = slice(128 * j, 128 * j + 128)
            g_lg[0, :, ls] = flat_v[592 + 144 * j : 736 + 144 * j].astype(F32)
            g_fu[0, :, ls] = flat_v[1024 + 48 * j : 1072 + 48 * j].astype(F32)
            g_out[0, :, ls] = flat_v[1168 + 32 * j : 1200 + 32 * j].astype(F32)[0:24]
        g_in[0, :, 0:128] = flat_v[1280:1328].astype(F32)
        g_in[0, :, 128:192] = flat_v[1328:1376].astype(F32)[:, 0:64]
        small = [pltpu.make_async_copy(v, o, sems.at[1 + i]) for i, (v, o) in enumerate(zip(grads_v, grads))]
        for c in small:
            c.start()
    for copy_in, copy_out in copies[len(copies) // 2 :]:
        copy_in.wait()
        copy_out.start()
    first = share * lax.axis_index("dp")
    lane = lax.broadcasted_iota(jnp.int32, (8, 1152), 1)
    norm_copy.wait()
    rows = []
    for at, ref, out in ((0, gain_v, o_gain), (16, bias_v, o_bias)):
        row = jnp.concatenate([norms_v[at + j : at + j + 1, :] for j in range(9)], axis=1)
        row = jnp.broadcast_to(row, (8, 1152))
        row = jnp.where(lane < HALF, row, pltpu.roll(row, 1152 - 64, axis=1))
        row = pltpu.roll(row, lax.rem(1152 - first, 1152), axis=1)
        ref[...] = row[0:1, 0:share]
        rows.append(pltpu.make_async_copy(ref, out, row_sem.at[1 + at // 16]))
        rows[-1].start()
    for c in rows:
        c.wait()
    if fused:
        for c in small:
            c.wait()
    for _, copy_out in copies:
        copy_out.wait()


def finish(block, field, norms, flat, share, shapes):
    fused = flat is not None
    any_spec = pl.BlockSpec(memory_space=pl.ANY)
    args = [block, field, norms] + ([flat] if fused else [])
    in_specs = [any_spec] * len(args)
    out_shape = [jax.ShapeDtypeStruct((SIDE, SIDE, ALL), BF)] * 2
    out_specs = [any_spec, any_spec]
    dma = pltpu.SemaphoreType.DMA
    scratch = [pltpu.VMEM((2, SIDE, SIDE, ALL), BF), dma((2, COPIES)), dma((2, COPIES)), pltpu.VMEM(norms.shape, F32)]
    scratch += [pltpu.VMEM((1, share), F32), pltpu.VMEM((1, share), F32), dma((3,))]
    if fused:
        out_shape += [jax.ShapeDtypeStruct(shape, F32) for shape in shapes]
        out_specs += [any_spec] * len(shapes)
        scratch += [pltpu.VMEM(flat.shape, BF), dma((1 + len(shapes),))]
        scratch += [pltpu.VMEM(shape, F32) for shape in shapes]
    out_shape += [jax.ShapeDtypeStruct((1, share), F32)] * 2
    out_specs += [any_spec] * 2
    return pl.pallas_call(
        functools.partial(finish_kernel, share, fused),
        out_shape=out_shape,
        in_specs=in_specs,
        out_specs=out_specs,
        scratch_shapes=scratch,
        compiler_params=pltpu.CompilerParams(vmem_limit_bytes=64 * 1024 * 1024 - 65536),
    )(*args)


def on_device(features, cotangent, holes, w_ll, w_gl, w_lg, w_in, w_fu, w_out, gains, biases):
    dps, reps = lax.axis_size("dp"), lax.axis_size("rep")
    share = gains.shape[1]
    shards = (w_ll, w_gl, w_lg, w_in, w_fu, w_out)
    if dps == 8 and reps == 4:
        weights = [w[0] for w in shards]
        block, field, norms, flat = run_block(features[0], cotangent[0], holes[0], weights, [gains], [biases], True)
        block_out, input_grad, *small = finish(block, field, norms, flat, share, [w.shape for w in shards])
        return (block_out[None], input_grad[None], *small)
    full = [lax.all_gather(w, "dp", axis=1, tiled=True)[0] for w in shards]
    table = jnp.concatenate([gains, biases], axis=0).astype(F32)
    table = lax.all_gather(table, "dp", axis=1, tiled=True)
    table = jnp.pad(table, ((0, 0), (0, 1152 - table.shape[1])), constant_values=1.0).reshape(18, 128)
    table = jnp.pad(table, ((0, 6), (0, 0)))
    weights = [jnp.concatenate([full[0], full[2]], axis=1), full[1], full[3].T, full[4], full[4].T, full[5]]
    block, field, norms, g_ll, g_gl, g_lg, g_in, g_fu, g_out = run_block(
        features[0], cotangent[0], holes[0], weights, [table], None, False
    )
    grads = []
    for g in (g_ll, g_gl, g_lg, g_in.T, g_fu, g_out):
        g = lax.psum(g[None], "rep")
        grads.append(lax.psum_scatter(g, "dp", scatter_dimension=1, tiled=True))
    block_out, input_grad, *small = finish(block, field, norms, None, share, ())
    return (block_out[None], input_grad[None], *grads, *small)


def solution(mesh):
    whole = P(("dp", "rep"), None, None, None)
    rows = P(None, "dp", None)
    in_specs = (whole, whole, P(("dp", "rep"), None, None)) + (rows,) * 6 + (P(None, "dp"),) * 2
    out_specs = (whole, whole) + (rows,) * 6 + (P(None, "dp"),) * 2
    return jax.shard_map(on_device, mesh=mesh, in_specs=in_specs, out_specs=out_specs, check_vma=False)
```

```python
import functools
import math

import jax
import jax.numpy as jnp
import ml_dtypes
import numpy as np
from jax import lax
from jax.experimental import pallas as pl
from jax.experimental.pallas import tpu as pltpu
from jax.sharding import PartitionSpec as P

EPS = 1e-05
K0 = math.sqrt(2.0 / math.pi)
K1 = 0.044715
MESH = pl.DeviceIdType.MESH
F32 = jnp.float32
BF = jnp.bfloat16
SIDE = 64
LOC = 128
GLO = 384
HALF = 192
ALL = LOC + GLO
WIDTHS = (HALF, GLO, LOC, GLO)
POS = SIDE * SIDE
FREQ = SIDE * (SIDE // 2 + 1)


def dft_table():
    a = np.arange(16)[:, None, None, None, None]
    j = np.arange(4)[None, :, None, None, None]
    w = np.arange(64)[None, None, :, None, None]
    k1 = np.arange(4)[None, None, None, :, None]
    l = np.arange(32)[None, None, None, None, :]
    angle = 2 * np.pi / 64 * (((a + 16 * j) * k1 + w * l) % 64)
    main_re = np.cos(angle).reshape(16, 256, 128) / 64
    main_im = -np.sin(angle).reshape(16, 256, 128) / 64
    k = np.arange(64)[None, None, None, :]
    a, j, w = a[..., 0], j[..., 0], w[..., 0]
    angle = 2 * np.pi / 64 * (((a + 16 * j) * k + 32 * w) % 64)
    ext_re = np.cos(angle).reshape(16, 256, 64) / 64
    ext_im = -np.sin(angle).reshape(16, 256, 64) / 64
    return np.concatenate([main_re, main_im, ext_re, ext_im], axis=-1).astype(ml_dtypes.bfloat16)


def dot(a, b, ca=1, cb=0):
    return lax.dot_general(a, b, (((ca,), (cb,)), ((), ())), preferred_element_type=F32)


def gate(y):
    y2 = y * y
    return y2, 0.5 + 0.5 * jnp.tanh(y * (K0 + K0 * K1 * y2))


def gelu_value(y):
    return y * gate(y)[1]


def gelu_both(y):
    y2, s = gate(y)
    value = y * s
    return value, s + value * (1.0 - s) * (2.0 * K0 + 6.0 * K0 * K1 * y2)


def gelu_slope(y):
    return gelu_both(y)[1]


def cmul(z, c, s):
    return (z[0] * c - z[1] * s, z[0] * s + z[1] * c)


def dft4(z, sign):
    (ar, ai), (br, bi), (cr, ci), (dr, di) = z
    pr, pi, qr, qi = ar + cr, ai + ci, ar - cr, ai - ci
    rr, ri, sr, si = br + dr, bi + di, br - dr, bi - di
    tr, ti = (si, -sr) if sign < 0 else (-si, sr)
    return [(pr + rr, pi + ri), (qr + tr, qi + ti), (pr - rr, pi - ri), (qr - tr, qi - ti)]


def dft16(z, sign):
    cols = []
    for n2 in range(4):
        part = dft4([z[4 * n1 + n2] for n1 in range(4)], sign)
        for k1 in range(1, 4):
            e = n2 * k1
            if e == 0:
                continue
            if e == 4:
                re, im = part[k1]
                part[k1] = (im, -re) if sign < 0 else (-im, re)
            else:
                ang = sign * 2 * math.pi * e / 16
                part[k1] = cmul(part[k1], math.cos(ang), math.sin(ang))
        cols.append(part)
    out = [None] * 16
    for k1 in range(4):
        part = dft4([cols[n2][k1] for n2 in range(4)], sign)
        for k2 in range(4):
            out[k1 + 4 * k2] = part[k2]
    return out


def dyf_pos(t):
    if t < 12:
        return 2304 + 384 * (t // 3), 128 + 128 * (t % 3)
    u = t - 12
    return 1152 + 384 * (u // 2), 256 + 128 * (u % 2)


def rows8(x):
    acc = x[0:8]
    for r in range(8, x.shape[0], 8):
        acc = acc + x[r : r + 8]
    return acc


def lane_pair(x):
    return x[:, 0:128] + x[:, 128:256]


def await_bytes(ref, sem):
    pltpu.make_async_copy(ref, ref, sem).wait()


class Ring:
    def __init__(self, dps, reps):
        self.D, self.R = dps, reps
        self.N = dps * reps
        self.dp = lax.axis_index("dp")
        self.rp = lax.axis_index("rep")
        self.me = self.dp * reps + self.rp
        self.core = lax.rem(self.rp, 2)
        self.x = lax.div(self.rp, 2)
        self.y = lax.rem(self.dp, 2)
        self.z = lax.div(self.dp, 2)

    def dev(self, i):
        return (lax.div(i, self.R), lax.rem(i, self.R))

    def barrier(self):
        sem = pltpu.get_barrier_semaphore()

        def body(d, c):
            peer = lax.rem(self.me + d, self.N)
            pl.semaphore_signal(sem, inc=1, device_id=self.dev(peer), device_id_type=MESH)
            return c

        lax.fori_loop(1, self.N, body, 0)
        pl.semaphore_wait(sem, self.N - 1)

    def send(self, src, dst, ss, rs, device):
        pltpu.make_async_remote_copy(
            src_ref=src, dst_ref=dst, send_sem=ss, recv_sem=rs, device_id=device, device_id_type=MESH
        ).start()

    def sibling(self):
        return (self.dp, self.rp + 1 - 2 * self.core)

    def across(self):
        return (self.dp, lax.rem(self.rp + 2, 4))

    def beside(self):
        return (self.dp + 1 - 2 * self.y, self.rp)


class Gather:
    def __init__(self, ring, own, buf, sems, base):
        self.ring, self.own, self.buf, self.sems, self.base = ring, own, buf, sems, base
        self.lo, self.q = 0, own.shape[0] // 4

    def sem(self, i):
        return self.sems.at[self.base + i]

    def rows(self, i):
        return pl.ds(pl.multiple_of(self.lo + i * self.q, 16), self.q)

    def place(self):
        rows = self.rows(self.ring.rp)
        self.buf[self.ring.z, self.ring.y, rows] = self.own[rows]

    def along_z(self):
        g = self.ring
        rows = self.rows(g.rp)
        for d in range(1, 4):
            there = (2 * lax.rem(g.z + d, 4) + g.y, g.rp)
            g.send(self.own.at[rows], self.buf.at[g.z, g.y, rows], self.sem(0), self.sem(1), there)

    def along_y(self):
        g = self.ring
        await_bytes(self.buf.at[pl.ds(0, 3), 0, pl.ds(0, self.q)], self.sem(1))
        part = self.buf.at[:, g.y, self.rows(g.rp)]
        g.send(part, part, self.sem(2), self.sem(3), g.beside())

    def along_x(self):
        g = self.ring
        await_bytes(self.buf.at[:, 0, pl.ds(0, self.q)], self.sem(3))
        part = self.buf.at[:, :, self.rows(g.rp)]
        g.send(part, part, self.sem(4), self.sem(5), g.across())
        g.send(part, part, self.sem(6), self.sem(7), g.sibling())

    def between(self):
        g = self.ring
        await_bytes(self.buf.at[:, :, pl.ds(0, self.q)], self.sem(5))
        part = self.buf.at[:, :, self.rows(lax.rem(g.rp + 2, 4))]
        g.send(part, part, self.sem(8), self.sem(9), g.sibling())

    def last(self):
        one = self.buf.at[:, :, pl.ds(0, self.q)]
        for i in (7, 9, 4, 6, 8):
            await_bytes(one, self.sem(i))
        await_bytes(self.buf.at[pl.ds(0, 3), 0, pl.ds(0, self.q)], self.sem(0))
        await_bytes(self.buf.at[:, 0, pl.ds(0, self.q)], self.sem(2))


class Scatter:
    def __init__(self, ring, buf, scratch, sems, base):
        self.ring, self.buf, self.sems, self.base = ring, buf, sems, base
        self.one, self.two, self.three, self.four, self.done = scratch
        self.q = buf.shape[2] // 4
        self.slot = 2 * ring.core + ring.x

    def sem(self, i):
        return self.sems.at[self.base + i]

    def rows(self, index, n):
        return pl.ds(pl.multiple_of(index * self.q, 16), n * self.q)

    def between(self):
        g = self.ring
        there = self.buf.at[:, :, self.rows(2 * (1 - g.core), 2)]
        g.send(there, self.one, self.sem(0), self.sem(1), g.sibling())

    def add(self, zi, yi, at, other):
        self.buf[zi, yi, at] = (self.buf[zi, yi, at].astype(F32) + other.astype(F32)).astype(BF)

    def along_x(self):
        g = self.ring
        await_bytes(self.one, self.sem(1))

        def body(s, c):
            zi, yi = lax.div(s, 2), lax.rem(s, 2)
            self.add(zi, yi, self.rows(2 * g.core, 2), self.one[zi, yi])
            return c

        lax.fori_loop(0, 8, body, 0)
        there = self.buf.at[:, :, self.rows(2 * g.core + 1 - g.x, 1)]
        g.send(there, self.two, self.sem(2), self.sem(3), g.across())

    def along_y(self):
        g = self.ring
        await_bytes(self.two, self.sem(3))
        at = self.rows(self.slot, 1)

        def body(s, c):
            zi, yi = lax.div(s, 2), lax.rem(s, 2)
            self.add(zi, yi, at, self.two[zi, yi])
            return c

        lax.fori_loop(0, 8, body, 0)
        g.send(self.buf.at[:, 1 - g.y, at], self.three, self.sem(4), self.sem(5), g.beside())

    def along_z(self):
        g = self.ring
        await_bytes(self.three, self.sem(5))
        at = self.rows(self.slot, 1)
        for k in range(4):
            self.add(k, g.y, at, self.three[k])
        for d in range(1, 4):
            zz = lax.rem(g.z + d, 4)
            g.send(self.buf.at[zz, g.y, at], self.four.at[g.z], self.sem(6), self.sem(7), (2 * zz + g.y, g.rp))
        self.four[g.z] = self.buf[g.z, g.y, at]

    def to_copies(self):
        g = self.ring
        await_bytes(self.four.at[pl.ds(0, 3)], self.sem(7))
        total = self.four[0].astype(F32)
        for k in range(1, 4):
            total = total + self.four[k].astype(F32)
        self.done[self.slot] = total.astype(BF)
        mine = self.done.at[self.slot]
        for d in range(1, 4):
            g.send(mine, mine, self.sem(8), self.sem(9), (g.dp, lax.rem(g.rp + d, 4)))

    def last(self):
        three = self.done.at[pl.ds(0, 3)]
        await_bytes(three, self.sem(9))
        await_bytes(self.one, self.sem(0))
        await_bytes(self.two, self.sem(2))
        await_bytes(self.three, self.sem(4))
        await_bytes(self.four.at[pl.ds(0, 3)], self.sem(6))
        await_bytes(three, self.sem(8))


class GatherHalf(Gather):
    def __init__(self, ring, own, buf, sems, base, lo, n):
        super().__init__(ring, own, buf, sems, base)
        self.lo, self.q = lo, n // 2

    def place(self):
        rows = self.rows(self.ring.core)
        self.buf[self.ring.z, self.ring.y, rows] = self.own[rows]

    def along_z(self):
        g = self.ring
        rows = self.rows(g.core)
        for d in range(1, 4):
            there = (2 * lax.rem(g.z + d, 4) + g.y, g.rp)
            g.send(self.own.at[rows], self.buf.at[g.z, g.y, rows], self.sem(0), self.sem(1), there)

    def along_y(self):
        g = self.ring
        await_bytes(self.buf.at[pl.ds(0, 3), 0, pl.ds(0, self.q)], self.sem(1))
        part = self.buf.at[:, g.y, self.rows(g.core)]
        g.send(part, part, self.sem(2), self.sem(3), g.beside())

    def between(self):
        g = self.ring
        await_bytes(self.buf.at[:, 0, pl.ds(0, self.q)], self.sem(3))
        part = self.buf.at[:, :, self.rows(g.core)]
        g.send(part, part, self.sem(4), self.sem(5), g.sibling())

    def last(self):
        one = self.buf.at[:, :, pl.ds(0, self.q)]
        await_bytes(one, self.sem(5))
        await_bytes(one, self.sem(4))
        await_bytes(self.buf.at[pl.ds(0, 3), 0, pl.ds(0, self.q)], self.sem(0))
        await_bytes(self.buf.at[:, 0, pl.ds(0, self.q)], self.sem(2))


class ScatterHalf:
    def __init__(self, ring, buf, scratch, sems, base):
        self.ring, self.buf, self.sems, self.base = ring, buf, sems, base
        self.one, self.three, self.four, self.part, self.two, self.done = scratch
        self.q = buf.shape[2] // 2

    def sem(self, i):
        return self.sems.at[self.base + i]

    def rows(self, index):
        return pl.ds(pl.multiple_of(index * self.q, 16), self.q)

    def between(self):
        g = self.ring
        g.send(self.buf.at[:, :, self.rows(1 - g.core)], self.one, self.sem(0), self.sem(1), g.sibling())

    def add(self, zi, yi, other):
        at = self.rows(self.ring.core)
        self.buf[zi, yi, at] = (self.buf[zi, yi, at].astype(F32) + other.astype(F32)).astype(BF)

    def along_y(self):
        g = self.ring
        await_bytes(self.one, self.sem(1))

        def body(s, c):
            zi, yi = lax.div(s, 2), lax.rem(s, 2)
            self.add(zi, yi, self.one[zi, yi])
            return c

        lax.fori_loop(0, 8, body, 0)
        there = self.buf.at[:, 1 - g.y, self.rows(g.core)]
        g.send(there, self.three, self.sem(2), self.sem(3), g.beside())

    def along_z(self):
        g = self.ring
        await_bytes(self.three, self.sem(3))
        at = self.rows(g.core)
        for k in range(4):
            self.add(k, g.y, self.three[k])
        for d in range(1, 4):
            zz = lax.rem(g.z + d, 4)
            g.send(self.buf.at[zz, g.y, at], self.four.at[g.z], self.sem(4), self.sem(5), (2 * zz + g.y, g.rp))
        self.four[g.z] = self.buf[g.z, g.y, at]

    def along_x(self):
        g = self.ring
        await_bytes(self.four.at[pl.ds(0, 3)], self.sem(5))
        total = self.four[0].astype(F32)
        for k in range(1, 4):
            total = total + self.four[k].astype(F32)
        self.part[...] = total.astype(BF)
        g.send(self.part, self.two, self.sem(6), self.sem(7), g.across())

    def back(self):
        g = self.ring
        await_bytes(self.two, self.sem(7))
        self.done[g.core] = (self.part[...].astype(F32) + self.two[...].astype(F32)).astype(BF)
        mine = self.done.at[g.core]
        g.send(mine, mine, self.sem(8), self.sem(9), g.sibling())

    def last(self):
        half = self.done.at[0]
        await_bytes(half, self.sem(9))
        await_bytes(self.one, self.sem(0))
        await_bytes(self.three, self.sem(2))
        await_bytes(self.four.at[pl.ds(0, 3)], self.sem(4))
        await_bytes(self.part, self.sem(6))
        await_bytes(half, self.sem(8))


class ScatterDirect(ScatterHalf):
    def __init__(self, ring, buf, scratch, sems, base):
        self.ring, self.buf, self.sems, self.base = ring, buf, sems, base
        self.one, self.eight, self.part, self.two, self.done = scratch
        self.q = buf.shape[2] // 2

    def along_yz(self):
        g = self.ring
        await_bytes(self.one, self.sem(1))
        at = self.rows(g.core)
        for zi in range(4):
            for yi in range(2):
                self.add(zi, yi, self.one[zi, yi])

        def body(d, c):
            there = lax.rem(g.dp + d, 8)
            src = self.buf.at[lax.div(there, 2), lax.rem(there, 2), at]
            g.send(src, self.eight.at[g.dp], self.sem(2), self.sem(3), (there, g.rp))
            return c

        lax.fori_loop(1, 8, body, 0)
        self.eight[g.dp] = self.buf[g.z, g.y, at]

    def along_x(self):
        g = self.ring
        await_bytes(self.eight.at[pl.ds(0, 7)], self.sem(3))
        total = self.eight[0].astype(F32)
        for k in range(1, 8):
            total = total + self.eight[k].astype(F32)
        self.part[...] = total.astype(BF)
        g.send(self.part, self.two, self.sem(6), self.sem(7), g.across())

    def last(self):
        half = self.done.at[0]
        await_bytes(half, self.sem(9))
        await_bytes(self.one, self.sem(0))
        await_bytes(self.eight.at[pl.ds(0, 7)], self.sem(2))
        await_bytes(self.part, self.sem(6))
        await_bytes(half, self.sem(8))


AR_ROWS = (4, 6, 2, 6, 2, 4, 6, 4, 2)
CHUNKS = (448, 576, 256, 96)
STARTS = (0, 448, 1024, 1280)


def mask_tile(row):
    at0 = lax.broadcasted_iota(jnp.int32, (SIDE, SIDE), 0)
    at1 = lax.broadcasted_iota(jnp.int32, (SIDE, SIDE), 1)
    diag = jnp.where(at0 == at1, jnp.broadcast_to(row, (SIDE, SIDE)), 0.0)
    return dot(diag.astype(BF), jnp.ones((SIDE, 128), BF))


def shifted(x, edge, by):
    moved = pltpu.roll(x, by % x.shape[0], axis=0)
    at = lax.rem(lax.broadcasted_iota(jnp.int32, x.shape, 0), SIDE)
    return jnp.where(at == edge, 0.0, moved)


def gl_runs(shards):
    runs = []
    share = 9 * GLO // shards
    row = 0
    while row < 9 * GLO:
        n = min(GLO - row % GLO, share - row % share)
        runs.append((row // GLO, row % GLO, row // share, row % share, n))
        row += n
    return runs


def col(row):
    return jnp.broadcast_to(row, (128, 128)).T


def two(x):
    return jnp.concatenate([x, x], axis=1)


def lane_sums(x):
    ones = jnp.ones((8, 128), F32)
    dims = (((1,), (1,)), ((), ()))
    sums = lax.dot_general(ones, x, dims, precision=lax.Precision.HIGHEST, preferred_element_type=F32)
    return [sums[0:1, r : r + 128] for r in range(0, x.shape[0], 128)]


def moments(total, square, n):
    mean = total / n
    scale = lax.rsqrt(square / n - mean * mean + EPS)
    return scale, mean * scale


def kernel(dps, reps, fused, *refs):
    it = iter(refs)

    def take(n):
        return [next(it) for _ in range(n)]

    feat_h, cot_h, holes, tab_h = take(4)
    if fused:
        w_ll, w_gl, w_lg, w_in, w_fu, w_out, gain_in, bias_in = take(8)
    else:
        WCAT, WGLN, WINT, WFU, WFUT, WOUT, GBI = take(7)
    block_out, field_out, norm_out = take(3)
    if fused:
        (flat_out,) = take(1)
    else:
        out_ll, out_gl, out_lg, out_in, out_fu, out_out = take(6)
    F, WF, Z3, D3, PX, DY, PS, ST, PF, Y, J, DC, A, COT = take(14)
    EXA, EXB, DYX, ACF, COLS, COLF, ROWP, GBR, GOUT, WGL = take(10)
    ARB = take(9)
    ar_s, ar_r, io_sem = take(3)
    if fused:
        WCAT, WINT, WFU, WFUT, WOUT, WI, GBB, g_sem, rs_sem = take(9)
        OWN, WB, RS = take(3), take(4), [take(n) for n in (6, 5, 6, 5)]
    ring = Ring(dps, reps)
    D, R, N = ring.D, ring.R, ring.N
    me, dp, rp = ring.me, ring.dp, ring.rp
    count = float(POS * N)
    fcount = float(FREQ * N)

    copy_l = pltpu.make_async_copy(feat_h.at[:, :, 0:LOC], Z3.at[1:65, :, 128:256], io_sem.at[0])
    copy_l.start()
    copy_f = pltpu.make_async_copy(feat_h.at[:, :, LOC:ALL], F.at[1:65], io_sem.at[1])
    copy_f.start()
    copy_a = pltpu.make_async_copy(tab_h, A, io_sem.at[2])
    copy_a.start()
    copy_c = pltpu.make_async_copy(cot_h, COT, io_sem.at[3])
    copy_c.start()

    def put(src, dst):
        copy = pltpu.make_async_copy(src, dst, io_sem.at[7])
        copy.start()
        copy.wait()

    def ar_start(k):
        def body(d, c):
            peer = lax.rem(me + d, N)
            ring.send(ARB[k].at[me], ARB[k].at[me], ar_s.at[k], ar_r.at[k], ring.dev(peer))
            return c

        lax.fori_loop(1, N, body, 0)

    def ar_wait(k):
        await_bytes(ARB[k].at[pl.ds(0, N - 1)], ar_r.at[k])
        await_bytes(ARB[k].at[pl.ds(0, N - 1)], ar_s.at[k])
        return jnp.sum(ARB[k][...], axis=0)

    def put_rows(k, at, rows):
        for i, row in enumerate(rows):
            ARB[k][me, at + i : at + i + 1, :] = row

    if fused:
        O1, O2, OF = OWN
        half = pl.ds(pl.multiple_of(48 * ring.core, 16), 48)
        O1[0:48, :] = w_in[:, 0:128]
        O1[48:96, :] = jnp.concatenate([w_in[:, 128:192], jnp.zeros((48, 64), BF)], axis=1)
        own = gain_in.shape[1]
        for kind, ref in ((0, gain_in), (1, bias_in)):
            row = jnp.concatenate([ref[...].astype(F32), jnp.zeros((1, 256 - own), F32)], axis=1)
            for j in range(2):
                GBB[dp, 2 * kind + j : 2 * kind + j + 1, :] = row[:, 128 * j : 128 * j + 128]
        WI[dp, half] = O1[half]
        for j in range(3):
            OF[48 * j : 48 * j + 48, :] = w_fu[:, 128 * j : 128 * j + 128]
            part = w_out[:, 128 * j : 128 * j + 128].astype(F32)
            part = jnp.concatenate([part, jnp.zeros((8, 128), F32)], axis=0)
            OF[144 + 32 * j : 176 + 32 * j, :] = part.astype(BF)
            O2[144 + 144 * j : 288 + 144 * j, :] = w_lg[:, 128 * j : 128 * j + 128]
        OF[240:256, :] = jnp.zeros((16, 128), BF)
        O2[0:144, :] = w_ll[...]
        O1[0:432, :] = w_gl[...]
        O1[432:448, :] = jnp.zeros((16, 128), BF)
        W1, W2, WFO, GI = WB
        gather_1 = Gather(ring, O1, W1, g_sem, 6)
        gather_2a = GatherHalf(ring, O2, W2, g_sem, 26, 0, 288)
        gather_2b = GatherHalf(ring, O2, W2, g_sem, 32, 288, 288)
        gather_f = Gather(ring, OF, WFO, g_sem, 16)
        for g in (gather_f, gather_2a, gather_2b, gather_1):
            g.place()

    ring.barrier()

    def spread(src, dst, ss, rs):
        def body(d, c):
            ring.send(src, dst, ss, rs, (lax.rem(dp + d, D), rp))
            return c

        lax.fori_loop(1, D, body, 0)

    if fused:
        spread(WI.at[dp, half], WI.at[dp, half], g_sem.at[0], g_sem.at[1])
        spread(GBB.at[dp], GBB.at[dp], g_sem.at[4], g_sem.at[5])

    edge_row = jnp.zeros((SIDE, 384), BF)
    for ref in (F, Z3, D3):
        ref[0] = edge_row
        ref[65] = edge_row
    DC[0] = jnp.zeros((SIDE, ALL), BF)
    DC[65] = jnp.zeros((SIDE, ALL), BF)

    def make_wf(i, c):
        for e in range(4):
            WF[4 * i + e] = mask_tile(0.25 + holes[pl.ds(4 * i + e, 1), :].astype(F32)).astype(BF)
        return c

    lax.fori_loop(0, 16, make_wf, 0)
    if fused:
        gather_f.along_z()
        gather_2a.along_z()
    copy_l.wait()

    def make_z3(i, c):
        for e in range(2):
            h = 2 * i + e + 1
            x = Z3[h, :, 128:256].astype(F32)
            Z3[h, :, 0:128] = shifted(x, 0, 1).astype(BF)
            Z3[h, :, 256:384] = shifted(x, 63, -1).astype(BF)
        return c

    lax.fori_loop(0, 32, make_z3, 0)
    copy_f.wait()

    if fused:
        await_bytes(WI.at[pl.ds(0, D - 1), pl.ds(0, 48)], g_sem.at[1])
        part = WI.at[:, half]
        ring.send(part, part, g_sem.at[2], g_sem.at[3], ring.sibling())
        await_bytes(part, g_sem.at[3])
        gather_f.along_y()
        first = jnp.concatenate([WI[s, 0:48] for s in range(D)], axis=0).astype(F32)
        WINT[0:128, :] = first.T.astype(BF)
        first = jnp.concatenate([WI[s, 48:96] for s in range(D)], axis=0).astype(F32)
        WINT[128:192, :] = (first.T)[0:64].astype(BF)

    def tile(ref, h0, lo, hi):
        return jnp.concatenate([ref[h0 + 16 * j + 1, :, lo:hi] for j in range(4)], axis=0)

    def rows_of(h0):
        return pl.ds(pl.multiple_of(h0 * HALF, 8), HALF)

    ACF[0:512] = jnp.zeros((512, 128), F32)

    def input_proj(i, c):
        w = WINT[...]
        res = [dot(w, tile(F, 4 * i + e, 0, GLO), 1, 1) for e in range(4)]
        for e in range(4):
            PS[4 * i + e] = res[e]
        ACF[0:HALF] += sum(lane_pair(ps) for ps in res)
        ACF[256 : 256 + HALF] += sum(lane_pair(ps * ps) for ps in res)
        return c

    lax.fori_loop(0, 4, input_proj, 0)

    def spec_rows():
        return lane_sums(ACF[0:512])

    put_rows(0, 0, spec_rows())
    ar_start(0)

    if fused:
        gather_2a.along_y()
        gather_2b.along_z()
        await_bytes(GBB.at[pl.ds(0, D - 1)], g_sem.at[5])
        wide = []
        for kind in range(2):
            parts = []
            for s in range(D):
                parts.append(GBB[s, 2 * kind : 2 * kind + 1, :])
                parts.append(GBB[s, 2 * kind + 1 : 2 * kind + 2, 0 : own - 128])
            row = jnp.concatenate(parts + [jnp.ones((1, 1152 - own * D), F32)], axis=1)
            wide.append(jnp.broadcast_to(row, (8, 1152)))
    else:
        wide = []
        for kind in range(2):
            row = jnp.concatenate([GBI[9 * kind + j : 9 * kind + j + 1, :] for j in range(9)], axis=1)
            wide.append(jnp.broadcast_to(row, (8, 1152)))

    def piece(kind, offset, width):
        return pltpu.roll(wide[kind], (1152 - offset) % 1152, axis=1)[0:1, 0:width]

    for kind in range(2):
        at = 2 + kind
        spec = piece(kind, 0, 256)
        freq = piece(kind, HALF, 384)
        glo = piece(kind, HALF + GLO + LOC, 384)
        COLS[at, 0:128] = col(spec[:, 0:128])
        COLS[at, 128:192] = col(spec[:, 128:256])[0:64]
        for j in range(2):
            GBR[kind, j : j + 1, :] = spec[:, 128 * j : 128 * j + 128]
        for j in range(3):
            COLF[at, 128 * j : 128 * j + 128] = col(freq[:, 128 * j : 128 * j + 128])
            GBR[kind, 2 + j : 3 + j, :] = freq[:, 128 * j : 128 * j + 128]
            GBR[kind, 6 + j : 7 + j, :] = glo[:, 128 * j : 128 * j + 128]
        loc = piece(kind, HALF + GLO, 128)
        GBR[kind, 5:6, :] = loc
        ROWP[at : at + 1, 0:128] = loc
        ROWP[at : at + 1, 128:512] = glo

    def fold(ref):
        ref[4] = ref[0] * ref[2]
        ref[5] = ref[3] - ref[1] * ref[2]

    if fused:
        gather_f.along_x()

    copy_a.wait()
    tot = ar_wait(0)
    if fused:
        gather_2b.along_y()
        gather_1.along_z()
    for r, (lo, n) in enumerate(((0, 128), (128, 64))):
        scale, ms = moments(tot[r : r + 1], tot[r + 2 : r + 3], count)
        COLS[0, lo : lo + n] = col(scale)[0:n]
        COLS[1, lo : lo + n] = col(ms)[0:n]
    fold(COLS)

    EXA[...] = jnp.zeros_like(EXA)

    def spec_front(i, c):
        gain, bias = two(COLS[4]), two(COLS[5])
        ext = None
        for e in range(4):
            h0 = 4 * i + e
            sp = gelu_value(PS[h0] * gain + bias)
            DY[rows_of(h0), 0:256] = sp
            res = dot(sp.astype(BF), A[h0])
            DY[rows_of(h0), 256:512] = res[:, 0:256]
            ext = res[:, 256:384] if ext is None else ext + res[:, 256:384]
        EXA[...] += ext
        return c

    lax.fori_loop(0, 4, spec_front, 0)
    if fused:
        gather_2a.between()
        gather_f.between()
    low_half = lax.broadcasted_iota(jnp.int32, (HALF, 128), 1) < 64

    def split_ext(x):
        re = jnp.where(low_half, x, 0.0)
        im = jnp.where(low_half, pltpu.roll(x, 64, axis=1), 0.0)
        return re, im

    def join_ext(re, im):
        return jnp.where(low_half, re, pltpu.roll(im, 64, axis=1))

    ext_re, ext_im = split_ext(EXA[...])
    ST[16, 0:HALF] = ext_re.astype(BF)
    ST[16, HALF : 2 * HALF] = ext_im.astype(BF)

    def grab(ref, g, base):
        z = []
        for a in range(16):
            rows = pl.ds(pl.multiple_of(a * HALF + g * 8, 8), 8)
            z.append((ref[rows, base : base + 128], ref[rows, base + 128 : base + 256]))
        return z

    def fwd_fft(i, c):
        halves = [dft16(grab(DY, 2 * i + s, 256), -1) for s in range(2)]
        for k in range(16):
            for comp in range(2):
                both = jnp.concatenate([halves[0][k][comp], halves[1][k][comp]], axis=0)
                ST[k, pl.ds(pl.multiple_of(comp * HALF + i * 16, 16), 16)] = both.astype(BF)
        return c

    lax.fori_loop(0, 12, fwd_fft, 0)

    if fused:
        gather_2b.between()
        gather_f.last()
        for j in range(3):
            parts = [WFO[s // 2, s % 2, 48 * j : 48 * j + 48] for s in range(D)]
            fu = jnp.concatenate(parts, axis=0)
            WFU[:, 128 * j : 128 * j + 128] = fu
            WFUT[128 * j : 128 * j + 128, :] = fu.astype(F32).T.astype(BF)
            parts = [WFO[s // 2, s % 2, 144 + 32 * j : 176 + 32 * j].astype(F32)[0:24] for s in range(D)]
            WOUT[:, 128 * j : 128 * j + 128] = jnp.concatenate(parts, axis=0).astype(BF)

    def unit(ts):
        w = WFUT[...]
        s0 = s1 = None
        for t in ts:
            pf = dot(w, jnp.concatenate([ST[2 * t], ST[2 * t + 1]], axis=1))
            PF[2 * t] = pf[:, 0:128]
            PF[2 * t + 1] = pf[:, 128:256]
            s0 = lane_pair(pf) if s0 is None else s0 + lane_pair(pf)
            s1 = lane_pair(pf * pf) if s1 is None else s1 + lane_pair(pf * pf)
        return s0, s1

    pf = dot(WFUT[...], ST[16])
    PF[16] = pf
    ACF[0:384] = pf
    ACF[384:768] = pf * pf

    def unit_step(i, c):
        s0, s1 = unit([4 * i + e for e in range(4)])
        ACF[0:384] += s0
        ACF[384:768] += s1
        return c

    lax.fori_loop(0, 2, unit_step, 0)

    def freq_rows():
        return lane_sums(ACF[...])

    put_rows(1, 0, freq_rows())
    ar_start(1)

    if fused:
        gather_1.along_y()
        gather_2a.last()
        gather_2b.last()
        for s in range(D):
            for j in range(4):
                WCAT[144 * s : 144 * s + 144, 128 * j : 128 * j + 128] = W2[s // 2, s % 2, 144 * j : 144 * j + 144]

    def slab(ref, i, off, lo, hi, n=8):
        return ref[pl.ds(n * i + off, n), :, lo:hi].reshape(n * SIDE, hi - lo)

    def block_rows(i):
        return pl.ds(pl.multiple_of(512 * i, 512), 512)

    def conv_loc(i, c):
        lhs = jnp.concatenate([slab(Z3, i, a, 0, 384) for a in range(3)], axis=1)
        PX[block_rows(i), :] = dot(lhs, WCAT[...])
        return c

    lax.fori_loop(0, 8, conv_loc, 0)
    if fused:
        gather_1.along_x()

    tot = ar_wait(1)
    for j in range(3):
        scale, ms = moments(tot[j : j + 1], tot[j + 3 : j + 4], fcount)
        COLF[0, 128 * j : 128 * j + 128] = col(scale)
        COLF[1, 128 * j : 128 * j + 128] = col(ms)
    fold(COLF)
    lane = lax.broadcasted_iota(jnp.int32, (8, 128), 1)
    doubled = jnp.where(lax.rem(lane, 32) == 0, 1.0, 2.0).astype(F32)

    def freq_act(v, rows):
        return v * COLF[4, rows] + COLF[5, rows]

    def inv_fft(i, c):
        halves = []
        for s in range(2):
            z = []
            rr = pl.ds(pl.multiple_of(16 * i + 8 * s, 8), 8)
            ri = pl.ds(pl.multiple_of(HALF + 16 * i + 8 * s, 8), 8)
            for k in range(16):
                re = gelu_value(freq_act(PF[k, rr], rr)) * doubled
                im = gelu_value(freq_act(PF[k, ri], ri)) * doubled
                z.append((re, im))
            halves.append(dft16(z, 1))
        for a in range(16):
            for comp in range(2):
                both = jnp.concatenate([halves[0][a][comp], halves[1][a][comp]], axis=0)
                Y[a, pl.ds(pl.multiple_of(i * 16, 16), 16), 128 * comp : 128 * comp + 128] = both.astype(BF)
        return c

    lax.fori_loop(0, 12, inv_fft, 0)
    mixed = gelu_value(PF[16] * COLF[4] + COLF[5])
    EXB[...] = join_ext(mixed[0:HALF], mixed[HALF : 2 * HALF]).astype(BF)
    ROWP[8:24, :] = jnp.zeros((16, ALL), F32)

    def slab_rows(h0, j):
        return pl.ds(pl.multiple_of((h0 + 16 * j) * SIDE, SIDE), SIDE)

    def join(i, c):
        ext, w = EXB[...], WOUT[...]
        s0 = s1 = None
        for e in range(4):
            h0 = 4 * i + e
            back = dot(jnp.concatenate([Y[h0], ext], axis=1), A[h0], 1, 1)
            joined = (DY[rows_of(h0), 0:256] + back).astype(BF)
            J[h0] = joined
            pg = dot(joined, w, 0, 0)
            for j in range(4):
                v = PX[slab_rows(h0, j), 128:512] + pg[64 * j : 64 * j + 64]
                PX[slab_rows(h0, j), 128:512] = v
                s0 = rows8(v) if s0 is None else s0 + rows8(v)
                s1 = rows8(v * v) if s1 is None else s1 + rows8(v * v)
        ROWP[8:16, 128:512] += s0
        ROWP[16:24, 128:512] += s1
        return c

    lax.fori_loop(0, 4, join, 0)

    def put_norm_rows(k, lo, tiles):
        for j in range(tiles):
            at = lo + 128 * j
            put_rows(k, j, [jnp.sum(ROWP[8:16, at : at + 128], axis=0, keepdims=True)])
            put_rows(k, tiles + j, [jnp.sum(ROWP[16:24, at : at + 128], axis=0, keepdims=True)])

    put_norm_rows(3, 128, 3)
    ar_start(3)

    if fused:
        gather_1.between()
        gather_1.last()
        for tap, c0, s, r0, n in gl_runs(D):
            WGL[tap // 3, c0 : c0 + n, 128 * (tap % 3) : 128 * (tap % 3) + 128] = W1[s // 2, s % 2, r0 : r0 + n]
    else:
        for tap in range(9):
            WGL[tap // 3, 0:384, 128 * (tap % 3) : 128 * (tap % 3) + 128] = WGLN[384 * tap : 384 * tap + 384]
    for tap in range(9):
        WGL[tap // 3, 384:512, 128 * (tap % 3) : 128 * (tap % 3) + 128] = WCAT[128 * tap : 128 * tap + 128, 0:128]

    def conv_glo(i, c):
        lhs = jnp.concatenate([slab(F, i, a, 0, 384) for a in range(3)], axis=1)
        gl = dot(lhs, jnp.concatenate([WGL[a, 0:384] for a in range(3)], axis=0))
        total = PX[block_rows(i), 0:128] + gl[:, 128:256] + shifted(gl[:, 0:128], 0, 1) + shifted(gl[:, 256:384], 63, -1)
        PX[block_rows(i), 0:128] = total
        ROWP[8:16, 0:128] += rows8(total)
        ROWP[16:24, 0:128] += rows8(total * total)
        return c

    lax.fori_loop(0, 8, conv_glo, 0)
    put_norm_rows(2, 0, 1)
    ar_start(2)

    def set_norm(tot, lo, tiles):
        for j in range(tiles):
            ls = slice(lo + 128 * j, lo + 128 * j + 128)
            scale, ms = moments(tot[j : j + 1], tot[tiles + j : tiles + j + 1], count)
            ROWP[0:1, ls] = scale
            ROWP[1:2, ls] = ms
            ROWP[4:5, ls] = scale * ROWP[2:3, ls]
            ROWP[5:6, ls] = ROWP[3:4, ls] - ms * ROWP[2:3, ls]

    def out_norm(lo, hi, sem):
        ROWP[8:24, lo:hi] = jnp.zeros((16, hi - lo), F32)

        def chunk(i, c):
            def one(hh, c2):
                h = 16 * i + hh
                for l0 in range(lo, hi, 128):
                    ls = slice(l0, l0 + 128)
                    s0 = s1 = None
                    for r in (0, 32):
                        at = pl.ds(pl.multiple_of(h * SIDE + r, 32), 32)
                        y = PX[at, ls] * ROWP[4:5, ls] + ROWP[5:6, ls]
                        value, slope = gelu_both(y)
                        dy = slope * (COT[h, r : r + 32, ls].astype(F32) * WF[h, r : r + 32].astype(F32))
                        DY[at, ls] = dy
                        if l0 == 0:
                            base = Z3[h + 1, r : r + 32, 128:256]
                        else:
                            base = F[h + 1, r : r + 32, l0 - 128 : l0]
                        DC[h + 1, r : r + 32, ls] = (base.astype(F32) + value).astype(BF)
                        s0 = rows8(dy) if s0 is None else s0 + rows8(dy)
                        s1 = rows8(dy * y) if s1 is None else s1 + rows8(dy * y)
                    ROWP[8:16, ls] += s0
                    ROWP[16:24, ls] += s1
                return c2

            lax.fori_loop(0, 16, one, 0)
            pltpu.make_async_copy(
                DC.at[pl.ds(16 * i + 1, 16), :, lo:hi], block_out.at[pl.ds(16 * i, 16), :, lo:hi], sem
            ).start()
            return c

        lax.fori_loop(0, 4, chunk, 0)

    copy_c.wait()
    set_norm(ar_wait(3), 128, 3)
    out_norm(128, 384, io_sem.at[4])
    put_norm_rows(5, 128, 2)
    ar_start(5)
    out_norm(384, 512, io_sem.at[8])
    put_norm_rows(8, 384, 1)
    ar_start(8)
    set_norm(ar_wait(2), 0, 1)
    out_norm(0, 128, io_sem.at[5])
    put_norm_rows(4, 0, 1)
    ar_start(4)

    def back_sums(tot, tiles, at):
        out = []
        for j in range(tiles):
            s1 = tot[j : j + 1]
            s2 = (tot[tiles + j : tiles + j + 1] - GBR[1, at + j : at + j + 1, :] * s1) / GBR[0, at + j : at + j + 1, :]
            norm_out[at + j : at + j + 1, :] = s2
            norm_out[16 + at + j : 17 + at + j, :] = s1
            out.append((s1, s2))
        return out

    norm_out[9:16, :] = jnp.zeros((7, 128), F32)
    norm_out[25:32, :] = jnp.zeros((7, 128), F32)

    def set_back(tot, lo, tiles, at):
        for j, (s1, s2) in enumerate(back_sums(tot, tiles, at)):
            ls = slice(lo + 128 * j, lo + 128 * j + 128)
            ROWP[6:7, ls] = ROWP[4:5, ls] * ROWP[0:1, ls] * (s2 / count)
            ROWP[7:8, ls] = ROWP[4:5, ls] * (ROWP[1:2, ls] * (s2 / count) - s1 / count)

    def norm_back(lo, hi, sem):
        pltpu.make_async_copy(DC.at[1:65, :, lo:hi], block_out.at[:, :, lo:hi], sem).wait()

        def one(h, c):
            for l0 in range(lo, hi, 128):
                ls = slice(l0, l0 + 128)
                for r in (0, 32):
                    at = pl.ds(pl.multiple_of(h * SIDE + r, 32), 32)
                    d = ROWP[4:5, ls] * DY[at, ls] - ROWP[6:7, ls] * PX[at, ls] + ROWP[7:8, ls]
                    DC[h + 1, r : r + 32, ls] = d.astype(BF)
            return c

        lax.fori_loop(0, SIDE, one, 0)

    set_back(ar_wait(5), 128, 2, 6)
    norm_back(128, 384, io_sem.at[4])
    set_back(ar_wait(8), 384, 1, 8)
    norm_back(384, 512, io_sem.at[8])

    EXA[...] = jnp.zeros_like(EXA)
    GOUT[...] = jnp.zeros_like(GOUT)

    def join_back(i, c):
        w = WOUT[...]
        dgs = []
        ext = None
        for e in range(4):
            h0 = 4 * i + e
            dg = tile(DC, h0, 128, 512)
            dgs.append(dg)
            dj = dot(w, dg, 1, 1)
            PX[rows_of(h0), 128:384] = dj
            res = dot(dj.astype(BF), A[h0])
            D3[pl.ds(3 * h0 + 1, 3), :, 0:256] = res[:, 0:256].astype(BF).reshape(3, SIDE, 256)
            ext = res[:, 256:384] if ext is None else ext + res[:, 256:384]
        EXA[...] += ext
        lhs = jnp.concatenate([J[4 * i + e] for e in range(4)], axis=1)
        GOUT[...] += dot(lhs, jnp.concatenate(dgs, axis=0))
        return c

    lax.fori_loop(0, 4, join_back, 0)

    def freq_back(i, c):
        z = []
        for a in range(16):
            at = pl.ds(pl.multiple_of(16 * lax.rem(i, 4), 16), 16)
            part = D3[3 * a + 1 + lax.div(i, 4), at, 0:256].astype(F32)
            z.append((part[:, 0:128], part[:, 128:256]))
        for half in range(2):
            hs = slice(8 * half, 8 * half + 8)
            w = dft16([(re[hs], im[hs]) for re, im in z], -1)
            for comp in range(2):
                row = comp * HALF + 16 * i + 8 * half
                rows = pl.ds(pl.multiple_of(row, 8), 8)
                s0 = s1 = None
                for k in range(16):
                    y = freq_act(PF[k, rows], rows)
                    dy = gelu_slope(y) * (w[k][comp] * doubled)
                    r0, l0 = dyf_pos(k)
                    DY[pl.ds(pl.multiple_of(r0 + row, 8), 8), l0 : l0 + 128] = dy
                    s0 = dy if s0 is None else s0 + dy
                    s1 = dy * y if s1 is None else s1 + dy * y
                ACF[rows] = s0
                ACF[pl.ds(pl.multiple_of(384 + row, 8), 8)] = s1
        return c

    lax.fori_loop(0, 12, freq_back, 0)
    ext_re, ext_im = split_ext(EXA[...])
    y = PF[16] * COLF[4] + COLF[5]
    dy = gelu_slope(y) * jnp.concatenate([ext_re, ext_im], axis=0)
    DYX[...] = dy
    ACF[0:384] += dy
    ACF[384:768] += dy * y
    put_rows(6, 0, freq_rows())
    ar_start(6)

    set_back(ar_wait(4), 0, 1, 5)
    norm_back(0, 128, io_sem.at[5])

    def make_d3(i, c):
        for e in range(2):
            h = 2 * i + e + 1
            x = DC[h, :, 0:128]
            D3[h, :, 0:128] = shifted(x.astype(F32), 63, -1).astype(BF)
            D3[h, :, 128:256] = x
            D3[h, :, 256:384] = shifted(x.astype(F32), 0, 1).astype(BF)
        return c

    lax.fori_loop(0, 32, make_d3, 0)

    def wgrad_glo(i, first):
        zt = slab(F, i, 1, 0, 384, 16).T
        res = dot(zt, jnp.concatenate([slab(D3, i, 2 - a, 0, 384, 16) for a in range(3)], axis=1))
        for tap in range(9):
            r = 384 * tap
            part = res[:, 128 * tap : 128 * tap + 128]
            DY[r : r + 384, 0:128] = part if first else DY[r : r + 384, 0:128] + part

    def wgrad_loc(i, first):
        zt = slab(Z3, i, 1, 0, 384, 16).T
        for a in range(3):
            res = dot(zt, slab(DC, i, 2 - a, 0, 512, 16))
            r = 384 * a
            if first:
                DY[1152 + r : 1536 + r, 128:256] = res[:, 0:128]
                DY[r : r + 384, 128:512] = res[:, 128:512]
            else:
                DY[1152 + r : 1536 + r, 128:256] += res[:, 0:128]
                DY[r : r + 384, 128:512] += res[:, 128:512]

    def rest(f, after_first=None):
        def body(i, c):
            f(i, False)
            return c

        f(0, True)
        if after_first is not None:
            after_first()
        lax.fori_loop(1, 4, body, 0)

    rest(wgrad_glo)
    if fused:
        for tap, c0, s, r0, n in gl_runs(D):
            r = 384 * tap + c0
            W1[s // 2, s % 2, r0 : r0 + n] = DY[r : r + n, 0:128].astype(BF)
        for s in range(D):
            W1[s // 2, s % 2, 432:448] = jnp.zeros((16, 128), BF)
        scatter_1 = ScatterHalf(ring, W1, RS[0], rs_sem, 0)
        scatter_2 = Scatter(ring, W2, RS[1], rs_sem, 10)
        scatter_f = ScatterHalf(ring, WFO, RS[2], rs_sem, 20)
        scatter_i = ScatterDirect(ring, GI, RS[3], rs_sem, 30)
        scatter_1.between()
    rest(wgrad_loc, scatter_1.along_y if fused else None)
    if fused:
        for s in range(D):
            W2[s // 2, s % 2, 0:144] = DY[1152 + 144 * s : 1296 + 144 * s, 128:256].astype(BF)
            for j in range(3):
                ls = slice(128 + 128 * j, 256 + 128 * j)
                W2[s // 2, s % 2, 144 + 144 * j : 288 + 144 * j] = DY[144 * s : 144 * s + 144, ls].astype(BF)
        scatter_2.between()
    else:
        put(DY.at[0:3456, 0:128], out_gl)
        put(DY.at[1152:2304, 128:256], out_ll)
        put(DY.at[0:1152, 128:512], out_lg)

    tot = ar_wait(6)
    for j, (s1, s2) in enumerate(back_sums(tot, 3, 2)):
        at = slice(128 * j, 128 * j + 128)
        COLF[6, at] = COLF[4, at] * COLF[0, at] * col(s2 / fcount)
        COLF[7, at] = COLF[4, at] * (COLF[1, at] * col(s2 / fcount) - col(s1 / fcount))

    def gfu_at(j, lo=0, n=384):
        return (slice(384 * j + lo, 384 * j + lo + n), slice(384, 512))

    def dpf_tile(k, dy):
        return (COLF[4] * dy - COLF[6] * PF[k] + COLF[7]).astype(BF)

    dpf = dpf_tile(16, DYX[...])
    res = dot(ST[16], dpf, 1, 1)
    for j in range(3):
        PX[gfu_at(j)] = res[:, 128 * j : 128 * j + 128]
    ds = dot(WFU[...], dpf)
    EXB[...] = join_ext(ds[0:HALF], ds[HALF : 2 * HALF]).astype(BF)
    for t in range(4):
        spots = [dyf_pos(4 * t + e) for e in range(4)]
        parts = [dpf_tile(4 * t + e, DY[r : r + 384, l : l + 128]) for e, (r, l) in enumerate(spots)]
        dpf = jnp.concatenate(parts, axis=1)
        res = dot(jnp.concatenate([ST[4 * t + e] for e in range(4)], axis=1), dpf, 1, 1)
        for j in range(3):
            PX[gfu_at(j)] += res[:, 128 * j : 128 * j + 128]
        ds = dot(WFU[...], dpf)
        for e, (r, l) in enumerate(spots):
            DY[r : r + 384, l : l + 128] = ds[:, 128 * e : 128 * e + 128]
        if fused and t == 1:
            scatter_1.along_z()
            scatter_2.along_x()
    if fused:
        for s in range(D):
            for j in range(3):
                ls = slice(128 * j, 128 * j + 128)
                WFO[s // 2, s % 2, 48 * j : 48 * j + 48] = PX[gfu_at(j, 48 * s, 48)].astype(BF)
                part = jnp.concatenate([GOUT[24 * s : 24 * s + 24, ls], jnp.zeros((8, 128), F32)], axis=0)
                WFO[s // 2, s % 2, 144 + 32 * j : 176 + 32 * j] = part.astype(BF)
            WFO[s // 2, s % 2, 240:256] = jnp.zeros((16, 128), BF)
        scatter_f.between()
    else:
        for j in range(3):
            put(PX.at[gfu_at(j)], out_fu.at[:, 128 * j : 128 * j + 128])
        put(GOUT, out_out)

    def adj_fft(i, c):
        halves = []
        for s in range(2):
            z = []
            for k in range(16):
                r0, l0 = dyf_pos(k)
                pair = []
                for comp in range(2):
                    at = pl.ds(pl.multiple_of(r0 + comp * HALF + 16 * i + 8 * s, 8), 8)
                    pair.append(DY[at, l0 : l0 + 128])
                z.append(tuple(pair))
            halves.append(dft16(z, 1))
        for a in range(16):
            for comp in range(2):
                both = jnp.concatenate([halves[0][a][comp], halves[1][a][comp]], axis=0)
                Y[a, pl.ds(pl.multiple_of(i * 16, 16), 16), 128 * comp : 128 * comp + 128] = both.astype(BF)
        return c

    lax.fori_loop(0, 12, adj_fft, 0)
    if fused:
        scatter_f.along_y()
    ACF[0:512] = jnp.zeros((512, 128), F32)

    def spec_back(i, c):
        gain, bias, ext = two(COLS[4]), two(COLS[5]), EXB[...]
        s0 = s1 = None
        for e in range(4):
            h0 = 4 * i + e
            back = dot(jnp.concatenate([Y[h0], ext], axis=1), A[h0], 1, 1)
            y = PS[h0] * gain + bias
            dy = gelu_slope(y) * (PX[rows_of(h0), 128:384] + back)
            DY[rows_of(h0), 256:512] = dy
            s0 = lane_pair(dy) if s0 is None else s0 + lane_pair(dy)
            s1 = lane_pair(dy * y) if s1 is None else s1 + lane_pair(dy * y)
        ACF[0:HALF] += s0
        ACF[256 : 256 + HALF] += s1
        return c

    lax.fori_loop(0, 4, spec_back, 0)
    put_rows(7, 0, spec_rows())
    ar_start(7)

    def dgrad(i, c):
        lhs = jnp.concatenate([slab(DC, i, 2 - a, 128, 512) for a in range(3)], axis=1)
        rhs = jnp.concatenate([WCAT[384 * a : 384 * a + 384, 128:512] for a in range(3)], axis=1)
        res = dot(lhs, rhs, 1, 1)
        lhs = jnp.concatenate([slab(D3, i, 2 - a, 0, 384) for a in range(3)], axis=1)
        both = dot(lhs, jnp.concatenate([WGL[a] for a in range(3)], axis=1), 1, 1)
        PX[block_rows(i), 128:512] = both[:, 0:384]
        loc = both[:, 384:512] + res[:, 128:256] + shifted(res[:, 0:128], 63, -1) + shifted(res[:, 256:384], 0, 1)
        loc = loc.reshape(8, SIDE, 128)
        at = pl.ds(8 * i, 8)
        COT[at, :, 0:128] = (loc + COT[at, :, 0:128].astype(F32) * WF[at].astype(F32)).astype(BF)
        return c

    lax.fori_loop(0, 1, dgrad, 0)
    if fused:
        scatter_1.along_x()
        scatter_2.along_y()
        scatter_f.along_z()
    lax.fori_loop(1, 3, dgrad, 0)

    tot = ar_wait(7)
    for r, (s1, s2) in enumerate(back_sums(tot, 2, 0)):
        n = 128 - 64 * r
        at = slice(128 * r, 128 * r + n)
        COLS[6, at] = COLS[4, at] * COLS[0, at] * col(s2 / count)[0:n]
        COLS[7, at] = COLS[4, at] * (COLS[1, at] * col(s2 / count)[0:n] - col(s1 / count)[0:n])
    GOUT[...] = jnp.zeros_like(GOUT)

    def spec_grad(i, c):
        f4, f6, f7 = two(COLS[4]), two(COLS[6]), two(COLS[7])
        ds = []
        for e in range(4):
            h0 = 4 * i + e
            d = (f4 * DY[rows_of(h0), 256:512] - f6 * PS[h0] + f7).astype(BF)
            J[h0] = d
            ds.append(d)
        rhs = jnp.concatenate([tile(F, 4 * i + e, 0, GLO) for e in range(4)], axis=0)
        GOUT[...] += dot(jnp.concatenate(ds, axis=1), rhs)
        return c

    lax.fori_loop(0, 4, spec_grad, 0)
    if fused:
        gin = jnp.concatenate([GOUT[...], jnp.zeros((64, 384), F32)], axis=0).T
        for s in range(D):
            GI[s // 2, s % 2, 0:48] = gin[48 * s : 48 * s + 48, 0:128].astype(BF)
            GI[s // 2, s % 2, 48:96] = gin[48 * s : 48 * s + 48, 128:256].astype(BF)
        scatter_i.between()
        scatter_f.along_x()
        scatter_1.back()
    else:
        put(GOUT, out_in)
    lax.fori_loop(3, 4, dgrad, 0)
    if fused:
        scatter_i.along_yz()
        scatter_f.back()
        scatter_2.along_z()
    lax.fori_loop(4, 7, dgrad, 0)
    if fused:
        scatter_i.along_x()
    lax.fori_loop(7, 8, dgrad, 0)
    if fused:
        scatter_2.to_copies()

    def field_copy(h):
        return pltpu.make_async_copy(COT.at[pl.ds(h, 4)], field_out.at[pl.ds(h, 4)], io_sem.at[6])

    def spec_field(i, c):
        w = WINT[...]
        for e in range(4):
            h0 = 4 * i + e
            dg = dot(J[h0], w, 0, 0)
            for j in range(4):
                h = h0 + 16 * j
                total = PX[slab_rows(h0, j), 128:512] + dg[64 * j : 64 * j + 64]
                wf = WF[h].astype(F32)
                for l0 in range(0, 384, 128):
                    ls = slice(128 + l0, 256 + l0)
                    COT[h, :, ls] = (total[:, l0 : l0 + 128] + COT[h, :, ls].astype(F32) * wf).astype(BF)
        for j in range(4):
            field_copy(4 * i + 16 * j).start()
        return c

    lax.fori_loop(0, 2, spec_field, 0)
    if fused:
        scatter_i.back()
    lax.fori_loop(2, 4, spec_field, 0)
    if fused:
        for n, sc in enumerate((scatter_1, scatter_2, scatter_f, scatter_i)):
            sc.last()
            for r in range(CHUNKS[n] // sc.q):
                at = STARTS[n] + r * sc.q
                pltpu.make_async_copy(sc.done.at[r], flat_out.at[at : at + sc.q], io_sem.at[7]).start()
        await_bytes(WI.at[pl.ds(0, D - 1), pl.ds(0, 48)], g_sem.at[0])
        await_bytes(WI.at[:, half], g_sem.at[2])
        await_bytes(GBB.at[pl.ds(0, D - 1)], g_sem.at[4])
        pltpu.make_async_copy(flat_out, flat_out, io_sem.at[7]).wait()
    pltpu.make_async_copy(COT, field_out, io_sem.at[6]).wait()


def run_block(features, cotangent, holes, weights, gains, biases, fused):
    dps, reps = lax.axis_size("dp"), lax.axis_size("rep")
    N = dps * reps
    any_spec = pl.BlockSpec(memory_space=pl.ANY)
    vmem = pl.BlockSpec(memory_space=pltpu.VMEM)
    table = jnp.asarray(dft_table())
    args = [features, cotangent, holes, table] + list(weights) + list(gains)
    if fused:
        args = args + list(biases)
    out_shape = [
        jax.ShapeDtypeStruct((SIDE, SIDE, ALL), BF),
        jax.ShapeDtypeStruct((SIDE, SIDE, ALL), BF),
        jax.ShapeDtypeStruct((32, 128), F32),
    ]
    if fused:
        out_shape.append(jax.ShapeDtypeStruct((sum(CHUNKS), 128), BF))
    else:
        for shape in ((1152, 128), (3456, 128), (1152, 384), (192, 384), (384, 384), (192, 384)):
            out_shape.append(jax.ShapeDtypeStruct(shape, F32))
    V = pltpu.VMEM
    dma = pltpu.SemaphoreType.DMA
    scratch = [
        V((66, SIDE, 384), BF),
        V((SIDE, SIDE, 128), BF),
        V((66, SIDE, 384), BF),
        V((66, SIDE, 384), BF),
        V((POS, ALL), F32),
        V((POS, ALL), F32),
        V((16, HALF, 256), F32),
        V((17, 384, 128), BF),
        V((17, 384, 128), F32),
        V((16, HALF, 256), BF),
        V((16, HALF, 256), BF),
        V((66, SIDE, ALL), BF),
        V((16, 256, 384), BF),
        V((SIDE, SIDE, ALL), BF),
        V((HALF, 128), F32),
        V((HALF, 128), BF),
        V((384, 128), F32),
        V((768, 128), F32),
        V((8, HALF, 128), F32),
        V((8, 384, 128), F32),
        V((24, ALL), F32),
        V((2, 16, 128), F32),
        V((HALF, 384), F32),
        V((3, ALL, 384), BF),
    ]
    scratch += [V((N, n, 128), F32) for n in AR_ROWS]
    scratch += [dma((9,)), dma((9,)), dma((9,))]
    if fused:
        scratch += [
            V((1152, ALL), BF),
            V((HALF, 384), BF),
            V((384, 384), BF),
            V((384, 384), BF),
            V((HALF, 384), BF),
            V((dps, 96, 128), BF),
            V((dps, 4, 128), F32),
            dma((38,)),
            dma((40,)),
        ]
        scratch += [V((n, 128), BF) for n in CHUNKS[:3]]
        scratch += [V((4, 2, n, 128), BF) for n in CHUNKS]
        for n, route in zip(CHUNKS, "hqhd"):
            h, q = n // 2, n // 4
            if route == "h":
                scratch += [V((4, 2, h, 128), BF), V((4, h, 128), BF), V((4, h, 128), BF)]
            elif route == "q":
                scratch += [V((4, 2, h, 128), BF), V((4, 2, q, 128), BF)] + [V((4, q, 128), BF)] * 3
            else:
                scratch += [V((4, 2, h, 128), BF), V((8, h, 128), BF)]
            if route != "q":
                scratch += [V((h, 128), BF), V((h, 128), BF), V((2, h, 128), BF)]
    return pl.pallas_call(
        functools.partial(kernel, dps, reps, fused),
        out_shape=out_shape,
        in_specs=[any_spec, any_spec, vmem, any_spec] + [vmem] * (len(args) - 4),
        out_specs=[any_spec, any_spec, vmem] + [any_spec] * (1 if fused else 6),
        scratch_shapes=scratch,
        compiler_params=pltpu.CompilerParams(
            collective_id=0, has_side_effects=True, vmem_limit_bytes=64 * 1024 * 1024 - 65536
        ),
        cost_estimate=pl.CostEstimate(flops=40_000_000_000, bytes_accessed=30_000_000, transcendentals=10_000_000),
    )(*args)


COPIES = 4


def finish_kernel(share, fused, *refs):
    it = iter(refs)

    def take(n):
        return [next(it) for _ in range(n)]

    maps = take(2)
    (norms,) = take(1)
    flat = take(1)[0] if fused else None
    outs = take(2)
    grads = take(6) if fused else []
    o_gain, o_bias = take(2)
    buf, in_sem, out_sem, norms_v, gain_v, bias_v, row_sem = take(7)
    n = SIDE // COPIES
    norm_copy = pltpu.make_async_copy(norms, norms_v, row_sem.at[0])
    copies = []
    for i in range(2):
        for c in range(COPIES):
            at = pl.ds(n * c, n)
            back = pltpu.make_async_copy(buf.at[i, at], outs[i].at[at], out_sem.at[i, c])
            copy = pltpu.make_async_copy(maps[i].at[at], buf.at[i, at], in_sem.at[i, c])
            copy.start()
            copies.append((copy, back))
    norm_copy.start()
    if fused:
        flat_v, sems = take(2)
        grads_v = take(6)
        copy = pltpu.make_async_copy(flat, flat_v, sems.at[0])
        copy.start()
    for copy_in, copy_out in copies[: len(copies) // 2]:
        copy_in.wait()
        copy_out.start()
    if fused:
        copy.wait()
        g_ll, g_gl, g_lg, g_in, g_fu, g_out = grads_v
        g_gl[0] = flat_v[0:432].astype(F32)
        g_ll[0] = flat_v[448:592].astype(F32)
        for j in range(3):
            ls = slice(128 * j, 128 * j + 128)
            g_lg[0, :, ls] = flat_v[592 + 144 * j : 736 + 144 * j].astype(F32)
            g_fu[0, :, ls] = flat_v[1024 + 48 * j : 1072 + 48 * j].astype(F32)
            g_out[0, :, ls] = flat_v[1168 + 32 * j : 1200 + 32 * j].astype(F32)[0:24]
        g_in[0, :, 0:128] = flat_v[1280:1328].astype(F32)
        g_in[0, :, 128:192] = flat_v[1328:1376].astype(F32)[:, 0:64]
        small = [pltpu.make_async_copy(v, o, sems.at[1 + i]) for i, (v, o) in enumerate(zip(grads_v, grads))]
        for c in small:
            c.start()
    for copy_in, copy_out in copies[len(copies) // 2 :]:
        copy_in.wait()
        copy_out.start()
    first = share * lax.axis_index("dp")
    lane = lax.broadcasted_iota(jnp.int32, (8, 1152), 1)
    norm_copy.wait()
    rows = []
    for at, ref, out in ((0, gain_v, o_gain), (16, bias_v, o_bias)):
        row = jnp.concatenate([norms_v[at + j : at + j + 1, :] for j in range(9)], axis=1)
        row = jnp.broadcast_to(row, (8, 1152))
        row = jnp.where(lane < HALF, row, pltpu.roll(row, 1152 - 64, axis=1))
        row = pltpu.roll(row, lax.rem(1152 - first, 1152), axis=1)
        ref[...] = row[0:1, 0:share]
        rows.append(pltpu.make_async_copy(ref, out, row_sem.at[1 + at // 16]))
        rows[-1].start()
    for c in rows:
        c.wait()
    if fused:
        for c in small:
            c.wait()
    for _, copy_out in copies:
        copy_out.wait()


def finish(block, field, norms, flat, share, shapes):
    fused = flat is not None
    any_spec = pl.BlockSpec(memory_space=pl.ANY)
    args = [block, field, norms] + ([flat] if fused else [])
    in_specs = [any_spec] * len(args)
    out_shape = [jax.ShapeDtypeStruct((SIDE, SIDE, ALL), BF)] * 2
    out_specs = [any_spec, any_spec]
    dma = pltpu.SemaphoreType.DMA
    scratch = [pltpu.VMEM((2, SIDE, SIDE, ALL), BF), dma((2, COPIES)), dma((2, COPIES)), pltpu.VMEM(norms.shape, F32)]
    scratch += [pltpu.VMEM((1, share), F32), pltpu.VMEM((1, share), F32), dma((3,))]
    if fused:
        out_shape += [jax.ShapeDtypeStruct(shape, F32) for shape in shapes]
        out_specs += [any_spec] * len(shapes)
        scratch += [pltpu.VMEM(flat.shape, BF), dma((1 + len(shapes),))]
        scratch += [pltpu.VMEM(shape, F32) for shape in shapes]
    out_shape += [jax.ShapeDtypeStruct((1, share), F32)] * 2
    out_specs += [any_spec] * 2
    return pl.pallas_call(
        functools.partial(finish_kernel, share, fused),
        out_shape=out_shape,
        in_specs=in_specs,
        out_specs=out_specs,
        scratch_shapes=scratch,
        compiler_params=pltpu.CompilerParams(vmem_limit_bytes=64 * 1024 * 1024 - 65536),
    )(*args)


def on_device(features, cotangent, holes, w_ll, w_gl, w_lg, w_in, w_fu, w_out, gains, biases):
    dps, reps = lax.axis_size("dp"), lax.axis_size("rep")
    share = gains.shape[1]
    shards = (w_ll, w_gl, w_lg, w_in, w_fu, w_out)
    if dps == 8 and reps == 4:
        weights = [w[0] for w in shards]
        block, field, norms, flat = run_block(features[0], cotangent[0], holes[0], weights, [gains], [biases], True)
        block_out, input_grad, *small = finish(block, field, norms, flat, share, [w.shape for w in shards])
        return (block_out[None], input_grad[None], *small)
    full = [lax.all_gather(w, "dp", axis=1, tiled=True)[0] for w in shards]
    table = jnp.concatenate([gains, biases], axis=0).astype(F32)
    table = lax.all_gather(table, "dp", axis=1, tiled=True)
    table = jnp.pad(table, ((0, 0), (0, 1152 - table.shape[1])), constant_values=1.0).reshape(18, 128)
    table = jnp.pad(table, ((0, 6), (0, 0)))
    weights = [jnp.concatenate([full[0], full[2]], axis=1), full[1], full[3].T, full[4], full[4].T, full[5]]
    block, field, norms, g_ll, g_gl, g_lg, g_in, g_fu, g_out = run_block(
        features[0], cotangent[0], holes[0], weights, [table], None, False
    )
    grads = []
    for g in (g_ll, g_gl, g_lg, g_in.T, g_fu, g_out):
        g = lax.psum(g[None], "rep")
        grads.append(lax.psum_scatter(g, "dp", scatter_dimension=1, tiled=True))
    block_out, input_grad, *small = finish(block, field, norms, None, share, ())
    return (block_out[None], input_grad[None], *grads, *small)


def solution(mesh):
    whole = P(("dp", "rep"), None, None, None)
    rows = P(None, "dp", None)
    in_specs = (whole, whole, P(("dp", "rep"), None, None)) + (rows,) * 6 + (P(None, "dp"),) * 2
    out_specs = (whole, whole) + (rows,) * 6 + (P(None, "dp"),) * 2
    return jax.shard_map(on_device, mesh=mesh, in_specs=in_specs, out_specs=out_specs, check_vma=False)
```
